32 devices in a mesh: dp: 4 (over y, x), erow: 2 (over core), ecol: 4 (over z).
Axes of the slice: x: 2, y: 2, z: 4, core: 2. Of those that a mesh axis runs over, the one named last changes fastest.
Arguments:
- tokens: bfloat16 [16, 512, 1024], P(('dp', 'ecol'), 'erow'), may hold values from -6 to 6
- lengths: int32 [16], P(('dp', 'ecol')), may hold values from 384 to 512, as said below
- routes: int32 [16, 512, 2], P(('dp', 'ecol'), 'erow'), may hold values from 0 to 7, as said below
- attn_gain: float32 [1024], replicated, may hold values from 0.1 to 1.9
- query_weight: bfloat16 [1024, 1024], replicated, may hold values from -0.1875 to 0.1875
- key_weight: bfloat16 [1024, 1024], replicated, may hold values from -0.1875 to 0.1875
- value_weight: bfloat16 [1024, 1024], replicated, may hold values from -0.1875 to 0.1875
- out_weight: bfloat16 [1024, 1024], replicated, may hold values from -1.5 to 1.5
- relative_bias: float32 [16, 32], replicated, may hold values from -4 to 4
- moe_gain: float32 [1024], replicated, may hold values from 0.1 to 1.9
- router_weight: float32 [1024, 8], replicated, may hold values from -0.09375 to 0.09375
- gate_weight: bfloat16 [8, 1024, 2816], P(('erow', 'ecol')), may hold values from -0.1875 to 0.1875
- up_weight: bfloat16 [8, 1024, 2816], P(('erow', 'ecol')), may hold values from -0.1875 to 0.1875
- down_weight: bfloat16 [8, 2816, 1024], P(('erow', 'ecol')), may hold values from -4 to 4
- cotangent: bfloat16 [16, 512, 1024], P(('dp', 'ecol'), 'erow'), may hold values from -6 to 6
Outputs:
- output: bfloat16 [16, 512, 1024], P(('dp', 'ecol'), 'erow')
- grad_tokens: float32 [16, 512, 1024], P(('dp', 'ecol'), 'erow')
- grad_attn_gain: float32 [1024], P(('dp', 'erow', 'ecol'))
- grad_query: float32 [1024, 1024], P(('dp', 'erow', 'ecol'))
- grad_key: float32 [1024, 1024], P(('dp', 'erow', 'ecol'))
- grad_value: float32 [1024, 1024], P(('dp', 'erow', 'ecol'))
- grad_out: float32 [1024, 1024], P(('dp', 'erow', 'ecol'))
- grad_bias: float32 [512], P(('dp', 'erow', 'ecol'))
- grad_moe_gain: float32 [1024], P(('dp', 'erow', 'ecol'))
- grad_router: float32 [1024, 8], P(('dp', 'erow', 'ecol'))
- grad_gate: float32 [8, 1024, 2816], P(('erow', 'ecol'), 'dp')
- grad_up: float32 [8, 1024, 2816], P(('erow', 'ecol'), 'dp')
- grad_down: float32 [8, 2816, 1024], P(('erow', 'ecol'), 'dp')
The draws below stay inside these ranges and needn't reach their ends.
Inputs may be any that keep to these rules, and one draw needn't show every extreme that they name: `lengths`: every item has more than 383 live positions; some item has exactly 512. The two experts of a position differ. In every draw one expert is named first at the first 80 positions of every aligned block of 256 positions (the rows of one device); padded positions carry routes too.
All inputs are finite; a program needn't handle non-finite values.
Results may differ from the reference program's by a relative error of at most 0.025.
Values may be sent and summed in bfloat16 or wider, within the bound.
A program may use at most 384 MiB of HBM per device.

```python
from functools import partial
import jax
import jax.numpy as jnp
from jax import lax

D = 1024
HEADS = 16
FF = 2816
BUCKETS = 32
TOK_DEV = 256
LEN = 512
ITEMS = 16
EXPERTS = 8
CAP = 80
N_DP = 4
N_EROW = 2
N_ECOL = 4


def draw_lengths(key, part):
    key = jax.random.fold_in(key, 11)
    drawn_key, longest_key = jax.random.split(key)
    drawn = jax.random.randint(drawn_key, (ITEMS,), TOK_DEV + TOK_DEV // 2, LEN + 1, dtype=jnp.int32)
    longest = jax.random.randint(longest_key, (), 0, ITEMS, dtype=jnp.int32)
    return jnp.where(jnp.arange(ITEMS, dtype=jnp.int32) == longest, LEN, drawn).astype(jnp.int32)


def draw_routes(key, part):
    key = jax.random.fold_in(key, 23)
    favored_key, leading_key, step_key = jax.random.split(key, 3)
    favored = jax.random.randint(favored_key, (), 0, EXPERTS, dtype=jnp.int32)
    leading = jax.random.randint(leading_key, (ITEMS, LEN), 0, EXPERTS, dtype=jnp.int32)
    step_pick = jax.random.randint(step_key, (ITEMS, LEN), 1, EXPERTS, dtype=jnp.int32)
    local_place = jnp.arange(LEN, dtype=jnp.int32) % TOK_DEV
    leading = jnp.where(local_place[None, :] < CAP, favored, leading)
    trailing = (leading + step_pick) % EXPERTS
    return jnp.stack([leading, trailing], axis=-1).astype(jnp.int32)


def shard_levels(key, shape, pieces, low, top_value):
    level = 1.0
    for dim, shards_of in pieces:
        draws = jax.random.uniform(jax.random.fold_in(jax.random.fold_in(key, 6), dim), (shards_of,), jnp.float32, low / len(pieces), top_value / len(pieces))
        level = level * jnp.repeat(jnp.exp(draws), shape[dim] // shards_of).reshape((-1,) + (1,) * (len(shape) - 1 - dim))
    return level


def noise(stream_key, dims, spread, most, cuts=(), kind=jnp.bfloat16):
    result = spread * jax.random.normal(stream_key, dims, jnp.float32)
    if cuts:
        result = result * shard_levels(stream_key, dims, cuts, -0.22, 0.18)
    return jnp.clip(result, -most, most).astype(kind)


def setup_inputs(seed: int = 0) -> dict:
    splits = jax.random.split(jax.random.key(seed), 16)
    return {
        "tokens": noise(splits[0], (ITEMS, LEN, D), 1.0, 6.0, ((0, 16), (1, 2))),
        "lengths": draw_lengths(jax.random.fold_in(splits[15], 71), 0),
        "routes": draw_routes(jax.random.fold_in(splits[15], 71), 0),
        "attn_gain": jnp.clip(1.0 + 0.18 * jax.random.normal(splits[3], (D,), jnp.float32), 0.1, 1.9),
        "query_weight": noise(splits[4], (D, D), D ** -0.5, 0.1875),
        "key_weight": noise(splits[5], (D, D), D ** -0.5, 0.1875),
        "value_weight": noise(splits[6], (D, D), D ** -0.5, 0.1875),
        "out_weight": noise(splits[7], (D, D), (D // 64) ** -0.5, 1.5),
        "relative_bias": noise(splits[8], (HEADS, BUCKETS), 1.0, 4.0, (), jnp.float32),
        "moe_gain": jnp.clip(1.0 + 0.18 * jax.random.normal(splits[9], (D,), jnp.float32), 0.1, 1.9),
        "router_weight": noise(splits[10], (D, EXPERTS), (4 * D) ** -0.5, 0.09375, (), jnp.float32),
        "gate_weight": noise(splits[11], (EXPERTS, D, FF), D ** -0.5, 0.1875, ((0, 8),)),
        "up_weight": noise(splits[12], (EXPERTS, D, FF), D ** -0.5, 0.1875, ((0, 8),)),
        "down_weight": noise(splits[13], (EXPERTS, FF, D), (max(1, FF // 1024)) ** -0.5, 4.0, ((0, 8),)),
        "cotangent": noise(splits[14], (ITEMS, LEN, D), 1.0, 6.0, ((0, 16), (1, 2))),
    }


@jax.custom_vjp
def low(v):
    return lax.optimization_barrier(v.astype(jnp.bfloat16)).astype(jnp.float32)

@jax.custom_vjp
def low_back(v):
    return v

def low_keep(v):
    return (low(v), None)

def low_pass(kept, grad):
    return (grad,)

def back_keep(v):
    return (v, None)

def back_low(kept, grad):
    return (low(grad),)
low.defvjp(low_keep, low_pass)
low_back.defvjp(back_keep, back_low)
epsilon = 1e-06
highest = lax.Precision.HIGHEST
thresholds = (12, 16, 23, 32, 46, 64, 91)

def rms_scale(inputs, norm_gain):
    return inputs * lax.rsqrt(lax.optimization_barrier(jnp.mean(inputs * inputs, axis=-1, keepdims=True)) + epsilon) * norm_gain

def bucket_of(offset):
    distance = jnp.abs(offset)
    larger = 8 + sum(((distance >= bound_at).astype(jnp.int32) for bound_at in thresholds))
    return (jnp.where(offset > 0, 16, 0) + jnp.where(distance < 8, distance, larger)).astype(jnp.int32)

def both_round(values):
    return low(low_back(values))

def mat_product(left_side, right_side):
    return jnp.matmul(left_side, right_side, precision=highest)

def attend_item(packed):
    query_rows, key_rows, value_rows, seq_length, item_bias = packed
    seq_rows, model_width = query_rows.shape
    head_count = item_bias.shape[0]
    head_size = model_width // head_count
    places = jnp.arange(seq_rows, dtype=jnp.int32)
    bucket_ids = bucket_of(places[None, :] - places[:, None])
    query_heads = query_rows.reshape(seq_rows, head_count, head_size)
    key_heads = key_rows.reshape(seq_rows, head_count, head_size)
    value_heads = value_rows.reshape(seq_rows, head_count, head_size)
    scores = jnp.einsum('qhd,khd->hqk', query_heads, key_heads, precision=highest) * 0.125 + item_bias[:, bucket_ids]
    scores = jnp.where((places < seq_length)[None, None, :], scores, -1000000000.0)
    scores = low_back(scores)
    attn_probs = low(jax.nn.softmax(scores, axis=-1))
    attended = jnp.einsum('hqk,khd->qhd', attn_probs, value_heads, precision=highest)
    return attended.reshape(seq_rows, model_width)

def expert_apply(packed):
    row_block, gate_mat, up_mat, down_mat = packed
    gate_part = low_back(jnp.matmul(row_block, gate_mat, precision=highest))
    up_part = low_back(jnp.matmul(row_block, up_mat, precision=highest))
    hidden = low(jax.nn.gelu(gate_part) * up_part)
    return low(low_back(jnp.matmul(hidden, down_mat, precision=highest)))

def forward(lengths, routes, tokens, attn_gain, query_weight, key_weight, value_weight, out_weight, relative_bias, moe_gain, router_weight, gate_weight, up_weight, down_weight):
    item_count, seq_rows, model_width = tokens.shape
    expert_count = router_weight.shape[1]
    normed = low(rms_scale(tokens, attn_gain))
    query_rows = both_round(mat_product(normed, query_weight))
    key_rows = both_round(mat_product(normed, key_weight))
    value_rows = both_round(mat_product(normed, value_weight))
    item_bias = jnp.broadcast_to(relative_bias[None], (item_count,) + relative_bias.shape)
    attended = lax.map(jax.checkpoint(attend_item), (query_rows, key_rows, value_rows, lengths, item_bias))
    mixed = both_round(attended)
    residual = tokens + low_back(mat_product(mixed, out_weight))
    moe_in = rms_scale(residual, moe_gain)
    gate_probs = jax.nn.softmax(mat_product(moe_in, router_weight), axis=-1)
    gate_pick = jnp.take_along_axis(gate_probs, routes, axis=-1)
    token_live = jnp.arange(seq_rows, dtype=jnp.int32)[None, :] < lengths[:, None]
    pair_live = jnp.broadcast_to(token_live[:, :, None], routes.shape).reshape(item_count, N_EROW, 2 * TOK_DEV)
    chosen = routes.reshape(item_count, N_EROW, 2 * TOK_DEV)
    route_hot = ((chosen[..., None] == jnp.arange(expert_count, dtype=jnp.int32)) & pair_live[..., None]).astype(jnp.int32)
    earlier = (jnp.cumsum(route_hot, axis=2) - route_hot).astype(jnp.int32)
    position = lax.optimization_barrier(jnp.sum(earlier * route_hot, axis=-1)).astype(jnp.int32)
    kept_pairs = pair_live & (position < CAP)
    item_ids = jnp.arange(item_count, dtype=jnp.int32)[:, None, None]
    piece_ids = jnp.arange(N_EROW, dtype=jnp.int32)[None, :, None]
    slot_ids = (((item_ids // N_ECOL * expert_count + chosen) * N_EROW + piece_ids) * N_ECOL + item_ids % N_ECOL) * CAP + position
    slot_total = N_DP * expert_count * N_EROW * N_ECOL * CAP
    slot_ids = jnp.where(kept_pairs, slot_ids, slot_total).astype(jnp.int32).reshape(-1)
    pair_rows = low_back(jnp.broadcast_to(low(moe_in)[:, :, None, :], routes.shape + (model_width,))).reshape(-1, model_width)
    buffer = jnp.zeros((slot_total, model_width), jnp.float32).at[slot_ids].add(pair_rows, mode='drop')
    by_expert = buffer.reshape(N_DP, expert_count, -1, model_width).transpose(1, 0, 2, 3).reshape(expert_count, -1, model_width)
    results = lax.map(jax.checkpoint(expert_apply), (by_expert, gate_weight, up_weight, down_weight))
    results = results.reshape(expert_count, N_DP, -1, model_width).transpose(1, 0, 2, 3).reshape(slot_total, model_width)
    pair_out = results.at[slot_ids].get(mode='fill', fill_value=0.0).reshape(routes.shape + (model_width,))
    return residual + lax.optimization_barrier(jnp.sum(gate_pick[..., None] * pair_out, axis=2))

def reference(tokens, lengths, routes, attn_gain, query_weight, key_weight, value_weight, out_weight, relative_bias, moe_gain, router_weight, gate_weight, up_weight, down_weight, cotangent):
    floats = (tokens.astype(jnp.float32), attn_gain.astype(jnp.float32), query_weight.astype(jnp.float32), key_weight.astype(jnp.float32), value_weight.astype(jnp.float32), out_weight.astype(jnp.float32), relative_bias.astype(jnp.float32), moe_gain.astype(jnp.float32), router_weight.astype(jnp.float32), gate_weight.astype(jnp.float32), up_weight.astype(jnp.float32), down_weight.astype(jnp.float32))
    output, pull_back = jax.vjp(partial(forward, lengths, routes), *floats)
    gradients = pull_back(cotangent.astype(jnp.float32))
    return (output.astype(jnp.bfloat16), gradients[0], gradients[1], gradients[2], gradients[3], gradients[4], gradients[5], gradients[6].reshape(-1), gradients[7], gradients[8], gradients[9], gradients[10], gradients[11])
```

```python
import functools

import jax
import jax.numpy as jnp
from jax import lax
from jax.experimental import pallas as pl
from jax.experimental.pallas import tpu as pltpu
from jax.sharding import PartitionSpec as P

epsilon = 1e-06
highest = lax.Precision.HIGHEST
thresholds = (12, 16, 23, 32, 46, 64, 91)
MESH = pl.DeviceIdType.MESH
LANES = 128
VMEM_LIMIT = 60 * 1024 * 1024


def rms_scale(inputs, norm_gain):
    return (
        inputs * lax.rsqrt(jnp.mean(inputs * inputs, axis=-1, keepdims=True) + epsilon) * norm_gain
    )


def bucket_of(offset):
    distance = jnp.abs(offset)
    larger = 8 + sum(((distance >= bound_at).astype(jnp.int32) for bound_at in thresholds))
    return jnp.where(offset > 0, 16, 0) + jnp.where(distance < 8, distance, larger)


def rounded(values):
    return values.astype(jnp.bfloat16)


def product(left_side, right_side):
    return jnp.dot(left_side, right_side, preferred_element_type=jnp.float32)


def product_back(left_side, right_side):
    return lax.dot_general(
        left_side, right_side, (((1,), (1,)), ((), ())), preferred_element_type=jnp.float32
    )


def product_left(left_side, right_side):
    return lax.dot_general(
        left_side, right_side, (((0,), (0,)), ((), ())), preferred_element_type=jnp.float32
    )


def greet(devices):
    barrier = pltpu.get_barrier_semaphore()
    for device in devices:
        pl.semaphore_signal(barrier, 1, device_id=device, device_id_type=MESH)
    pl.semaphore_wait(barrier, len(devices))


def remote(source, target, send_sem, recv_sem, device):
    return pltpu.make_async_remote_copy(
        src_ref=source,
        dst_ref=target,
        send_sem=send_sem,
        recv_sem=recv_sem,
        device_id=device,
        device_id_type=MESH,
    )


def exchange_kernel(sizes, blocks, landed, send_sems, recv_sems, own_sem):
    rows, columns = sizes
    group = rows * columns
    me = lax.axis_index("erow") * columns + lax.axis_index("ecol")
    peers = []
    for shift in range(1, group):
        peer = lax.rem(me + shift, group)
        peers.append((peer, {"erow": lax.div(peer, columns), "ecol": lax.rem(peer, columns)}))
    greet([device for _, device in peers])
    own = pltpu.make_async_copy(blocks.at[me], landed.at[me], own_sem)
    own.start()
    copies = []
    for at, (peer, device) in enumerate(peers):
        copy = remote(blocks.at[peer], landed.at[me], send_sems.at[at], recv_sems.at[at], device)
        copy.start()
        copies.append(copy)
    for copy in copies:
        copy.wait()
    own.wait()


def exchange(blocks, sizes, number):
    peers = sizes[0] * sizes[1] - 1
    return pl.pallas_call(
        functools.partial(exchange_kernel, sizes),
        out_shape=jax.ShapeDtypeStruct(blocks.shape, blocks.dtype),
        in_specs=[pl.BlockSpec(memory_space=pl.ANY)],
        out_specs=pl.BlockSpec(memory_space=pl.ANY),
        scratch_shapes=[
            pltpu.SemaphoreType.DMA((peers,)),
            pltpu.SemaphoreType.DMA((peers,)),
            pltpu.SemaphoreType.DMA,
        ],
        compiler_params=pltpu.CompilerParams(collective_id=number, has_side_effects=True),
    )(blocks)


def replicas(block):
    half = block.shape[0] // 2
    first = [(at, at ^ 1) for at in range(4)]
    second = [(at, at ^ 2) for at in range(4)]
    by_first = lax.ppermute(block, "dp", first)
    by_second = lax.ppermute(block, "dp", second)
    upper = lax.ppermute(by_first[:half], "dp", second)
    lower = lax.ppermute(by_second[half:], "dp", first)
    return jnp.concatenate([block, by_first, by_second, upper, lower], axis=0)


def reduce_kernel(sizes, widths, *refs):
    n_dp, n_row, n_col, depth = sizes
    count = len(widths)
    grads, totals = refs[:count], refs[count : 2 * count]
    held = [refs[2 * count + 7 * at : 2 * count + 7 * at + 7] for at in range(count)]
    send_sems, recv_sems = refs[-2:]
    dp, row, col = lax.axis_index("dp"), lax.axis_index("erow"), lax.axis_index("ecol")
    slow, fast = lax.div(dp, 2), lax.rem(dp, 2)
    over_row = {"erow": 1 - row}
    over_fast = {"dp": slow * 2 + 1 - fast}
    over_slow = {"dp": (1 - slow) * 2 + fast}
    over_col = [{"ecol": lax.rem(col + shift, n_col)} for shift in range(1, n_col)]
    greet([over_row, over_fast, over_slow] + over_col)
    flying = {}

    def launch(at, number, source, target, device):
        copy = remote(source, target, send_sems.at[at, number], recv_sems.at[at, number], device)
        copy.start()
        flying[at, number] = copy

    def parts(at):
        width = widths[at]
        if width >= 2 * LANES:
            return ((0, 0, width // 2), (1, width // 2, width // 2))
        return ((0, 0, width),)

    def step(at, stage):
        from_row, row_sum, from_near, near_sum, from_far, far_sum, from_col = held[at]
        if stage == 0:
            launch(at, 0, grads[at].at[:, :, 1 - row], from_row, over_row)
        elif stage == 1:
            flying[at, 0].wait()
            for high in range(2):
                for low in range(2):
                    row_sum[high, low] = (
                        grads[at][high, low, row].astype(jnp.float32)
                        + from_row[high, low].astype(jnp.float32)
                    ).astype(row_sum.dtype)
            for which, start, width in parts(at):
                cut = pl.ds(start, width)
                if which == 0:
                    launch(at, 1, row_sum.at[:, 1 - fast, :, cut], from_near.at[:, :, cut], over_fast)
                else:
                    launch(at, 2, row_sum.at[1 - slow, :, :, cut], from_near.at[:, :, cut], over_slow)
        elif stage == 2:
            for which, start, width in parts(at):
                cut = pl.ds(start, width)
                flying[at, 1 + which].wait()
                for place in range(2):
                    if which == 0:
                        kept = row_sum[place, fast, :, cut]
                    else:
                        kept = row_sum[slow, place, :, cut]
                    near_sum[place, :, cut] = (
                        kept.astype(jnp.float32) + from_near[place, :, cut].astype(jnp.float32)
                    ).astype(near_sum.dtype)
                if which == 0:
                    launch(at, 3, near_sum.at[1 - slow, :, cut], from_far.at[:, cut], over_slow)
                else:
                    launch(at, 4, near_sum.at[1 - fast, :, cut], from_far.at[:, cut], over_fast)
        elif stage == 3:
            for which, start, width in parts(at):
                cut = pl.ds(start, width)
                flying[at, 3 + which].wait()
                kept = near_sum[slow if which == 0 else fast, :, cut]
                total = kept.astype(jnp.float32) + from_far[:, cut].astype(jnp.float32)
                far_sum[:, :, cut] = total.reshape(n_col, depth, width).astype(far_sum.dtype)
            for shift in range(1, n_col):
                peer = lax.rem(col + shift, n_col)
                launch(at, 4 + shift, far_sum.at[peer], from_col.at[shift - 1], over_col[shift - 1])
        else:
            total = far_sum[col].astype(jnp.float32)
            for shift in range(1, n_col):
                flying[at, 4 + shift].wait()
                total = total + from_col[shift - 1].astype(jnp.float32)
            totals[at][...] = total

    for turn in range(count + 4):
        for at in range(count):
            if 0 <= turn - at <= 4:
                step(at, turn - at)


def reduce_shares(grads, sizes, number):
    n_dp, n_row, n_col = sizes
    depth = grads[0].shape[0] // (n_dp * n_row * n_col)
    strip = n_col * depth
    widths = tuple(grad.shape[1] for grad in grads)
    shaped = [grad.reshape(2, 2, n_row, strip, grad.shape[1]) for grad in grads]
    scratch = []
    for grad in grads:
        kind, width = grad.dtype, grad.shape[1]
        late = kind if depth % 16 == 0 else jnp.float32
        scratch += [
            pltpu.VMEM((2, 2, strip, width), kind),
            pltpu.VMEM((2, 2, strip, width), kind),
            pltpu.VMEM((2, strip, width), kind),
            pltpu.VMEM((2, strip, width), kind),
            pltpu.VMEM((strip, width), kind),
            pltpu.VMEM((n_col, depth, width), late),
            pltpu.VMEM((n_col - 1, depth, width), late),
        ]
    sems = (len(grads), 4 + n_col)
    return pl.pallas_call(
        functools.partial(reduce_kernel, (n_dp, n_row, n_col, depth), widths),
        out_shape=[jax.ShapeDtypeStruct((depth, width), jnp.float32) for width in widths],
        in_specs=[pl.BlockSpec(memory_space=pltpu.VMEM)] * len(grads),
        out_specs=[pl.BlockSpec(memory_space=pltpu.VMEM)] * len(grads),
        scratch_shapes=scratch + [pltpu.SemaphoreType.DMA(sems), pltpu.SemaphoreType.DMA(sems)],
        compiler_params=pltpu.CompilerParams(
            collective_id=number, has_side_effects=True, vmem_limit_bytes=VMEM_LIMIT
        ),
    )(*shaped)


def gelu_parts(gate_part):
    inner = 0.7978845608028654 * (gate_part + 0.044715 * gate_part * gate_part * gate_part)
    bend = jnp.tanh(inner)
    value = 0.5 * gate_part * (1.0 + bend)
    slope = 0.5 * (1.0 + bend) + 0.5 * gate_part * (1.0 - bend * bend) * 0.7978845608028654 * (
        1.0 + 3.0 * 0.044715 * gate_part * gate_part
    )
    return value, slope


def split_scalar(values):
    high = lax.reduce_precision(values, 8, 7)
    low = values - high
    panel = jnp.concatenate([high, low], axis=1)
    return rounded(jnp.pad(panel, ((0, 0), (0, LANES - 2))))


def join_scalar(panel):
    return panel[:, 0:1].astype(jnp.float32) + panel[:, 1:2].astype(jnp.float32)


def expert_parts(rows, picks, down_rows, gate_mat, up_mat):
    gate_part = product(rows, gate_mat)
    up_part = product(rows, up_mat)
    value, slope = gelu_parts(gate_part)
    hidden = value * up_part
    back = picks * down_rows
    gate_back = rounded(back * up_part * slope)
    up_back = rounded(back * value)
    return hidden, gate_back, up_back


def body(
    tokens,
    lengths,
    routes,
    attn_gain,
    query_weight,
    key_weight,
    value_weight,
    out_weight,
    relative_bias,
    moe_gain,
    router_weight,
    gate_weight,
    up_weight,
    down_weight,
    cotangent,
):
    tok_rows = tokens.shape[1]
    width = tokens.shape[2]
    head_count, bucket_count = relative_bias.shape
    head_size = width // head_count
    expert_count = router_weight.shape[1]
    capacity = 5 * tok_rows // (2 * expert_count)
    room = -(-capacity // 16) * 16
    n_dp, n_row, n_col = (lax.axis_size(name) for name in ("dp", "erow", "ecol"))
    group = n_row * n_col
    slot_count = expert_count * room
    piece = lax.axis_index("erow")
    replica = lax.axis_index("dp")
    inputs = tokens[0].astype(jnp.float32)
    seq_length = lengths[0]
    gate_mat, up_mat, down_mat = gate_weight[0], up_weight[0], down_weight[0]
    hidden_width = gate_mat.shape[1]

    query_pos = piece * tok_rows + jnp.arange(tok_rows, dtype=jnp.int32)
    key_pos = jnp.concatenate([query_pos, query_pos + (1 - 2 * piece) * tok_rows])
    bucket_ids = bucket_of(key_pos[None, :] - query_pos[:, None])
    bias_onehot = (
        jnp.arange(bucket_count, dtype=jnp.int32)[:, None, None] == bucket_ids[None]
    ).astype(jnp.bfloat16)
    bias_full = jnp.einsum(
        "zt,tyx->zyx", relative_bias, bias_onehot, precision=highest, preferred_element_type=jnp.float32
    )
    key_live = key_pos < seq_length
    tok_live = query_pos < seq_length
    pair_routes = routes[0]
    route_flat = pair_routes.reshape(-1)
    pair_live = jnp.broadcast_to(tok_live[:, None], pair_routes.shape).reshape(-1)
    expert_range = jnp.arange(expert_count, dtype=jnp.int32)
    route_hot = ((route_flat[:, None] == expert_range[None, :]) & pair_live[:, None]).astype(jnp.int32)
    earlier = jnp.cumsum(route_hot, axis=0) - route_hot
    position = jnp.sum(earlier * route_hot, axis=1)
    kept_pairs = pair_live & (position < capacity)
    slot_ids = jnp.where(kept_pairs, route_flat * room + position, -1).reshape(tok_rows, 2)
    slot_range = jnp.arange(slot_count, dtype=jnp.int32)
    select_lead = (slot_ids[:, 0:1] == slot_range[None, :]).astype(jnp.bfloat16)
    select_trail = (slot_ids[:, 1:2] == slot_range[None, :]).astype(jnp.bfloat16)
    select_both = select_lead + select_trail
    choice_hot = (pair_routes[:, :, None] == expert_range[None, None, :]).astype(jnp.float32)

    def sent(rows, number):
        return exchange(rows.reshape(group, room, rows.shape[1]), (n_row, n_col), number).reshape(
            rows.shape
        )

    out_grad_low = cotangent[0]
    out_grad = out_grad_low.astype(jnp.float32)
    got_grads = sent(rounded(product_left(select_both, out_grad_low)), 0)
    all_grads = replicas(got_grads)
    down_rows = product_back(all_grads, down_mat)

    normed = rounded(rms_scale(inputs, attn_gain))
    queries = rounded(product(normed, query_weight))
    both_local = jnp.concatenate(
        [rounded(product(normed, key_weight)), rounded(product(normed, value_weight))], axis=1
    )
    both_other = lax.ppermute(both_local, "erow", [(0, 1), (1, 0)])
    both_all = jnp.concatenate([both_local, both_other], axis=0)
    seq_rows = both_all.shape[0]
    query_heads = queries.reshape(tok_rows, head_count, head_size)
    key_heads = both_all[:, :width].reshape(seq_rows, head_count, head_size)
    value_heads = both_all[:, width:].reshape(seq_rows, head_count, head_size)
    scores = (
        jnp.einsum("qhd,khd->hqk", query_heads, key_heads, preferred_element_type=jnp.float32) * 0.125
        + bias_full
    )
    scores = jnp.where(key_live[None, None, :], scores, -1000000000.0)
    attn_probs = jax.nn.softmax(scores, axis=-1)
    probs_low = rounded(attn_probs)
    mixed = rounded(
        jnp.einsum("hqk,khd->qhd", probs_low, value_heads, preferred_element_type=jnp.float32).reshape(
            tok_rows, width
        )
    )
    residual = inputs + product(mixed, out_weight)
    moe_in = rms_scale(residual, moe_gain)
    gate_probs = jax.nn.softmax(jnp.dot(moe_in, router_weight, precision=highest), axis=-1)
    gate_pick = jnp.sum(gate_probs[:, None, :] * choice_hot, axis=-1)

    slot_pick = lax.dot_general(
        select_lead.astype(jnp.float32), gate_pick[:, 0:1], (((0,), (0,)), ((), ())), precision=highest
    ) + lax.dot_general(
        select_trail.astype(jnp.float32), gate_pick[:, 1:2], (((0,), (0,)), ((), ())), precision=highest
    )
    slot_rows = rounded(product_left(select_both, rounded(moe_in)))
    got = sent(jnp.concatenate([slot_rows, split_scalar(slot_pick)], axis=1), 1)
    all_got = replicas(got)
    own_rows, own_picks = got[:, :width], join_scalar(got[:, width:])
    hidden, gate_back, up_back = expert_parts(
        own_rows, own_picks, down_rows[: got.shape[0]], gate_mat, up_mat
    )
    pick_slots = jnp.sum(hidden * down_rows[: got.shape[0]], axis=1, keepdims=True)
    row_back = rounded(product_back(gate_back, gate_mat) + product_back(up_back, up_mat))
    back = sent(jnp.concatenate([row_back, split_scalar(pick_slots)], axis=1), 2)
    expert_out = rounded(product(rounded(hidden), down_mat))
    out_slots = sent(expert_out, 3)
    output = rounded(
        residual
        + gate_pick[:, 0:1] * product(select_lead, out_slots)
        + gate_pick[:, 1:2] * product(select_trail, out_slots)
    )

    slot_pick_back = join_scalar(back[:, width:])
    pick_back = jnp.concatenate(
        [
            jnp.dot(select_lead.astype(jnp.float32), slot_pick_back, precision=highest),
            jnp.dot(select_trail.astype(jnp.float32), slot_pick_back, precision=highest),
        ],
        axis=1,
    )
    prob_back = jnp.sum(pick_back[:, :, None] * choice_hot, axis=1)
    logit_back = gate_probs * (prob_back - jnp.sum(gate_probs * prob_back, axis=-1, keepdims=True))
    router_grad = lax.dot_general(moe_in, logit_back, (((0,), (0,)), ((), ())), precision=highest)
    moe_back = product(select_both, back[:, :width]) + lax.dot_general(
        logit_back, router_weight, (((1,), (1,)), ((), ())), precision=highest
    )
    _, moe_pull = jax.vjp(rms_scale, residual, moe_gain)
    residual_part, moe_gain_grad = moe_pull(moe_back)
    residual_grad = out_grad + residual_part
    branch_grad = rounded(residual_grad)
    out_wgrad = product_left(mixed, branch_grad)
    mixed_grad = rounded(product_back(branch_grad, out_weight)).reshape(tok_rows, head_count, head_size)

    prob_part = jnp.einsum("qhd,khd->hqk", mixed_grad, value_heads, preferred_element_type=jnp.float32)
    score_back = rounded(
        attn_probs * (prob_part - jnp.sum(attn_probs * prob_part, axis=-1, keepdims=True))
    )
    query_grad = rounded(
        jnp.einsum("hqk,khd->qhd", score_back, key_heads, preferred_element_type=jnp.float32) * 0.125
    ).reshape(tok_rows, width)
    key_part = (
        jnp.einsum("hqk,qhd->khd", score_back, query_heads, preferred_element_type=jnp.float32) * 0.125
    ).reshape(seq_rows, width)
    value_part = jnp.einsum(
        "hqk,qhd->khd", probs_low, mixed_grad, preferred_element_type=jnp.float32
    ).reshape(seq_rows, width)
    both_part = jnp.concatenate([key_part, value_part], axis=1)
    far_part = lax.ppermute(rounded(both_part[tok_rows:]), "erow", [(0, 1), (1, 0)])
    both_grad = rounded(both_part[:tok_rows] + far_part.astype(jnp.float32))
    key_grad, value_grad = both_grad[:, :width], both_grad[:, width:]
    bias_grad = jnp.einsum("tlx,mlx->tm", score_back, bias_onehot, preferred_element_type=jnp.float32)
    normed_grad = (
        product_back(query_grad, query_weight)
        + product_back(key_grad, key_weight)
        + product_back(value_grad, value_weight)
    )
    _, attn_pull = jax.vjp(rms_scale, inputs, attn_gain)
    input_part, attn_gain_grad = attn_pull(normed_grad)
    token_grad = residual_grad + input_part

    width_share, hidden_share = width // n_dp, hidden_width // n_dp
    all_rows, all_picks = all_got[:, :width], join_scalar(all_got[:, width:])
    all_hidden, all_gate_back, all_up_back = expert_parts(
        all_rows, all_picks, down_rows, gate_mat, up_mat
    )
    rows_part = lax.dynamic_slice_in_dim(all_rows, replica * width_share, width_share, 1)
    hidden_part = lax.dynamic_slice_in_dim(
        rounded(all_picks * all_hidden), replica * hidden_share, hidden_share, 1
    )
    gate_total = product_left(rows_part, all_gate_back)
    up_total = product_left(rows_part, all_up_back)
    down_total = product_left(hidden_part, all_grads)

    device_count = n_dp * n_row * n_col
    bias_column = jnp.pad(
        bias_grad.reshape(device_count, -1),
        ((0, 0), (0, (width - head_count * bucket_count) // device_count)),
    ).reshape(-1, 1)
    small = jnp.concatenate([attn_gain_grad[:, None], moe_gain_grad[:, None], bias_column, router_grad], axis=1)
    small = jnp.pad(small, ((0, 0), (0, LANES - small.shape[1])))
    wgrads = [rounded(out_wgrad)] + [
        rounded(product_left(normed, grad)) for grad in (query_grad, key_grad, value_grad)
    ]
    out_sum, query_sum, key_sum, value_sum, small_sum = reduce_shares(
        wgrads + [small], (n_dp, n_row, n_col), 4
    )
    bias_share = head_count * bucket_count // device_count
    return (
        output[None],
        token_grad[None],
        small_sum[:, 0],
        query_sum,
        key_sum,
        value_sum,
        out_sum,
        small_sum[:bias_share, 2],
        small_sum[:, 1],
        small_sum[:, 3 : 3 + expert_count],
        gate_total[None],
        up_total[None],
        down_total[None],
    )


def solution(mesh):
    rows = P(("dp", "ecol"), "erow", None)
    experts = P(("erow", "ecol"), None, None)
    every = ("dp", "erow", "ecol")
    shares = P(("erow", "ecol"), "dp", None)
    return jax.shard_map(
        body,
        mesh=mesh,
        in_specs=(
            (rows, P(("dp", "ecol")), rows) + (P(),) * 8 + (experts, experts, experts, rows)
        ),
        out_specs=(rows, rows, P(every))
        + (P(every, None),) * 4
        + (P(every), P(every), P(every, None), shares, shares, shares),
        check_vma=False,
    )
```

```python
import functools

import jax
import jax.numpy as jnp
from jax import lax
from jax.experimental import pallas as pl
from jax.experimental.pallas import tpu as pltpu
from jax.sharding import PartitionSpec as P

epsilon = 1e-06
highest = lax.Precision.HIGHEST
thresholds = (12, 16, 23, 32, 46, 64, 91)
MESH = pl.DeviceIdType.MESH
LANES = 128
VMEM_LIMIT = 60 * 1024 * 1024


def rms_scale(inputs, norm_gain):
    return (
        inputs * lax.rsqrt(jnp.mean(inputs * inputs, axis=-1, keepdims=True) + epsilon) * norm_gain
    )


def bucket_of(offset):
    distance = jnp.abs(offset)
    larger = 8 + sum(((distance >= bound_at).astype(jnp.int32) for bound_at in thresholds))
    return jnp.where(offset > 0, 16, 0) + jnp.where(distance < 8, distance, larger)


def rounded(values):
    return values.astype(jnp.bfloat16)


def product(left_side, right_side):
    return jnp.dot(left_side, right_side, preferred_element_type=jnp.float32)


def product_back(left_side, right_side):
    return lax.dot_general(
        left_side, right_side, (((1,), (1,)), ((), ())), preferred_element_type=jnp.float32
    )


def product_left(left_side, right_side):
    return lax.dot_general(
        left_side, right_side, (((0,), (0,)), ((), ())), preferred_element_type=jnp.float32
    )


def greet(devices):
    barrier = pltpu.get_barrier_semaphore()
    for device in devices:
        pl.semaphore_signal(barrier, 1, device_id=device, device_id_type=MESH)
    pl.semaphore_wait(barrier, len(devices))


def remote(source, target, send_sem, recv_sem, device):
    return pltpu.make_async_remote_copy(
        src_ref=source,
        dst_ref=target,
        send_sem=send_sem,
        recv_sem=recv_sem,
        device_id=device,
        device_id_type=MESH,
    )


def flipped(index, mask, size):
    bit = 1
    while bit < size:
        if mask & bit:
            index = index + bit * (1 - 2 * lax.rem(lax.div(index, bit), 2))
        bit *= 2
    return index


def partners(n_row, n_col):
    row, col = lax.axis_index("erow"), lax.axis_index("ecol")
    return [
        {"erow": flipped(row, place % n_row, n_row), "ecol": flipped(col, place // n_row, n_col)}
        for place in range(n_row * n_col)
    ]


def exchange_kernel(sizes, blocks, landed, send_sems, recv_sems, own_sem):
    devices = partners(*sizes)
    greet(devices[1:])
    own = pltpu.make_async_copy(blocks.at[0], landed.at[0], own_sem)
    own.start()
    copies = []
    for place in range(1, len(devices)):
        copy = remote(
            blocks.at[place],
            landed.at[place],
            send_sems.at[place - 1],
            recv_sems.at[place - 1],
            devices[place],
        )
        copy.start()
        copies.append(copy)
    for copy in copies:
        copy.wait()
    own.wait()


def exchange(blocks, sizes, number):
    peers = sizes[0] * sizes[1] - 1
    return pl.pallas_call(
        functools.partial(exchange_kernel, sizes),
        out_shape=jax.ShapeDtypeStruct(blocks.shape, blocks.dtype),
        in_specs=[pl.BlockSpec(memory_space=pl.ANY)],
        out_specs=pl.BlockSpec(memory_space=pl.ANY),
        scratch_shapes=[
            pltpu.SemaphoreType.DMA((peers,)),
            pltpu.SemaphoreType.DMA((peers,)),
            pltpu.SemaphoreType.DMA,
        ],
        compiler_params=pltpu.CompilerParams(collective_id=number, has_side_effects=True),
    )(blocks)


def replicas(block):
    half = block.shape[0] // 2
    first = [(at, at ^ 1) for at in range(4)]
    second = [(at, at ^ 2) for at in range(4)]
    by_first = lax.ppermute(block, "dp", first)
    by_second = lax.ppermute(block, "dp", second)
    upper = lax.ppermute(by_first[:half], "dp", second)
    lower = lax.ppermute(by_second[half:], "dp", first)
    return jnp.concatenate([block, by_first, by_second, upper, lower], axis=0)


def reduce_kernel(sizes, widths, *refs):
    n_dp, n_row, n_col, depth = sizes
    count = len(widths)
    grads, totals = refs[:count], refs[count : 2 * count]
    held = [refs[2 * count + 7 * at : 2 * count + 7 * at + 7] for at in range(count)]
    send_sems, recv_sems = refs[-2:]
    dp, row, col = lax.axis_index("dp"), lax.axis_index("erow"), lax.axis_index("ecol")
    slow, fast = lax.div(dp, 2), lax.rem(dp, 2)
    over_row = {"erow": 1 - row}
    over_fast = {"dp": slow * 2 + 1 - fast}
    over_slow = {"dp": (1 - slow) * 2 + fast}
    over_col = [{"ecol": lax.rem(col + shift, n_col)} for shift in range(1, n_col)]
    greet([over_row, over_fast, over_slow] + over_col)
    flying = {}

    def launch(at, number, source, target, device):
        copy = remote(source, target, send_sems.at[at, number], recv_sems.at[at, number], device)
        copy.start()
        flying[at, number] = copy

    def parts(at):
        width = widths[at]
        if width >= 2 * LANES:
            return ((0, 0, width // 2), (1, width // 2, width // 2))
        return ((0, 0, width),)

    def step(at, stage):
        from_row, row_sum, from_near, near_sum, from_far, far_sum, from_col = held[at]
        if stage == 0:
            launch(at, 0, grads[at].at[:, :, 1 - row], from_row, over_row)
        elif stage == 1:
            flying[at, 0].wait()
            for high in range(2):
                for low in range(2):
                    row_sum[high, low] = (
                        grads[at][high, low, row].astype(jnp.float32)
                        + from_row[high, low].astype(jnp.float32)
                    ).astype(row_sum.dtype)
            for which, start, width in parts(at):
                cut = pl.ds(start, width)
                if which == 0:
                    launch(at, 1, row_sum.at[:, 1 - fast, :, cut], from_near.at[:, :, cut], over_fast)
                else:
                    launch(at, 2, row_sum.at[1 - slow, :, :, cut], from_near.at[:, :, cut], over_slow)
        elif stage == 2:
            for which, start, width in parts(at):
                cut = pl.ds(start, width)
                flying[at, 1 + which].wait()
                for place in range(2):
                    if which == 0:
                        kept = row_sum[place, fast, :, cut]
                    else:
                        kept = row_sum[slow, place, :, cut]
                    near_sum[place, :, cut] = (
                        kept.astype(jnp.float32) + from_near[place, :, cut].astype(jnp.float32)
                    ).astype(near_sum.dtype)
                if which == 0:
                    launch(at, 3, near_sum.at[1 - slow, :, cut], from_far.at[:, cut], over_slow)
                else:
                    launch(at, 4, near_sum.at[1 - fast, :, cut], from_far.at[:, cut], over_fast)
        elif stage == 3:
            for which, start, width in parts(at):
                cut = pl.ds(start, width)
                flying[at, 3 + which].wait()
                kept = near_sum[slow if which == 0 else fast, :, cut]
                total = kept.astype(jnp.float32) + from_far[:, cut].astype(jnp.float32)
                far_sum[:, :, cut] = total.reshape(n_col, depth, width).astype(far_sum.dtype)
            for shift in range(1, n_col):
                peer = lax.rem(col + shift, n_col)
                launch(at, 4 + shift, far_sum.at[peer], from_col.at[shift - 1], over_col[shift - 1])
        else:
            total = far_sum[col].astype(jnp.float32)
            for shift in range(1, n_col):
                flying[at, 4 + shift].wait()
                total = total + from_col[shift - 1].astype(jnp.float32)
            totals[at][...] = total

    for turn in range(count + 4):
        for at in range(count):
            if 0 <= turn - at <= 4:
                step(at, turn - at)


def reduce_shares(grads, sizes, number):
    n_dp, n_row, n_col = sizes
    depth = grads[0].shape[0] // (n_dp * n_row * n_col)
    strip = n_col * depth
    widths = tuple(grad.shape[1] for grad in grads)
    shaped = [grad.reshape(2, 2, n_row, strip, grad.shape[1]) for grad in grads]
    scratch = []
    for grad in grads:
        kind, width = grad.dtype, grad.shape[1]
        late = kind if depth % 16 == 0 else jnp.float32
        scratch += [
            pltpu.VMEM((2, 2, strip, width), kind),
            pltpu.VMEM((2, 2, strip, width), kind),
            pltpu.VMEM((2, strip, width), kind),
            pltpu.VMEM((2, strip, width), kind),
            pltpu.VMEM((strip, width), kind),
            pltpu.VMEM((n_col, depth, width), late),
            pltpu.VMEM((n_col - 1, depth, width), late),
        ]
    sems = (len(grads), 4 + n_col)
    return pl.pallas_call(
        functools.partial(reduce_kernel, (n_dp, n_row, n_col, depth), widths),
        out_shape=[jax.ShapeDtypeStruct((depth, width), jnp.float32) for width in widths],
        in_specs=[pl.BlockSpec(memory_space=pltpu.VMEM)] * len(grads),
        out_specs=[pl.BlockSpec(memory_space=pltpu.VMEM)] * len(grads),
        scratch_shapes=scratch + [pltpu.SemaphoreType.DMA(sems), pltpu.SemaphoreType.DMA(sems)],
        compiler_params=pltpu.CompilerParams(
            collective_id=number, has_side_effects=True, vmem_limit_bytes=VMEM_LIMIT
        ),
    )(*shaped)


def iota(shape, dimension):
    return lax.broadcasted_iota(jnp.int32, shape, dimension)


def row_slots(routes, live, experts, room, capacity):
    tok = live.shape[1]
    names = iota((experts, tok), 0)
    hot = [(routes[k : k + 1] == names) & live for k in range(2)]
    both = jnp.where(hot[0] | hot[1], 1.0, 0.0).astype(jnp.bfloat16)
    before = jnp.where(iota((tok, tok), 0) < iota((tok, tok), 1), 1.0, 0.0).astype(jnp.bfloat16)
    earlier = product(both, before)
    slots = []
    for k in range(2):
        place = jnp.sum(jnp.where(hot[k], earlier, 0.0), axis=0, keepdims=True)
        slot = routes[k : k + 1].astype(jnp.float32) * room + place
        slots.append(jnp.where(live & (place < capacity), slot, -1.0))
    return slots


def bias_tables(relative_bias, table_width, offset):
    buckets = relative_bias.shape[1]
    place = iota((buckets, table_width), 1)
    distance = jnp.where(place < table_width // 2, place, place - table_width) + offset
    hot = jnp.where(bucket_of(distance) == iota((buckets, table_width), 0), 1.0, 0.0)
    return jnp.dot(relative_bias, hot, precision=highest, preferred_element_type=jnp.float32)


def skewed(row, rows):
    width = row.shape[1]
    full = pltpu.roll(jnp.broadcast_to(row, (rows, width)), 0, 1, stride=1, stride_axis=0)
    return full[:, : width // 2]


def front_kernel(
    dims,
    lengths,
    tokens,
    cotangent,
    routes_row,
    routes_col,
    attn_gain,
    moe_gain,
    relative_bias,
    router,
    query_weight,
    key_weight,
    value_weight,
    out_weight,
    normed_out,
    query_out,
    both_out,
    probs_out,
    mixed_out,
    residual_out,
    gates_out,
    rows_out,
    cot_landed,
    select,
    cot_slots,
    tables,
    held_weights,
    weight_sems,
    own_sem,
    send_sems,
    recv_sems,
    row_send,
    row_recv,
):
    heads, experts, room, capacity, n_row, n_col = dims
    tok, width = tokens.shape
    pair_width = 2 * width // heads
    loads = []
    for at, source in enumerate((key_weight, value_weight, query_weight, out_weight)):
        load = pltpu.make_async_copy(source, held_weights.at[at], weight_sems.at[at])
        load.start()
        loads.append(load)
    devices = partners(n_row, n_col)
    barrier = pltpu.get_barrier_semaphore()
    for device in devices[1:]:
        pl.semaphore_signal(barrier, 1, device_id=device, device_id_type=MESH)

    piece = lax.axis_index("erow")
    length = lengths[0]
    live = iota((1, tok), 1) + piece * tok < length
    slots = row_slots(routes_row[...], live, experts, room, capacity)
    names = iota((experts * room, tok), 0).astype(jnp.float32)
    hot = [jnp.where(names == slot, 1.0, 0.0).astype(jnp.bfloat16) for slot in slots]
    select[...] = hot[0] + hot[1]
    cot_slots[...] = product(select[...], cotangent[...]).astype(jnp.bfloat16).reshape(cot_slots.shape)
    pl.semaphore_wait(barrier, len(devices) - 1)
    own = pltpu.make_async_copy(cot_slots.at[0], cot_landed.at[0], own_sem)
    own.start()
    copies = []
    for place in range(1, len(devices)):
        copy = remote(
            cot_slots.at[place],
            cot_landed.at[place],
            send_sems.at[place - 1],
            recv_sems.at[place - 1],
            devices[place],
        )
        copy.start()
        copies.append(copy)

    inputs = tokens[...].astype(jnp.float32)
    scale = lax.rsqrt(jnp.mean(inputs * inputs, axis=1, keepdims=True) + epsilon)
    normed = (inputs * scale * attn_gain[...]).astype(jnp.bfloat16)
    normed_out[...] = normed
    loads[0].wait()
    both_out[:tok, :width] = product(normed, held_weights[0]).astype(jnp.bfloat16)
    loads[1].wait()
    both_out[:tok, width:] = product(normed, held_weights[1]).astype(jnp.bfloat16)
    pair_copy = remote(both_out.at[pl.ds(0, tok)], both_out.at[pl.ds(tok, tok)], row_send, row_recv, devices[1])
    pair_copy.start()
    loads[2].wait()
    query_out[...] = (product(normed, held_weights[2]) * 0.125).astype(jnp.bfloat16)
    offset = tok * (1 - 2 * piece)
    tables[:, : 2 * tok] = bias_tables(relative_bias[...], 2 * tok, 0)
    tables[:, 2 * tok :] = bias_tables(relative_bias[...], 2 * tok, offset)
    place = iota((1, 2 * tok), 1)
    position = jnp.where(place < tok, place + piece * tok, place - tok + (1 - piece) * tok)
    dead = jnp.where(position < length, 0.0, -1000000000.0)
    low_half = iota((tok, pair_width), 1) < pair_width // 2
    pair_copy.wait()

    def attend(pair, carry):
        lanes = pl.ds(pl.multiple_of(pair * pair_width, pair_width), pair_width)
        value_lanes = pl.ds(pl.multiple_of(width + pair * pair_width, pair_width), pair_width)
        queries, keys, values = query_out[:, lanes], both_out[:, lanes], both_out[:, value_lanes]
        results = []
        for member in range(2):
            mask = low_half if member == 0 else jnp.logical_not(low_half)
            head = 2 * pair + member
            scores = product_back(jnp.where(mask, queries, jnp.zeros_like(queries)), keys)
            table = tables[pl.ds(head, 1)]
            bias = jnp.concatenate([skewed(table[:, : 2 * tok], tok), skewed(table[:, 2 * tok :], tok)], axis=1)
            scores = scores + bias + dead
            powers = jnp.exp(scores - jnp.max(scores, axis=1, keepdims=True))
            probs = (powers * (1.0 / jnp.sum(powers, axis=1, keepdims=True))).astype(jnp.bfloat16)
            probs_out[pl.ds(head, 1)] = probs[None]
            results.append(product(probs, values))
        mixed_out[:, lanes] = jnp.where(low_half, results[0], results[1]).astype(jnp.bfloat16)
        return carry

    lax.fori_loop(0, heads // 2, attend, 0)
    loads[3].wait()
    residual = inputs + product(mixed_out[...], held_weights[3])
    residual_out[...] = residual
    scale = lax.rsqrt(jnp.mean(residual * residual, axis=1, keepdims=True) + epsilon)
    moe_in = residual * scale * moe_gain[...]
    logits = jnp.dot(moe_in, router[...], precision=highest, preferred_element_type=jnp.float32)
    lane = iota(logits.shape, 1)
    logits = jnp.where(lane < experts, logits, -1e30)
    powers = jnp.exp(logits - jnp.max(logits, axis=1, keepdims=True))
    gates = powers / jnp.sum(powers, axis=1, keepdims=True)
    gates_out[...] = gates
    panel = jnp.zeros((experts * room, LANES), jnp.float32)
    for k in range(2):
        pick = jnp.sum(jnp.where(routes_col[:, k : k + 1] == lane, gates, 0.0), axis=1, keepdims=True)
        high = pick.astype(jnp.bfloat16)
        low = (pick - high.astype(jnp.float32)).astype(jnp.bfloat16)
        parts = jnp.where(lane == 0, high, jnp.where(lane == 1, low, jnp.zeros_like(low)))
        panel = panel + product(hot[k], parts)
    rows = product(select[...], moe_in.astype(jnp.bfloat16))
    rows_out[:, :, :width] = rows.astype(jnp.bfloat16).reshape(rows_out.shape[0], -1, width)
    rows_out[:, :, width:] = panel.astype(jnp.bfloat16).reshape(rows_out.shape[0], -1, LANES)
    for copy in copies:
        copy.wait()
    own.wait()


def front(dims, number, lengths, tokens, cotangent, routes_row, routes_col, *params):
    heads, experts, room, capacity, n_row, n_col = dims
    tok, width = tokens.shape
    group = n_row * n_col
    blocks = experts * room // group
    half, single = jnp.bfloat16, jnp.float32
    vmem, anywhere = pl.BlockSpec(memory_space=pltpu.VMEM), pl.BlockSpec(memory_space=pl.ANY)
    shapes = [
        ((tok, width), half),
        ((tok, width), half),
        ((2 * tok, 2 * width), half),
        ((heads, tok, 2 * tok), half),
        ((tok, width), half),
        ((tok, width), single),
        ((tok, LANES), single),
        ((group, blocks, width + LANES), half),
        ((group, blocks, width), half),
    ]
    return pl.pallas_call(
        functools.partial(front_kernel, dims),
        out_shape=[jax.ShapeDtypeStruct(shape, kind) for shape, kind in shapes],
        in_specs=[pl.BlockSpec(memory_space=pltpu.SMEM)] + [vmem] * 8 + [anywhere] * 4,
        out_specs=[vmem] * 8 + [anywhere],
        scratch_shapes=[
            pltpu.VMEM((experts * room, tok), half),
            pltpu.VMEM((group, blocks, width), half),
            pltpu.VMEM((heads, 4 * tok), single),
            pltpu.VMEM((4, width, width), half),
            pltpu.SemaphoreType.DMA((4,)),
            pltpu.SemaphoreType.DMA,
            pltpu.SemaphoreType.DMA((group - 1,)),
            pltpu.SemaphoreType.DMA((group - 1,)),
            pltpu.SemaphoreType.DMA,
            pltpu.SemaphoreType.DMA,
        ],
        compiler_params=pltpu.CompilerParams(
            collective_id=number, has_side_effects=True, vmem_limit_bytes=VMEM_LIMIT
        ),
    )(lengths, tokens, cotangent, routes_row, routes_col, *params)


def gelu_parts(gate_part):
    inner = 0.7978845608028654 * (gate_part + 0.044715 * gate_part * gate_part * gate_part)
    bend = jnp.tanh(inner)
    value = 0.5 * gate_part * (1.0 + bend)
    slope = 0.5 * (1.0 + bend) + 0.5 * gate_part * (1.0 - bend * bend) * 0.7978845608028654 * (
        1.0 + 3.0 * 0.044715 * gate_part * gate_part
    )
    return value, slope


def split_scalar(values):
    high = lax.reduce_precision(values, 8, 7)
    low = values - high
    panel = jnp.concatenate([high, low], axis=1)
    return rounded(jnp.pad(panel, ((0, 0), (0, LANES - 2))))


def join_scalar(panel):
    return panel[:, 0:1].astype(jnp.float32) + panel[:, 1:2].astype(jnp.float32)


def expert_parts(rows, picks, down_rows, gate_mat, up_mat):
    gate_part = product(rows, gate_mat)
    up_part = product(rows, up_mat)
    value, slope = gelu_parts(gate_part)
    hidden = value * up_part
    back = picks * down_rows
    gate_back = rounded(back * up_part * slope)
    up_back = rounded(back * value)
    return hidden, gate_back, up_back


def body(
    tokens,
    lengths,
    routes,
    attn_gain,
    query_weight,
    key_weight,
    value_weight,
    out_weight,
    relative_bias,
    moe_gain,
    router_weight,
    gate_weight,
    up_weight,
    down_weight,
    cotangent,
):
    tok_rows = tokens.shape[1]
    width = tokens.shape[2]
    head_count, bucket_count = relative_bias.shape
    head_size = width // head_count
    expert_count = router_weight.shape[1]
    capacity = 5 * tok_rows // (2 * expert_count)
    room = -(-capacity // 16) * 16
    n_dp, n_row, n_col = (lax.axis_size(name) for name in ("dp", "erow", "ecol"))
    group = n_row * n_col
    slot_count = expert_count * room
    piece = lax.axis_index("erow")
    replica = lax.axis_index("dp")
    inputs = tokens[0].astype(jnp.float32)
    seq_length = lengths[0]
    gate_mat, up_mat, down_mat = gate_weight[0], up_weight[0], down_weight[0]
    hidden_width = gate_mat.shape[1]

    query_pos = piece * tok_rows + jnp.arange(tok_rows, dtype=jnp.int32)
    key_pos = jnp.concatenate([query_pos, query_pos + (1 - 2 * piece) * tok_rows])
    bucket_ids = bucket_of(key_pos[None, :] - query_pos[:, None])
    bias_onehot = (
        jnp.arange(bucket_count, dtype=jnp.int32)[:, None, None] == bucket_ids[None]
    ).astype(jnp.bfloat16)
    tok_live = query_pos < seq_length
    pair_routes = routes[0]
    near_routes = (
        (pair_routes % n_col) ^ lax.axis_index("ecol")
    ) * n_row + ((pair_routes // n_col) ^ piece)
    route_flat = near_routes.reshape(-1)
    pair_live = jnp.broadcast_to(tok_live[:, None], pair_routes.shape).reshape(-1)
    expert_range = jnp.arange(expert_count, dtype=jnp.int32)
    route_hot = ((route_flat[:, None] == expert_range[None, :]) & pair_live[:, None]).astype(jnp.int32)
    earlier = jnp.cumsum(route_hot, axis=0) - route_hot
    position = jnp.sum(earlier * route_hot, axis=1)
    kept_pairs = pair_live & (position < capacity)
    slot_ids = jnp.where(kept_pairs, route_flat * room + position, -1).reshape(tok_rows, 2)
    slot_range = jnp.arange(slot_count, dtype=jnp.int32)
    select_lead = (slot_ids[:, 0:1] == slot_range[None, :]).astype(jnp.bfloat16)
    select_trail = (slot_ids[:, 1:2] == slot_range[None, :]).astype(jnp.bfloat16)
    select_both = select_lead + select_trail
    choice_hot = (pair_routes[:, :, None] == expert_range[None, None, :]).astype(jnp.float32)

    def sent(rows, number):
        return exchange(rows.reshape(group, room, rows.shape[1]), (n_row, n_col), number).reshape(
            rows.shape
        )

    out_grad = cotangent[0].astype(jnp.float32)
    routes_row = jnp.pad(near_routes.T, ((0, 6), (0, 0)))
    (
        normed,
        queries,
        both_all,
        probs_low,
        mixed,
        residual,
        gates,
        slot_rows,
        got_grads,
    ) = front(
        (head_count, expert_count, room, capacity, n_row, n_col),
        0,
        lengths,
        tokens[0],
        cotangent[0],
        routes_row,
        pair_routes,
        attn_gain[None],
        moe_gain[None],
        relative_bias,
        jnp.pad(router_weight, ((0, 0), (0, LANES - expert_count))),
        query_weight,
        key_weight,
        value_weight,
        out_weight,
    )
    got_grads = got_grads.reshape(slot_count, width)
    all_grads = replicas(got_grads)
    down_rows = product_back(all_grads, down_mat)
    seq_rows = both_all.shape[0]
    query_heads = queries.reshape(tok_rows, head_count, head_size)
    key_heads = both_all[:, :width].reshape(seq_rows, head_count, head_size)
    value_heads = both_all[:, width:].reshape(seq_rows, head_count, head_size)
    attn_probs = probs_low.astype(jnp.float32)
    gate_probs = gates[:, :expert_count]
    gate_pick = jnp.sum(gate_probs[:, None, :] * choice_hot, axis=-1)
    moe_in = rms_scale(residual, moe_gain)
    got = sent(slot_rows.reshape(slot_count, -1), 1)
    all_got = replicas(got)
    own_rows, own_picks = got[:, :width], join_scalar(got[:, width:])
    hidden, gate_back, up_back = expert_parts(
        own_rows, own_picks, down_rows[: got.shape[0]], gate_mat, up_mat
    )
    pick_slots = jnp.sum(hidden * down_rows[: got.shape[0]], axis=1, keepdims=True)
    row_back = rounded(product_back(gate_back, gate_mat) + product_back(up_back, up_mat))
    back = sent(jnp.concatenate([row_back, split_scalar(pick_slots)], axis=1), 2)
    expert_out = rounded(product(rounded(hidden), down_mat))
    out_slots = sent(expert_out, 3)
    output = rounded(
        residual
        + gate_pick[:, 0:1] * product(select_lead, out_slots)
        + gate_pick[:, 1:2] * product(select_trail, out_slots)
    )

    slot_pick_back = join_scalar(back[:, width:])
    pick_back = jnp.concatenate(
        [
            jnp.dot(select_lead.astype(jnp.float32), slot_pick_back, precision=highest),
            jnp.dot(select_trail.astype(jnp.float32), slot_pick_back, precision=highest),
        ],
        axis=1,
    )
    prob_back = jnp.sum(pick_back[:, :, None] * choice_hot, axis=1)
    logit_back = gate_probs * (prob_back - jnp.sum(gate_probs * prob_back, axis=-1, keepdims=True))
    router_grad = lax.dot_general(moe_in, logit_back, (((0,), (0,)), ((), ())), precision=highest)
    moe_back = product(select_both, back[:, :width]) + lax.dot_general(
        logit_back, router_weight, (((1,), (1,)), ((), ())), precision=highest
    )
    _, moe_pull = jax.vjp(rms_scale, residual, moe_gain)
    residual_part, moe_gain_grad = moe_pull(moe_back)
    residual_grad = out_grad + residual_part
    branch_grad = rounded(residual_grad)
    out_wgrad = product_left(mixed, branch_grad)
    mixed_grad = rounded(product_back(branch_grad, out_weight)).reshape(tok_rows, head_count, head_size)

    prob_part = jnp.einsum("qhd,khd->hqk", mixed_grad, value_heads, preferred_element_type=jnp.float32)
    score_back = rounded(
        attn_probs * (prob_part - jnp.sum(attn_probs * prob_part, axis=-1, keepdims=True))
    )
    query_grad = rounded(
        jnp.einsum("hqk,khd->qhd", score_back, key_heads, preferred_element_type=jnp.float32) * 0.125
    ).reshape(tok_rows, width)
    key_part = (
        jnp.einsum("hqk,qhd->khd", score_back, query_heads, preferred_element_type=jnp.float32)
    ).reshape(seq_rows, width)
    value_part = jnp.einsum(
        "hqk,qhd->khd", probs_low, mixed_grad, preferred_element_type=jnp.float32
    ).reshape(seq_rows, width)
    both_part = jnp.concatenate([key_part, value_part], axis=1)
    far_part = lax.ppermute(rounded(both_part[tok_rows:]), "erow", [(0, 1), (1, 0)])
    both_grad = rounded(both_part[:tok_rows] + far_part.astype(jnp.float32))
    key_grad, value_grad = both_grad[:, :width], both_grad[:, width:]
    bias_grad = jnp.einsum("tlx,mlx->tm", score_back, bias_onehot, preferred_element_type=jnp.float32)
    normed_grad = (
        product_back(query_grad, query_weight)
        + product_back(key_grad, key_weight)
        + product_back(value_grad, value_weight)
    )
    _, attn_pull = jax.vjp(rms_scale, inputs, attn_gain)
    input_part, attn_gain_grad = attn_pull(normed_grad)
    token_grad = residual_grad + input_part

    width_share, hidden_share = width // n_dp, hidden_width // n_dp
    all_rows, all_picks = all_got[:, :width], join_scalar(all_got[:, width:])
    all_hidden, all_gate_back, all_up_back = expert_parts(
        all_rows, all_picks, down_rows, gate_mat, up_mat
    )
    rows_part = lax.dynamic_slice_in_dim(all_rows, replica * width_share, width_share, 1)
    hidden_part = lax.dynamic_slice_in_dim(
        rounded(all_picks * all_hidden), replica * hidden_share, hidden_share, 1
    )
    gate_total = product_left(rows_part, all_gate_back)
    up_total = product_left(rows_part, all_up_back)
    down_total = product_left(hidden_part, all_grads)

    device_count = n_dp * n_row * n_col
    bias_column = jnp.pad(
        bias_grad.reshape(device_count, -1),
        ((0, 0), (0, (width - head_count * bucket_count) // device_count)),
    ).reshape(-1, 1)
    small = jnp.concatenate([attn_gain_grad[:, None], moe_gain_grad[:, None], bias_column, router_grad], axis=1)
    small = jnp.pad(small, ((0, 0), (0, LANES - small.shape[1])))
    wgrads = [rounded(out_wgrad)] + [
        rounded(product_left(normed, grad)) for grad in (query_grad, key_grad, value_grad)
    ]
    out_sum, query_sum, key_sum, value_sum, small_sum = reduce_shares(
        wgrads + [small], (n_dp, n_row, n_col), 4
    )
    bias_share = head_count * bucket_count // device_count
    return (
        output[None],
        token_grad[None],
        small_sum[:, 0],
        query_sum,
        key_sum,
        value_sum,
        out_sum,
        small_sum[:bias_share, 2],
        small_sum[:, 1],
        small_sum[:, 3 : 3 + expert_count],
        gate_total[None],
        up_total[None],
        down_total[None],
    )


def solution(mesh):
    rows = P(("dp", "ecol"), "erow", None)
    experts = P(("erow", "ecol"), None, None)
    every = ("dp", "erow", "ecol")
    shares = P(("erow", "ecol"), "dp", None)
    return jax.shard_map(
        body,
        mesh=mesh,
        in_specs=(
            (rows, P(("dp", "ecol")), rows) + (P(),) * 8 + (experts, experts, experts, rows)
        ),
        out_specs=(rows, rows, P(every))
        + (P(every, None),) * 4
        + (P(every), P(every), P(every, None), shares, shares, shares),
        check_vma=False,
    )
```

```python
import functools

import jax
import jax.numpy as jnp
from jax import lax
from jax.experimental import pallas as pl
from jax.experimental.pallas import tpu as pltpu
from jax.sharding import PartitionSpec as P

epsilon = 1e-06
highest = lax.Precision.HIGHEST
thresholds = (12, 16, 23, 32, 46, 64, 91)
MESH = pl.DeviceIdType.MESH
LANES = 128
VMEM_LIMIT = 60 * 1024 * 1024


def rms_scale(inputs, norm_gain):
    return (
        inputs * lax.rsqrt(jnp.mean(inputs * inputs, axis=-1, keepdims=True) + epsilon) * norm_gain
    )


def bucket_of(offset):
    distance = jnp.abs(offset)
    larger = 8 + sum(((distance >= bound_at).astype(jnp.int32) for bound_at in thresholds))
    return jnp.where(offset > 0, 16, 0) + jnp.where(distance < 8, distance, larger)


def rounded(values):
    return values.astype(jnp.bfloat16)


def product(left_side, right_side):
    return jnp.dot(left_side, right_side, preferred_element_type=jnp.float32)


def product_back(left_side, right_side):
    return lax.dot_general(
        left_side, right_side, (((1,), (1,)), ((), ())), preferred_element_type=jnp.float32
    )


def product_left(left_side, right_side):
    return lax.dot_general(
        left_side, right_side, (((0,), (0,)), ((), ())), preferred_element_type=jnp.float32
    )


def greet(devices):
    barrier = pltpu.get_barrier_semaphore()
    for device in devices:
        pl.semaphore_signal(barrier, 1, device_id=device, device_id_type=MESH)
    pl.semaphore_wait(barrier, len(devices))


def remote(source, target, send_sem, recv_sem, device):
    return pltpu.make_async_remote_copy(
        src_ref=source,
        dst_ref=target,
        send_sem=send_sem,
        recv_sem=recv_sem,
        device_id=device,
        device_id_type=MESH,
    )


def flipped(index, mask, size):
    bit = 1
    while bit < size:
        if mask & bit:
            index = index + bit * (1 - 2 * lax.rem(lax.div(index, bit), 2))
        bit *= 2
    return index


def partners(n_row, n_col):
    row, col = lax.axis_index("erow"), lax.axis_index("ecol")
    return [
        {"erow": flipped(row, place % n_row, n_row), "ecol": flipped(col, place // n_row, n_col)}
        for place in range(n_row * n_col)
    ]


def exchange_kernel(sizes, blocks, landed, send_sems, recv_sems, own_sem):
    devices = partners(*sizes)
    greet(devices[1:])
    own = pltpu.make_async_copy(blocks.at[0], landed.at[0], own_sem)
    own.start()
    copies = []
    for place in range(1, len(devices)):
        copy = remote(
            blocks.at[place],
            landed.at[place],
            send_sems.at[place - 1],
            recv_sems.at[place - 1],
            devices[place],
        )
        copy.start()
        copies.append(copy)
    for copy in copies:
        copy.wait()
    own.wait()


def exchange(blocks, sizes, number):
    peers = sizes[0] * sizes[1] - 1
    return pl.pallas_call(
        functools.partial(exchange_kernel, sizes),
        out_shape=jax.ShapeDtypeStruct(blocks.shape, blocks.dtype),
        in_specs=[pl.BlockSpec(memory_space=pl.ANY)],
        out_specs=pl.BlockSpec(memory_space=pl.ANY),
        scratch_shapes=[
            pltpu.SemaphoreType.DMA((peers,)),
            pltpu.SemaphoreType.DMA((peers,)),
            pltpu.SemaphoreType.DMA,
        ],
        compiler_params=pltpu.CompilerParams(collective_id=number, has_side_effects=True),
    )(blocks)


def replicas(block):
    half = block.shape[0] // 2
    first = [(at, at ^ 1) for at in range(4)]
    second = [(at, at ^ 2) for at in range(4)]
    by_first = lax.ppermute(block, "dp", first)
    by_second = lax.ppermute(block, "dp", second)
    upper = lax.ppermute(by_first[:half], "dp", second)
    lower = lax.ppermute(by_second[half:], "dp", first)
    return [block, by_first, by_second, upper, lower]


class ShareSum:
    stages = 5

    def __init__(self, sizes, depth, grads, totals, held, send_sems, recv_sems):
        self.n_row, self.n_col = sizes
        self.depth, self.grads, self.totals, self.held = depth, grads, totals, held
        self.send_sems, self.recv_sems = send_sems, recv_sems
        dp, self.row, self.col = (lax.axis_index(name) for name in ("dp", "erow", "ecol"))
        self.slow, self.fast = lax.div(dp, 2), lax.rem(dp, 2)
        self.over_row = {"erow": 1 - self.row}
        self.over_fast = {"dp": self.slow * 2 + 1 - self.fast}
        self.over_slow = {"dp": (1 - self.slow) * 2 + self.fast}
        self.over_col = [{"ecol": flipped(self.col, mask, self.n_col)} for mask in range(1, self.n_col)]
        self.devices = [self.over_row, self.over_fast, self.over_slow] + self.over_col

    def parts(self, at):
        width = self.grads[at].shape[-1]
        if width >= 2 * LANES:
            return ((0, pl.ds(0, width // 2)), (1, pl.ds(width // 2, width // 2)))
        return ((0, pl.ds(0, width)),)

    def copy(self, at, number):
        from_row, from_near, from_far, late_sum, from_col = self.held[at]
        sems = (self.send_sems.at[at, number], self.recv_sems.at[at, number])
        if number == 0:
            return remote(self.grads[at].at[:, :, 1 - self.row], from_row, *sems, self.over_row)
        if number <= 4:
            which, cut = self.parts(at)[(number - 1) % 2]
            if number == 1:
                return remote(from_row.at[:, 1 - self.fast, :, cut], from_near.at[:, :, cut], *sems, self.over_fast)
            if number == 2:
                return remote(from_row.at[1 - self.slow, :, :, cut], from_near.at[:, :, cut], *sems, self.over_slow)
            if number == 3:
                return remote(from_near.at[1 - self.slow, :, cut], from_far.at[:, cut], *sems, self.over_slow)
            return remote(from_near.at[1 - self.fast, :, cut], from_far.at[:, cut], *sems, self.over_fast)
        mask = number - 4
        peer = flipped(self.col, mask, self.n_col)
        return remote(late_sum.at[peer], from_col.at[mask - 1], *sems, self.over_col[mask - 1])

    def step(self, at, stage):
        from_row, from_near, from_far, late_sum, from_col = self.held[at]
        if stage == 0:
            self.copy(at, 0).start()
        elif stage == 1:
            self.copy(at, 0).wait()
            for high in range(2):
                for low in range(2):
                    from_row[high, low] = (
                        self.grads[at][high, low, self.row].astype(jnp.float32)
                        + from_row[high, low].astype(jnp.float32)
                    ).astype(from_row.dtype)
            for which, _ in self.parts(at):
                self.copy(at, 1 + which).start()
        elif stage == 2:
            for which, cut in self.parts(at):
                self.copy(at, 1 + which).wait()
                for place in range(2):
                    kept = from_row[place, self.fast, :, cut] if which == 0 else from_row[self.slow, place, :, cut]
                    from_near[place, :, cut] = (
                        kept.astype(jnp.float32) + from_near[place, :, cut].astype(jnp.float32)
                    ).astype(from_near.dtype)
                self.copy(at, 3 + which).start()
        elif stage == 3:
            for which, cut in self.parts(at):
                self.copy(at, 3 + which).wait()
                kept = from_near[self.slow if which == 0 else self.fast, :, cut]
                total = kept.astype(jnp.float32) + from_far[:, cut].astype(jnp.float32)
                late_sum[:, :, cut] = total.reshape(self.n_col, self.depth, -1).astype(late_sum.dtype)
            for mask in range(1, self.n_col):
                self.copy(at, 4 + mask).start()
        else:
            total = late_sum[self.col].astype(jnp.float32)
            for mask in range(1, self.n_col):
                self.copy(at, 4 + mask).wait()
                total = total + from_col[mask - 1].astype(jnp.float32)
            self.totals[at][...] = total

    def turn(self, number):
        for at in range(len(self.grads)):
            if 0 <= number - at < self.stages:
                self.step(at, number - at)

    @property
    def turns(self):
        return len(self.grads) + self.stages - 1


def share_scratch(sizes, depth, width, kind):
    n_row, n_col = sizes
    strip = n_col * depth
    late = kind if depth % 16 == 0 else jnp.float32
    return [
        pltpu.VMEM((2, 2, strip, width), kind),
        pltpu.VMEM((2, strip, width), kind),
        pltpu.VMEM((strip, width), kind),
        pltpu.VMEM((n_col, depth, width), late),
        pltpu.VMEM((n_col - 1, depth, width), late),
    ]


def iota(shape, dimension):
    return lax.broadcasted_iota(jnp.int32, shape, dimension)


def row_slots(routes, live, experts, room, capacity):
    tok = live.shape[1]
    names = iota((experts, tok), 0)
    hot = [(routes[k : k + 1] == names) & live for k in range(2)]
    both = jnp.where(hot[0] | hot[1], 1.0, 0.0).astype(jnp.bfloat16)
    before = jnp.where(iota((tok, tok), 0) < iota((tok, tok), 1), 1.0, 0.0).astype(jnp.bfloat16)
    earlier = product(both, before)
    slots = []
    for k in range(2):
        place = jnp.sum(jnp.where(hot[k], earlier, 0.0), axis=0, keepdims=True)
        slot = routes[k : k + 1].astype(jnp.float32) * room + place
        slots.append(jnp.where(live & (place < capacity), slot, -1.0))
    return slots


def bias_tables(relative_bias, table_width, offset):
    buckets = relative_bias.shape[1]
    place = iota((buckets, table_width), 1)
    distance = jnp.where(place < table_width // 2, place, place - table_width) + offset
    hot = jnp.where(bucket_of(distance) == iota((buckets, table_width), 0), 1.0, 0.0)
    return jnp.dot(relative_bias, hot, precision=highest, preferred_element_type=jnp.float32)


def skewed(row, rows):
    width = row.shape[1]
    full = pltpu.roll(jnp.broadcast_to(row, (rows, width)), 0, 1, stride=1, stride_axis=0)
    return full[:, : width // 2]


def front_kernel(
    dims,
    lengths,
    tokens,
    cotangent,
    routes_row,
    routes_col,
    attn_gain,
    moe_gain,
    relative_bias,
    router,
    query_weight,
    key_weight,
    value_weight,
    out_weight,
    normed_out,
    query_out,
    both_out,
    probs_out,
    mixed_out,
    residual_out,
    gates_out,
    rows_out,
    cot_landed,
    select,
    cot_slots,
    tables,
    held_weights,
    weight_sems,
    own_sem,
    send_sems,
    recv_sems,
    row_send,
    row_recv,
):
    heads, experts, room, capacity, n_row, n_col = dims
    tok, width = tokens.shape
    pair_width = 2 * width // heads
    loads = []
    for at, source in enumerate((key_weight, value_weight, query_weight, out_weight)):
        load = pltpu.make_async_copy(source, held_weights.at[at], weight_sems.at[at])
        load.start()
        loads.append(load)
    devices = partners(n_row, n_col)
    barrier = pltpu.get_barrier_semaphore()
    for device in devices[1:]:
        pl.semaphore_signal(barrier, 1, device_id=device, device_id_type=MESH)

    piece = lax.axis_index("erow")
    length = lengths[0]
    live = iota((1, tok), 1) + piece * tok < length
    slots = row_slots(routes_row[...], live, experts, room, capacity)
    names = iota((experts * room, tok), 0).astype(jnp.float32)
    hot = [jnp.where(names == slot, 1.0, 0.0).astype(jnp.bfloat16) for slot in slots]
    select[...] = hot[0] + hot[1]
    cot_slots[...] = product(select[...], cotangent[...]).astype(jnp.bfloat16).reshape(cot_slots.shape)
    pl.semaphore_wait(barrier, len(devices) - 1)
    own = pltpu.make_async_copy(cot_slots.at[0], cot_landed.at[0], own_sem)
    own.start()
    copies = []
    for place in range(1, len(devices)):
        copy = remote(
            cot_slots.at[place],
            cot_landed.at[place],
            send_sems.at[place - 1],
            recv_sems.at[place - 1],
            devices[place],
        )
        copy.start()
        copies.append(copy)

    inputs = tokens[...].astype(jnp.float32)
    scale = lax.rsqrt(jnp.mean(inputs * inputs, axis=1, keepdims=True) + epsilon)
    normed = (inputs * scale * attn_gain[...]).astype(jnp.bfloat16)
    normed_out[...] = normed
    loads[0].wait()
    both_out[:tok, :width] = product(normed, held_weights[0]).astype(jnp.bfloat16)
    loads[1].wait()
    both_out[:tok, width:] = product(normed, held_weights[1]).astype(jnp.bfloat16)
    pair_copy = remote(both_out.at[pl.ds(0, tok)], both_out.at[pl.ds(tok, tok)], row_send, row_recv, devices[1])
    pair_copy.start()
    loads[2].wait()
    query_out[...] = (product(normed, held_weights[2]) * 0.125).astype(jnp.bfloat16)
    offset = tok * (1 - 2 * piece)
    tables[:, : 2 * tok] = bias_tables(relative_bias[...], 2 * tok, 0)
    tables[:, 2 * tok :] = bias_tables(relative_bias[...], 2 * tok, offset)
    place = iota((1, 2 * tok), 1)
    position = jnp.where(place < tok, place + piece * tok, place - tok + (1 - piece) * tok)
    dead = jnp.where(position < length, 0.0, -1000000000.0)
    low_half = iota((tok, pair_width), 1) < pair_width // 2
    pair_copy.wait()

    def attend(pair, carry):
        lanes = pl.ds(pl.multiple_of(pair * pair_width, pair_width), pair_width)
        value_lanes = pl.ds(pl.multiple_of(width + pair * pair_width, pair_width), pair_width)
        queries, keys, values = query_out[:, lanes], both_out[:, lanes], both_out[:, value_lanes]
        results = []
        for member in range(2):
            mask = low_half if member == 0 else jnp.logical_not(low_half)
            head = 2 * pair + member
            scores = product_back(jnp.where(mask, queries, jnp.zeros_like(queries)), keys)
            table = tables[pl.ds(head, 1)]
            bias = jnp.concatenate([skewed(table[:, : 2 * tok], tok), skewed(table[:, 2 * tok :], tok)], axis=1)
            scores = scores + bias + dead
            powers = jnp.exp(scores - jnp.max(scores, axis=1, keepdims=True))
            probs = (powers * (1.0 / jnp.sum(powers, axis=1, keepdims=True))).astype(jnp.bfloat16)
            probs_out[pl.ds(head, 1)] = probs[None]
            results.append(product(probs, values))
        mixed_out[:, lanes] = jnp.where(low_half, results[0], results[1]).astype(jnp.bfloat16)
        return carry

    lax.fori_loop(0, heads // 2, attend, 0)
    loads[3].wait()
    residual = inputs + product(mixed_out[...], held_weights[3])
    residual_out[...] = residual
    scale = lax.rsqrt(jnp.mean(residual * residual, axis=1, keepdims=True) + epsilon)
    moe_in = residual * scale * moe_gain[...]
    logits = jnp.dot(moe_in, router[...], precision=highest, preferred_element_type=jnp.float32)
    lane = iota(logits.shape, 1)
    logits = jnp.where(lane < experts, logits, -1e30)
    powers = jnp.exp(logits - jnp.max(logits, axis=1, keepdims=True))
    gates = powers / jnp.sum(powers, axis=1, keepdims=True)
    gates_out[...] = gates
    panel = jnp.zeros((experts * room, LANES), jnp.float32)
    for k in range(2):
        pick = jnp.sum(jnp.where(routes_col[:, k : k + 1] == lane, gates, 0.0), axis=1, keepdims=True)
        high = pick.astype(jnp.bfloat16)
        low = (pick - high.astype(jnp.float32)).astype(jnp.bfloat16)
        parts = jnp.where(lane == 0, high, jnp.where(lane == 1, low, jnp.zeros_like(low)))
        panel = panel + product(hot[k], parts)
    rows = product(select[...], moe_in.astype(jnp.bfloat16))
    rows_out[:, :, :width] = rows.astype(jnp.bfloat16).reshape(rows_out.shape[0], -1, width)
    rows_out[:, :, width:] = panel.astype(jnp.bfloat16).reshape(rows_out.shape[0], -1, LANES)
    for copy in copies:
        copy.wait()
    own.wait()


def front(dims, number, lengths, tokens, cotangent, routes_row, routes_col, *params):
    heads, experts, room, capacity, n_row, n_col = dims
    tok, width = tokens.shape
    group = n_row * n_col
    blocks = experts * room // group
    half, single = jnp.bfloat16, jnp.float32
    vmem, anywhere = pl.BlockSpec(memory_space=pltpu.VMEM), pl.BlockSpec(memory_space=pl.ANY)
    shapes = [
        ((tok, width), half),
        ((tok, width), half),
        ((2 * tok, 2 * width), half),
        ((heads, tok, 2 * tok), half),
        ((tok, width), half),
        ((tok, width), single),
        ((tok, LANES), single),
        ((group, blocks, width + LANES), half),
        ((group, blocks, width), half),
    ]
    return pl.pallas_call(
        functools.partial(front_kernel, dims),
        out_shape=[jax.ShapeDtypeStruct(shape, kind) for shape, kind in shapes],
        in_specs=[pl.BlockSpec(memory_space=pltpu.SMEM)] + [vmem] * 8 + [anywhere] * 4,
        out_specs=[vmem] * 8 + [anywhere],
        scratch_shapes=[
            pltpu.VMEM((experts * room, tok), half),
            pltpu.VMEM((group, blocks, width), half),
            pltpu.VMEM((heads, 4 * tok), single),
            pltpu.VMEM((4, width, width), half),
            pltpu.SemaphoreType.DMA((4,)),
            pltpu.SemaphoreType.DMA,
            pltpu.SemaphoreType.DMA((group - 1,)),
            pltpu.SemaphoreType.DMA((group - 1,)),
            pltpu.SemaphoreType.DMA,
            pltpu.SemaphoreType.DMA,
        ],
        compiler_params=pltpu.CompilerParams(
            collective_id=number, has_side_effects=True, vmem_limit_bytes=VMEM_LIMIT
        ),
    )(lengths, tokens, cotangent, routes_row, routes_col, *params)


def expert_kernel(
    tile,
    sizes,
    rows_sent,
    cot_own,
    gate_weight,
    up_weight,
    down_weight,
    back_landed,
    rows_landed,
    out_rows,
    hidden_all,
    gate_back_all,
    up_back_all,
    gate_mat,
    up_mat,
    down_mat,
    cot,
    down_rows,
    total,
    picks_back,
    back_sent,
    load_sems,
    own_sems,
    send_sems,
    recv_sems,
):
    group, room, width = cot_own.shape
    hidden_width = gate_mat.shape[1]
    loads = []
    for at, (source, target) in enumerate(
        ((cot_own, cot), (down_weight, down_mat), (gate_weight, gate_mat), (up_weight, up_mat))
    ):
        load = pltpu.make_async_copy(source, target, load_sems.at[at])
        load.start()
        loads.append(load)
    devices = partners(*sizes)
    greet(devices[1:])
    copies = {}
    for place in range(group):
        if place == 0:
            copy = pltpu.make_async_copy(rows_sent.at[0], rows_landed.at[0], own_sems.at[0])
        else:
            copy = remote(
                rows_sent.at[place],
                rows_landed.at[place],
                send_sems.at[0, place - 1],
                recv_sems.at[0, place - 1],
                devices[place],
            )
        copy.start()
        copies[0, place] = copy
    tiles = hidden_width // tile
    loads[0].wait()
    loads[1].wait()
    cot_rows = cot[...].reshape(group * room, width)

    def early(at, carry):
        cut = pl.ds(pl.multiple_of(at * tile, tile), tile)
        down_rows[:, cut] = product_back(cot_rows, down_mat[cut, :]).astype(jnp.bfloat16)
        return carry

    lax.fori_loop(0, tiles, early, 0)
    loads[2].wait()
    loads[3].wait()
    part = group // 2
    for half in range(2):
        places = range(half * part, (half + 1) * part)
        for place in places:
            copies[0, place].wait()
        held = slice(half * part, (half + 1) * part)
        strip = slice(half * part * room, (half + 1) * part * room)
        rows = rows_landed[held, :, :width].reshape(part * room, width)
        panel = rows_landed[held, :, width:].reshape(part * room, LANES)
        picks = panel[:, 0:1].astype(jnp.float32) + panel[:, 1:2].astype(jnp.float32)
        total[...] = jnp.zeros_like(total)
        picks_back[...] = jnp.zeros_like(picks_back)

        def middle(at, carry):
            cut = pl.ds(pl.multiple_of(at * tile, tile), tile)
            value, slope = gelu_parts(product(rows, gate_mat[:, cut]))
            up_part = product(rows, up_mat[:, cut])
            hidden = value * up_part
            hidden_all[strip, cut] = hidden.astype(jnp.bfloat16)
            back = down_rows[strip, cut].astype(jnp.float32)
            weighed = hidden * back
            picks_back[...] += sum(weighed[:, at : at + LANES] for at in range(0, tile, LANES))
            back = back * picks
            gate_back = (back * up_part * slope).astype(jnp.bfloat16)
            up_back = (back * value).astype(jnp.bfloat16)
            gate_back_all[strip, cut] = gate_back
            up_back_all[strip, cut] = up_back
            total[...] += product_back(gate_back, gate_mat[:, cut]) + product_back(up_back, up_mat[:, cut])
            return carry

        lax.fori_loop(0, tiles, middle, 0)
        back_sent[held, :, :width] = total[...].astype(jnp.bfloat16).reshape(part, room, width)
        pick = jnp.sum(picks_back[...], axis=1, keepdims=True)
        high = pick.astype(jnp.bfloat16)
        low = (pick - high.astype(jnp.float32)).astype(jnp.bfloat16)
        lane = iota((part * room, LANES), 1)
        parts = jnp.where(lane == 0, high, jnp.where(lane == 1, low, jnp.zeros_like(low)))
        back_sent[held, :, width:] = parts.reshape(part, room, LANES)
        for place in places:
            if place == 0:
                copy = pltpu.make_async_copy(back_sent.at[0], back_landed.at[0], own_sems.at[1])
            else:
                copy = remote(
                    back_sent.at[place],
                    back_landed.at[place],
                    send_sems.at[1, place - 1],
                    recv_sems.at[1, place - 1],
                    devices[place],
                )
            copy.start()
            copies[1, place] = copy

    def outward(at, carry):
        cut = pl.ds(pl.multiple_of(at * tile, tile), tile)
        out = product(hidden_all[...], down_mat[:, cut]).astype(jnp.bfloat16)
        out_rows[:, :, cut] = out.reshape(group, room, tile)
        return carry

    lax.fori_loop(0, width // tile, outward, 0)
    for place in range(group):
        copies[1, place].wait()


def experts_apply(sizes, number, rows_sent, cot_own, gate_weight, up_weight, down_weight):
    group, room, width = cot_own.shape
    hidden_width = gate_weight.shape[1]
    slots = group * room
    half, single = jnp.bfloat16, jnp.float32
    vmem, anywhere = pl.BlockSpec(memory_space=pltpu.VMEM), pl.BlockSpec(memory_space=pl.ANY)
    shapes = [
        rows_sent.shape,
        rows_sent.shape,
        cot_own.shape,
        (slots, hidden_width),
        (slots, hidden_width),
        (slots, hidden_width),
    ]
    return pl.pallas_call(
        functools.partial(expert_kernel, 256, sizes),
        out_shape=[jax.ShapeDtypeStruct(shape, half) for shape in shapes],
        in_specs=[anywhere] * 5,
        out_specs=[anywhere] + [vmem] * 5,
        scratch_shapes=[
            pltpu.VMEM((width, hidden_width), half),
            pltpu.VMEM((width, hidden_width), half),
            pltpu.VMEM((hidden_width, width), half),
            pltpu.VMEM((group, room, width), half),
            pltpu.VMEM((slots, hidden_width), half),
            pltpu.VMEM((slots // 2, width), single),
            pltpu.VMEM((slots // 2, LANES), single),
            pltpu.VMEM(rows_sent.shape, half),
            pltpu.SemaphoreType.DMA((4,)),
            pltpu.SemaphoreType.DMA((2,)),
            pltpu.SemaphoreType.DMA((2, group - 1)),
            pltpu.SemaphoreType.DMA((2, group - 1)),
        ],
        compiler_params=pltpu.CompilerParams(
            collective_id=number, has_side_effects=True, vmem_limit_bytes=VMEM_LIMIT
        ),
    )(rows_sent, cot_own, gate_weight, up_weight, down_weight)


def last_kernel(tile, sizes, depth, *refs):
    pieces = 5
    (normed, query_grad, key_grad, value_grad, mixed, branch_grad, small), refs = refs[:7], refs[7:]
    rows_in, refs = refs[:pieces], refs[pieces:]
    cots_in, refs = refs[:pieces], refs[pieces:]
    (own_in, weights, sums), refs = (refs[:3], refs[3:6], refs[6:11]), refs[11:]
    (gate_out, up_out, down_out), refs = refs[:3], refs[3:]
    (rows, cots, rows_left, mats, own_tiles, tiles_of, own_mats, out_tiles, down_tiles), refs = refs[:9], refs[9:]
    grads, refs = refs[:4], refs[4:]
    held, refs = [refs[5 * at : 5 * at + 5] for at in range(5)], refs[25:]
    load_sems, weight_sems, own_sems, out_sems, down_sem, send_sems, recv_sems = refs
    width, strip = normed.shape[1], grads[0].shape[3]
    hidden_width = weights[0].shape[1]
    tiles = hidden_width // tile
    slots = own_in[0].shape[0]
    total_rows = rows.shape[0]
    share = width // 4
    hidden_share = hidden_width // 4
    replica = lax.axis_index("dp")
    summed = ShareSum(sizes, depth, list(grads) + [small], sums, held, send_sems, recv_sems)
    barrier = pltpu.get_barrier_semaphore()
    for device in summed.devices:
        pl.semaphore_signal(barrier, 1, device_id=device, device_id_type=MESH)
    loads, start = [], 0
    for at, (row_piece, cot_piece) in enumerate(zip(rows_in, cots_in)):
        size = row_piece.shape[0]
        for number, (piece, target) in enumerate(((row_piece, rows), (cot_piece, cots))):
            load = pltpu.make_async_copy(piece, target.at[pl.ds(start, size)], load_sems.at[number, at])
            load.start()
            loads.append(load)
        start += size

    def weight_loads(at, slot):
        cut = pl.ds(pl.multiple_of(at * tile, tile), tile)
        return [
            pltpu.make_async_copy(source, mats.at[number, slot], weight_sems.at[number, slot])
            for number, source in enumerate((weights[0].at[:, cut], weights[1].at[:, cut]))
        ] + [pltpu.make_async_copy(weights[2].at[cut], own_mats.at[slot], weight_sems.at[2, slot])]

    def own_loads(at, slot):
        cut = pl.ds(pl.multiple_of(at * tile, tile), tile)
        return [
            pltpu.make_async_copy(
                source.at[:, cut], own_tiles.at[number, slot], own_sems.at[number, slot]
            )
            for number, source in enumerate(own_in)
        ]

    def out_copies(at, slot):
        cut = pl.ds(pl.multiple_of(at * tile, tile), tile)
        return [
            pltpu.make_async_copy(out_tiles.at[number, slot], target.at[:, cut], out_sems.at[number, slot])
            for number, target in enumerate((gate_out, up_out))
        ]

    for load in weight_loads(0, 0) + own_loads(0, 0):
        load.start()
    left = mixed[...].T
    shape = grads[0].shape
    grads[0][...] = product(left, branch_grad[...]).astype(jnp.bfloat16).reshape(shape)
    left = normed[...].T
    pl.semaphore_wait(barrier, len(summed.devices))
    summed.turn(0)
    grads[1][...] = product(left, query_grad[...]).astype(jnp.bfloat16).reshape(shape)
    grads[2][...] = product(left, key_grad[...]).astype(jnp.bfloat16).reshape(shape)
    grads[3][...] = product(left, value_grad[...]).astype(jnp.bfloat16).reshape(shape)
    summed.turn(1)
    for load in loads:
        load.wait()

    def weigh(at, carry):
        cut = pl.ds(pl.multiple_of(at * 256, 256), 256)
        panel = rows[cut, width:]
        picks = panel[:, 0:1].astype(jnp.float32) + panel[:, 1:2].astype(jnp.float32)
        cots[cut] = (cots[cut].astype(jnp.float32) * picks).astype(jnp.bfloat16)
        lanes = pl.ds(pl.multiple_of(replica * share, share), share)
        rows_left[:, cut] = rows[cut, lanes].T
        return carry

    lax.fori_loop(0, total_rows // 256, weigh, 0)
    first = lax.div(replica * hidden_share, tile)
    last = lax.div((replica + 1) * hidden_share - 1, tile)

    def each_tile(at, carry):
        slot = lax.rem(at, 2)
        for load in weight_loads(at, slot) + own_loads(at, slot):
            load.wait()

        @pl.when(at + 1 < tiles)
        def _():
            for load in weight_loads(at + 1, 1 - slot) + own_loads(at + 1, 1 - slot):
                load.start()

        for number in range(2, summed.turns):
            @pl.when(at == number - 2)
            def _(number=number):
                summed.turn(number)

        def each_block(block, carry):
            cut = pl.ds(pl.multiple_of(block * slots, slots), slots)
            value, slope = gelu_parts(product(rows[cut, :width], mats[0, slot]))
            up_part = product(rows[cut, :width], mats[1, slot])
            back = product_back(cots[cut], own_mats[slot])
            place = pl.ds(pl.multiple_of((block - 1) * slots, slots), slots)
            tiles_of[0, place] = (value * up_part).astype(jnp.bfloat16)
            tiles_of[1, place] = (back * up_part * slope).astype(jnp.bfloat16)
            tiles_of[2, place] = (back * value).astype(jnp.bfloat16)
            return carry

        lax.fori_loop(1, total_rows // slots, each_block, 0)

        @pl.when(at >= 2)
        def _():
            for copy in out_copies(at - 2, slot):
                copy.wait()

        for number in range(2):
            out_tiles[number, slot] = product(rows_left[:, :slots], own_tiles[number + 1, slot]) + product(
                rows_left[:, slots:], tiles_of[number + 1]
            )
        for copy in out_copies(at, slot):
            copy.start()

        @pl.when((at >= first) & (at <= last))
        def _():
            place = pl.ds(pl.multiple_of((at - first) * tile, tile), tile)
            down_tiles[place] = product_left(own_tiles[0, slot], cots[:slots]) + product_left(
                tiles_of[0], cots[slots:]
            )

        return carry

    lax.fori_loop(0, tiles, each_tile, 0)
    offset = pl.multiple_of(replica * hidden_share - first * tile, 8)
    down_copy = pltpu.make_async_copy(down_tiles.at[pl.ds(offset, hidden_share)], down_out, down_sem)
    down_copy.start()
    for at in (tiles - 2, tiles - 1):
        for copy in out_copies(at, at % 2):
            copy.wait()
    for number in range(tiles + 2, summed.turns):
        summed.turn(number)
    down_copy.wait()


def last(sizes, number, shared, small, rows_in, cots_in, own_in, weights):
    n_dp, n_row, n_col = sizes
    normed = shared[0]
    tok, width = normed.shape
    hidden_width = weights[0].shape[1]
    slots = own_in[0].shape[0]
    total_rows = n_dp * slots
    tile = 256
    depth = width // (n_dp * n_row * n_col)
    strip = n_col * depth
    half, single = jnp.bfloat16, jnp.float32
    vmem, anywhere = pl.BlockSpec(memory_space=pltpu.VMEM), pl.BlockSpec(memory_space=pl.ANY)
    small = small.reshape(2, 2, n_row, strip, small.shape[1])
    hidden_share = hidden_width // n_dp
    spans = -(-hidden_share // tile) + 1
    scratch = [
        pltpu.VMEM((total_rows, width + LANES), half),
        pltpu.VMEM((total_rows, width), half),
        pltpu.VMEM((width // n_dp, total_rows), half),
        pltpu.VMEM((2, 2, width, tile), half),
        pltpu.VMEM((3, 2, slots, tile), half),
        pltpu.VMEM((3, total_rows - slots, tile), half),
        pltpu.VMEM((2, tile, width), half),
        pltpu.VMEM((2, 2, width // n_dp, tile), single),
        pltpu.VMEM((spans * tile, width), single),
    ]
    scratch += [pltpu.VMEM((2, 2, n_row, strip, width), half)] * 4
    for _ in range(4):
        scratch += share_scratch((n_row, n_col), depth, width, half)
    scratch += share_scratch((n_row, n_col), depth, LANES, single)
    sems = (5, 4 + n_col)
    scratch += [
        pltpu.SemaphoreType.DMA((2, 5)),
        pltpu.SemaphoreType.DMA((3, 2)),
        pltpu.SemaphoreType.DMA((3, 2)),
        pltpu.SemaphoreType.DMA((2, 2)),
        pltpu.SemaphoreType.DMA,
        pltpu.SemaphoreType.DMA(sems),
        pltpu.SemaphoreType.DMA(sems),
    ]
    out_shape = [jax.ShapeDtypeStruct((depth, width), single)] * 4
    out_shape += [jax.ShapeDtypeStruct((depth, LANES), single)]
    out_shape += [jax.ShapeDtypeStruct((width // n_dp, hidden_width), single)] * 2
    out_shape += [jax.ShapeDtypeStruct((hidden_share, width), single)]
    return pl.pallas_call(
        functools.partial(last_kernel, tile, (n_row, n_col), depth),
        out_shape=out_shape,
        in_specs=[vmem] * 7 + [anywhere] * 16,
        out_specs=[vmem] * 5 + [anywhere] * 3,
        scratch_shapes=scratch,
        compiler_params=pltpu.CompilerParams(
            collective_id=number, has_side_effects=True, vmem_limit_bytes=VMEM_LIMIT
        ),
    )(*shared, small, *rows_in, *cots_in, *own_in, *weights)


def gelu_parts(gate_part):
    square = gate_part * gate_part
    inner = gate_part * (0.7978845608028654 + 0.035677408136300125 * square)
    half = 0.5 + 0.5 * jnp.tanh(inner)
    value = gate_part * half
    slope = half + value * (1.0 - half) * (1.5957691216057308 + 0.21406444881780075 * square)
    return value, slope


def join_scalar(panel):
    return panel[:, 0:1].astype(jnp.float32) + panel[:, 1:2].astype(jnp.float32)


def body(
    tokens,
    lengths,
    routes,
    attn_gain,
    query_weight,
    key_weight,
    value_weight,
    out_weight,
    relative_bias,
    moe_gain,
    router_weight,
    gate_weight,
    up_weight,
    down_weight,
    cotangent,
):
    tok_rows = tokens.shape[1]
    width = tokens.shape[2]
    head_count, bucket_count = relative_bias.shape
    head_size = width // head_count
    expert_count = router_weight.shape[1]
    capacity = 5 * tok_rows // (2 * expert_count)
    room = -(-capacity // 16) * 16
    n_dp, n_row, n_col = (lax.axis_size(name) for name in ("dp", "erow", "ecol"))
    group = n_row * n_col
    slot_count = expert_count * room
    piece = lax.axis_index("erow")
    replica = lax.axis_index("dp")
    inputs = tokens[0].astype(jnp.float32)
    seq_length = lengths[0]
    gate_mat, up_mat, down_mat = gate_weight[0], up_weight[0], down_weight[0]
    hidden_width = gate_mat.shape[1]

    query_pos = piece * tok_rows + jnp.arange(tok_rows, dtype=jnp.int32)
    key_pos = jnp.concatenate([query_pos, query_pos + (1 - 2 * piece) * tok_rows])
    bucket_ids = bucket_of(key_pos[None, :] - query_pos[:, None])
    bias_onehot = (
        jnp.arange(bucket_count, dtype=jnp.int32)[:, None, None] == bucket_ids[None]
    ).astype(jnp.bfloat16)
    tok_live = query_pos < seq_length
    pair_routes = routes[0]
    near_routes = (
        (pair_routes % n_col) ^ lax.axis_index("ecol")
    ) * n_row + ((pair_routes // n_col) ^ piece)
    route_flat = near_routes.reshape(-1)
    pair_live = jnp.broadcast_to(tok_live[:, None], pair_routes.shape).reshape(-1)
    expert_range = jnp.arange(expert_count, dtype=jnp.int32)
    route_hot = ((route_flat[:, None] == expert_range[None, :]) & pair_live[:, None]).astype(jnp.int32)
    earlier = jnp.cumsum(route_hot, axis=0) - route_hot
    position = jnp.sum(earlier * route_hot, axis=1)
    kept_pairs = pair_live & (position < capacity)
    slot_ids = jnp.where(kept_pairs, route_flat * room + position, -1).reshape(tok_rows, 2)
    slot_range = jnp.arange(slot_count, dtype=jnp.int32)
    select_lead = (slot_ids[:, 0:1] == slot_range[None, :]).astype(jnp.bfloat16)
    select_trail = (slot_ids[:, 1:2] == slot_range[None, :]).astype(jnp.bfloat16)
    select_both = select_lead + select_trail
    choice_hot = (pair_routes[:, :, None] == expert_range[None, None, :]).astype(jnp.float32)

    def sent(rows, number):
        return exchange(rows.reshape(group, room, rows.shape[1]), (n_row, n_col), number).reshape(
            rows.shape
        )

    out_grad = cotangent[0].astype(jnp.float32)
    routes_row = jnp.pad(near_routes.T, ((0, 6), (0, 0)))
    (
        normed,
        queries,
        both_all,
        probs_low,
        mixed,
        residual,
        gates,
        slot_rows,
        got_grads,
    ) = front(
        (head_count, expert_count, room, capacity, n_row, n_col),
        0,
        lengths,
        tokens[0],
        cotangent[0],
        routes_row,
        pair_routes,
        attn_gain[None],
        moe_gain[None],
        relative_bias,
        jnp.pad(router_weight, ((0, 0), (0, LANES - expert_count))),
        query_weight,
        key_weight,
        value_weight,
        out_weight,
    )
    seq_rows = both_all.shape[0]
    query_heads = queries.reshape(tok_rows, head_count, head_size)
    key_heads = both_all[:, :width].reshape(seq_rows, head_count, head_size)
    value_heads = both_all[:, width:].reshape(seq_rows, head_count, head_size)
    attn_probs = probs_low.astype(jnp.float32)
    gate_probs = gates[:, :expert_count]
    gate_pick = jnp.sum(gate_probs[:, None, :] * choice_hot, axis=-1)
    moe_in = rms_scale(residual, moe_gain)
    back, got, expert_out, own_hidden, own_gate_back, own_up_back = experts_apply(
        (n_row, n_col), 1, slot_rows, got_grads, gate_mat, up_mat, down_mat
    )
    back = back.reshape(slot_count, -1)
    all_grads = replicas(got_grads.reshape(slot_count, width))
    all_got = replicas(got.reshape(slot_count, -1))
    out_slots = sent(expert_out.reshape(slot_count, width), 3)
    output = rounded(
        residual
        + gate_pick[:, 0:1] * product(select_lead, out_slots)
        + gate_pick[:, 1:2] * product(select_trail, out_slots)
    )

    slot_pick_back = join_scalar(back[:, width:])
    pick_back = jnp.concatenate(
        [
            jnp.dot(select_lead.astype(jnp.float32), slot_pick_back, precision=highest),
            jnp.dot(select_trail.astype(jnp.float32), slot_pick_back, precision=highest),
        ],
        axis=1,
    )
    prob_back = jnp.sum(pick_back[:, :, None] * choice_hot, axis=1)
    logit_back = gate_probs * (prob_back - jnp.sum(gate_probs * prob_back, axis=-1, keepdims=True))
    router_grad = lax.dot_general(moe_in, logit_back, (((0,), (0,)), ((), ())), precision=highest)
    moe_back = product(select_both, back[:, :width]) + lax.dot_general(
        logit_back, router_weight, (((1,), (1,)), ((), ())), precision=highest
    )
    _, moe_pull = jax.vjp(rms_scale, residual, moe_gain)
    residual_part, moe_gain_grad = moe_pull(moe_back)
    residual_grad = out_grad + residual_part
    branch_grad = rounded(residual_grad)
    mixed_grad = rounded(product_back(branch_grad, out_weight)).reshape(tok_rows, head_count, head_size)

    prob_part = jnp.einsum("qhd,khd->hqk", mixed_grad, value_heads, preferred_element_type=jnp.float32)
    score_back = rounded(
        attn_probs * (prob_part - jnp.sum(attn_probs * prob_part, axis=-1, keepdims=True))
    )
    query_grad = rounded(
        jnp.einsum("hqk,khd->qhd", score_back, key_heads, preferred_element_type=jnp.float32) * 0.125
    ).reshape(tok_rows, width)
    key_part = (
        jnp.einsum("hqk,qhd->khd", score_back, query_heads, preferred_element_type=jnp.float32)
    ).reshape(seq_rows, width)
    value_part = jnp.einsum(
        "hqk,qhd->khd", probs_low, mixed_grad, preferred_element_type=jnp.float32
    ).reshape(seq_rows, width)
    both_part = jnp.concatenate([key_part, value_part], axis=1)
    far_part = lax.ppermute(rounded(both_part[tok_rows:]), "erow", [(0, 1), (1, 0)])
    both_grad = rounded(both_part[:tok_rows] + far_part.astype(jnp.float32))
    key_grad, value_grad = both_grad[:, :width], both_grad[:, width:]
    bias_grad = jnp.einsum("tlx,mlx->tm", score_back, bias_onehot, preferred_element_type=jnp.float32)
    normed_grad = (
        product_back(query_grad, query_weight)
        + product_back(key_grad, key_weight)
        + product_back(value_grad, value_weight)
    )
    _, attn_pull = jax.vjp(rms_scale, inputs, attn_gain)
    input_part, attn_gain_grad = attn_pull(normed_grad)
    token_grad = residual_grad + input_part

    device_count = n_dp * n_row * n_col
    bias_column = jnp.pad(
        bias_grad.reshape(device_count, -1),
        ((0, 0), (0, (width - head_count * bucket_count) // device_count)),
    ).reshape(-1, 1)
    small = jnp.concatenate([attn_gain_grad[:, None], moe_gain_grad[:, None], bias_column, router_grad], axis=1)
    small = jnp.pad(small, ((0, 0), (0, LANES - small.shape[1])))
    out_sum, query_sum, key_sum, value_sum, small_sum, gate_total, up_total, down_total = last(
        (n_dp, n_row, n_col),
        4,
        (normed, query_grad, key_grad, value_grad, mixed, branch_grad),
        small,
        all_got,
        all_grads,
        (own_hidden, own_gate_back, own_up_back),
        (gate_mat, up_mat, down_mat),
    )
    bias_share = head_count * bucket_count // device_count
    return (
        output[None],
        token_grad[None],
        small_sum[:, 0],
        query_sum,
        key_sum,
        value_sum,
        out_sum,
        small_sum[:bias_share, 2],
        small_sum[:, 1],
        small_sum[:, 3 : 3 + expert_count],
        gate_total[None],
        up_total[None],
        down_total[None],
    )


def solution(mesh):
    rows = P(("dp", "ecol"), "erow", None)
    experts = P(("erow", "ecol"), None, None)
    every = ("dp", "erow", "ecol")
    shares = P(("erow", "ecol"), "dp", None)
    return jax.shard_map(
        body,
        mesh=mesh,
        in_specs=(
            (rows, P(("dp", "ecol")), rows) + (P(),) * 8 + (experts, experts, experts, rows)
        ),
        out_specs=(rows, rows, P(every))
        + (P(every, None),) * 4
        + (P(every), P(every), P(every, None), shares, shares, shares),
        check_vma=False,
    )
```

```python
import functools

import jax
import jax.numpy as jnp
from jax import lax
from jax.experimental import pallas as pl
from jax.experimental.pallas import tpu as pltpu
from jax.sharding import PartitionSpec as P

epsilon = 1e-06
highest = lax.Precision.HIGHEST
thresholds = (12, 16, 23, 32, 46, 64, 91)
MESH = pl.DeviceIdType.MESH
LANES = 128
VMEM_LIMIT = 60 * 1024 * 1024


def bucket_of(offset):
    distance = jnp.abs(offset)
    larger = 8 + sum(((distance >= bound_at).astype(jnp.int32) for bound_at in thresholds))
    return jnp.where(offset > 0, 16, 0) + jnp.where(distance < 8, distance, larger)


def product(left_side, right_side):
    return jnp.dot(left_side, right_side, preferred_element_type=jnp.float32)


def product_back(left_side, right_side):
    return lax.dot_general(
        left_side, right_side, (((1,), (1,)), ((), ())), preferred_element_type=jnp.float32
    )


def product_left(left_side, right_side):
    return lax.dot_general(
        left_side, right_side, (((0,), (0,)), ((), ())), preferred_element_type=jnp.float32
    )


def greet(devices):
    barrier = pltpu.get_barrier_semaphore()
    for device in devices:
        pl.semaphore_signal(barrier, 1, device_id=device, device_id_type=MESH)
    pl.semaphore_wait(barrier, len(devices))


def remote(source, target, send_sem, recv_sem, device):
    return pltpu.make_async_remote_copy(
        src_ref=source,
        dst_ref=target,
        send_sem=send_sem,
        recv_sem=recv_sem,
        device_id=device,
        device_id_type=MESH,
    )


def flipped(index, mask, size):
    bit = 1
    while bit < size:
        if mask & bit:
            index = index + bit * (1 - 2 * lax.rem(lax.div(index, bit), 2))
        bit *= 2
    return index


def partners(n_row, n_col):
    row, col = lax.axis_index("erow"), lax.axis_index("ecol")
    return [
        {"erow": flipped(row, place % n_row, n_row), "ecol": flipped(col, place // n_row, n_col)}
        for place in range(n_row * n_col)
    ]


class Spread:
    def __init__(self, near, far, send_sems, recv_sems):
        dp = lax.axis_index("dp")
        slow, fast = lax.div(dp, 2), lax.rem(dp, 2)
        self.devices = [{"dp": slow * 2 + 1 - fast}, {"dp": (1 - slow) * 2 + fast}]
        self.near, self.far, self.send_sems, self.recv_sems = near, far, send_sems, recv_sems

    def first(self, source):
        return [
            remote(source, self.near.at[k], self.send_sems.at[k], self.recv_sems.at[k], self.devices[k])
            for k in range(2)
        ]

    def second(self, near=None):
        near = self.near if near is None else near
        half = self.far.shape[0] // 2
        return [
            remote(
                near.at[k, pl.ds(k * half, half)],
                self.far.at[pl.ds(k * half, half)],
                self.send_sems.at[2 + k],
                self.recv_sems.at[2 + k],
                self.devices[1 - k],
            )
            for k in range(2)
        ]


def start_all(copies):
    for copy in copies:
        copy.start()


def wait_all(copies):
    for copy in copies:
        copy.wait()


class ShareSum:
    stages = 5

    def __init__(self, sizes, depth, grads, totals, held, send_sems, recv_sems):
        self.n_row, self.n_col = sizes
        self.depth, self.grads, self.totals, self.held = depth, grads, totals, held
        self.send_sems, self.recv_sems = send_sems, recv_sems
        dp, self.row, self.col = (lax.axis_index(name) for name in ("dp", "erow", "ecol"))
        self.slow, self.fast = lax.div(dp, 2), lax.rem(dp, 2)
        self.over_row = {"erow": 1 - self.row}
        self.over_fast = {"dp": self.slow * 2 + 1 - self.fast}
        self.over_slow = {"dp": (1 - self.slow) * 2 + self.fast}
        self.over_col = [{"ecol": flipped(self.col, mask, self.n_col)} for mask in range(1, self.n_col)]
        self.devices = [self.over_row, self.over_fast, self.over_slow] + self.over_col

    def parts(self, at):
        width = self.grads[at].shape[-1]
        if width >= 2 * LANES:
            return ((0, pl.ds(0, width // 2)), (1, pl.ds(width // 2, width // 2)))
        return ((0, pl.ds(0, width)),)

    def copy(self, at, number):
        from_row, from_near, from_far, late_sum, from_col = self.held[at]
        sems = (self.send_sems.at[at, number], self.recv_sems.at[at, number])
        if number == 0:
            return remote(self.grads[at].at[:, :, 1 - self.row], from_row, *sems, self.over_row)
        if number <= 4:
            which, cut = self.parts(at)[(number - 1) % 2]
            if number == 1:
                return remote(from_row.at[:, 1 - self.fast, :, cut], from_near.at[:, :, cut], *sems, self.over_fast)
            if number == 2:
                return remote(from_row.at[1 - self.slow, :, :, cut], from_near.at[:, :, cut], *sems, self.over_slow)
            if number == 3:
                return remote(from_near.at[1 - self.slow, :, cut], from_far.at[:, cut], *sems, self.over_slow)
            return remote(from_near.at[1 - self.fast, :, cut], from_far.at[:, cut], *sems, self.over_fast)
        mask = number - 4
        peer = flipped(self.col, mask, self.n_col)
        return remote(late_sum.at[peer], from_col.at[mask - 1], *sems, self.over_col[mask - 1])

    def step(self, at, stage):
        from_row, from_near, from_far, late_sum, from_col = self.held[at]
        if stage == 0:
            self.copy(at, 0).start()
        elif stage == 1:
            self.copy(at, 0).wait()
            for high in range(2):
                for low in range(2):
                    from_row[high, low] = (
                        self.grads[at][high, low, self.row].astype(jnp.float32)
                        + from_row[high, low].astype(jnp.float32)
                    ).astype(from_row.dtype)
            for which, _ in self.parts(at):
                self.copy(at, 1 + which).start()
        elif stage == 2:
            for which, cut in self.parts(at):
                self.copy(at, 1 + which).wait()
                for place in range(2):
                    kept = from_row[place, self.fast, :, cut] if which == 0 else from_row[self.slow, place, :, cut]
                    from_near[place, :, cut] = (
                        kept.astype(jnp.float32) + from_near[place, :, cut].astype(jnp.float32)
                    ).astype(from_near.dtype)
                self.copy(at, 3 + which).start()
        elif stage == 3:
            for which, cut in self.parts(at):
                self.copy(at, 3 + which).wait()
                kept = from_near[self.slow if which == 0 else self.fast, :, cut]
                total = kept.astype(jnp.float32) + from_far[:, cut].astype(jnp.float32)
                late_sum[:, :, cut] = total.reshape(self.n_col, self.depth, -1).astype(late_sum.dtype)
            for mask in range(1, self.n_col):
                self.copy(at, 4 + mask).start()
        else:
            total = late_sum[self.col].astype(jnp.float32)
            for mask in range(1, self.n_col):
                self.copy(at, 4 + mask).wait()
                total = total + from_col[mask - 1].astype(jnp.float32)
            self.totals[at][...] = total

    def turn(self, number):
        for at in range(len(self.grads)):
            if 0 <= number - at < self.stages:
                self.step(at, number - at)

    @property
    def turns(self):
        return len(self.grads) + self.stages - 1


def share_scratch(sizes, depth, width, kind):
    n_row, n_col = sizes
    strip = n_col * depth
    late = kind if depth % 16 == 0 else jnp.float32
    return [
        pltpu.VMEM((2, 2, strip, width), kind),
        pltpu.VMEM((2, strip, width), kind),
        pltpu.VMEM((strip, width), kind),
        pltpu.VMEM((n_col, depth, width), late),
        pltpu.VMEM((n_col - 1, depth, width), late),
    ]


def iota(shape, dimension):
    return lax.broadcasted_iota(jnp.int32, shape, dimension)


def row_slots(routes, live, experts, room, capacity):
    tok = live.shape[1]
    names = iota((experts, tok), 0)
    hot = [(routes[k : k + 1] == names) & live for k in range(2)]
    both = jnp.where(hot[0] | hot[1], 1.0, 0.0).astype(jnp.bfloat16)
    before = jnp.where(iota((tok, tok), 0) < iota((tok, tok), 1), 1.0, 0.0).astype(jnp.bfloat16)
    earlier = product(both, before)
    slots = []
    for k in range(2):
        place = jnp.sum(jnp.where(hot[k], earlier, 0.0), axis=0, keepdims=True)
        slot = routes[k : k + 1].astype(jnp.float32) * room + place
        slots.append(jnp.where(live & (place < capacity), slot, -1.0))
    return slots


def bias_tables(relative_bias, table_width, offset):
    buckets = relative_bias.shape[1]
    place = iota((buckets, table_width), 1)
    distance = jnp.where(place < table_width // 2, place, place - table_width) + offset
    hot = jnp.where(bucket_of(distance) == iota((buckets, table_width), 0), 1.0, 0.0)
    return jnp.dot(relative_bias, hot, precision=highest, preferred_element_type=jnp.float32)


def skewed(row, rows):
    width = row.shape[1]
    full = pltpu.roll(jnp.broadcast_to(row, (rows, width)), 0, 1, stride=1, stride_axis=0)
    return full[:, : width // 2]


def front_kernel(
    dims,
    lengths,
    tokens,
    cotangent,
    routes_row,
    routes_col,
    attn_gain,
    moe_gain,
    relative_bias,
    router,
    query_weight,
    key_weight,
    value_weight,
    out_weight,
    normed_out,
    query_out,
    both_out,
    probs_out,
    mixed_out,
    residual_out,
    gates_out,
    rows_out,
    cot_landed,
    cot_near,
    select,
    cot_slots,
    tables,
    held_weights,
    weight_sems,
    own_sem,
    send_sems,
    recv_sems,
    row_send,
    row_recv,
    near_send,
    near_recv,
):
    heads, experts, room, capacity, n_row, n_col = dims
    tok, width = tokens.shape
    pair_width = 2 * width // heads
    loads = []
    for at, source in enumerate((key_weight, value_weight, query_weight, out_weight)):
        load = pltpu.make_async_copy(source, held_weights.at[at], weight_sems.at[at])
        load.start()
        loads.append(load)
    devices = partners(n_row, n_col)
    spread = Spread(cot_near, None, near_send, near_recv)
    part = len(devices) // 2
    barrier = pltpu.get_barrier_semaphore()
    for device in devices[1:] + spread.devices:
        pl.semaphore_signal(barrier, 1, device_id=device, device_id_type=MESH)

    piece = lax.axis_index("erow")
    length = lengths[0]
    live = iota((1, tok), 1) + piece * tok < length
    slots = row_slots(routes_row[...], live, experts, room, capacity)
    names = iota((experts * room, tok), 0).astype(jnp.float32)
    hot = [jnp.where(names == slot, 1.0, 0.0).astype(jnp.bfloat16) for slot in slots]
    select[...] = hot[0] + hot[1]
    cot_slots[...] = product(select[...], cotangent[...]).astype(jnp.bfloat16).reshape(cot_slots.shape)
    pl.semaphore_wait(barrier, len(devices) + 1)
    own = pltpu.make_async_copy(cot_slots.at[0], cot_landed.at[0], own_sem)
    own.start()
    copies = []
    for place in range(1, len(devices)):
        copy = remote(
            cot_slots.at[place],
            cot_landed.at[place],
            send_sems.at[place - 1],
            recv_sems.at[place - 1],
            devices[place],
        )
        copy.start()
        copies.append(copy)

    inputs = tokens[...].astype(jnp.float32)
    scale = lax.rsqrt(jnp.mean(inputs * inputs, axis=1, keepdims=True) + epsilon)
    normed = (inputs * scale * attn_gain[...]).astype(jnp.bfloat16)
    normed_out[...] = normed
    loads[0].wait()
    both_out[:tok, :width] = product(normed, held_weights[0]).astype(jnp.bfloat16)
    loads[1].wait()
    both_out[:tok, width:] = product(normed, held_weights[1]).astype(jnp.bfloat16)
    pair_copy = remote(both_out.at[pl.ds(0, tok)], both_out.at[pl.ds(tok, tok)], row_send, row_recv, devices[1])
    pair_copy.start()
    loads[2].wait()
    query_out[...] = (product(normed, held_weights[2]) * 0.125).astype(jnp.bfloat16)
    offset = tok * (1 - 2 * piece)
    tables[:, : 2 * tok] = bias_tables(relative_bias[...], 2 * tok, 0)
    tables[:, 2 * tok :] = bias_tables(relative_bias[...], 2 * tok, offset)
    place = iota((1, 2 * tok), 1)
    position = jnp.where(place < tok, place + piece * tok, place - tok + (1 - piece) * tok)
    dead = jnp.where(position < length, 0.0, -1000000000.0)
    low_half = iota((tok, pair_width), 1) < pair_width // 2
    pair_copy.wait()

    def attend(pair, carry):
        lanes = pl.ds(pl.multiple_of(pair * pair_width, pair_width), pair_width)
        value_lanes = pl.ds(pl.multiple_of(width + pair * pair_width, pair_width), pair_width)
        queries, keys, values = query_out[:, lanes], both_out[:, lanes], both_out[:, value_lanes]

        @pl.when(pair == 1)
        def _():
            wait_all([own] + copies[: part - 1])
            start_all(spread.first(cot_landed.at[pl.ds(0, part)]))

        results = []
        for member in range(2):
            mask = low_half if member == 0 else jnp.logical_not(low_half)
            head = 2 * pair + member
            scores = product_back(jnp.where(mask, queries, jnp.zeros_like(queries)), keys)
            table = tables[pl.ds(head, 1)]
            bias = jnp.concatenate([skewed(table[:, : 2 * tok], tok), skewed(table[:, 2 * tok :], tok)], axis=1)
            scores = scores + bias + dead
            powers = jnp.exp(scores - jnp.max(scores, axis=1, keepdims=True))
            probs = (powers * (1.0 / jnp.sum(powers, axis=1, keepdims=True))).astype(jnp.bfloat16)
            probs_out[pl.ds(head, 1)] = probs[None]
            results.append(product(probs, values))
        mixed_out[:, lanes] = jnp.where(low_half, results[0], results[1]).astype(jnp.bfloat16)
        return carry

    lax.fori_loop(0, heads // 2, attend, 0)
    loads[3].wait()
    residual = inputs + product(mixed_out[...], held_weights[3])
    residual_out[...] = residual
    scale = lax.rsqrt(jnp.mean(residual * residual, axis=1, keepdims=True) + epsilon)
    moe_in = residual * scale * moe_gain[...]
    logits = jnp.dot(moe_in, router[...], precision=highest, preferred_element_type=jnp.float32)
    lane = iota(logits.shape, 1)
    logits = jnp.where(lane < experts, logits, -1e30)
    powers = jnp.exp(logits - jnp.max(logits, axis=1, keepdims=True))
    gates = powers / jnp.sum(powers, axis=1, keepdims=True)
    gates_out[...] = gates
    panel = jnp.zeros((experts * room, LANES), jnp.float32)
    for k in range(2):
        pick = jnp.sum(jnp.where(routes_col[:, k : k + 1] == lane, gates, 0.0), axis=1, keepdims=True)
        high = pick.astype(jnp.bfloat16)
        low = (pick - high.astype(jnp.float32)).astype(jnp.bfloat16)
        parts = jnp.where(lane == 0, high, jnp.where(lane == 1, low, jnp.zeros_like(low)))
        panel = panel + product(hot[k], parts)
    rows = product(select[...], moe_in.astype(jnp.bfloat16))
    rows_out[:, :, :width] = rows.astype(jnp.bfloat16).reshape(rows_out.shape[0], -1, width)
    rows_out[:, :, width:] = panel.astype(jnp.bfloat16).reshape(rows_out.shape[0], -1, LANES)
    wait_all(copies[part - 1 :])
    wait_all(spread.first(cot_landed.at[pl.ds(0, part)]))


def front(dims, number, lengths, tokens, cotangent, routes_row, routes_col, *params):
    heads, experts, room, capacity, n_row, n_col = dims
    tok, width = tokens.shape
    group = n_row * n_col
    blocks = experts * room // group
    half, single = jnp.bfloat16, jnp.float32
    vmem, anywhere = pl.BlockSpec(memory_space=pltpu.VMEM), pl.BlockSpec(memory_space=pl.ANY)
    shapes = [
        ((tok, width), half),
        ((tok, width), half),
        ((2 * tok, 2 * width), half),
        ((heads, tok, 2 * tok), half),
        ((tok, width), half),
        ((tok, width), single),
        ((tok, LANES), single),
        ((group, blocks, width + LANES), half),
        ((group, blocks, width), half),
        ((2, group // 2, blocks, width), half),
    ]
    return pl.pallas_call(
        functools.partial(front_kernel, dims),
        out_shape=[jax.ShapeDtypeStruct(shape, kind) for shape, kind in shapes],
        in_specs=[pl.BlockSpec(memory_space=pltpu.SMEM)] + [vmem] * 8 + [anywhere] * 4,
        out_specs=[vmem] * 8 + [anywhere] * 2,
        scratch_shapes=[
            pltpu.VMEM((experts * room, tok), half),
            pltpu.VMEM((group, blocks, width), half),
            pltpu.VMEM((heads, 4 * tok), single),
            pltpu.VMEM((4, width, width), half),
            pltpu.SemaphoreType.DMA((4,)),
            pltpu.SemaphoreType.DMA,
            pltpu.SemaphoreType.DMA((group - 1,)),
            pltpu.SemaphoreType.DMA((group - 1,)),
            pltpu.SemaphoreType.DMA,
            pltpu.SemaphoreType.DMA,
            pltpu.SemaphoreType.DMA((2,)),
            pltpu.SemaphoreType.DMA((2,)),
        ],
        compiler_params=pltpu.CompilerParams(
            collective_id=number, has_side_effects=True, vmem_limit_bytes=VMEM_LIMIT
        ),
    )(lengths, tokens, cotangent, routes_row, routes_col, *params)


def expert_kernel(
    tile,
    sizes,
    rows_sent,
    cot_own,
    cot_near,
    gate_weight,
    up_weight,
    down_weight,
    back_landed,
    rows_landed,
    out_rows,
    hidden_all,
    gate_back_all,
    up_back_all,
    cot_far,
    cot_near_late,
    cot_far_late,
    rows_near,
    rows_far,
    gate_mat,
    up_mat,
    down_mat,
    cot,
    down_rows,
    total,
    picks_back,
    back_sent,
    load_sems,
    own_sems,
    send_sems,
    recv_sems,
    spread_send,
    spread_recv,
):
    group, room, width = cot_own.shape
    hidden_width = gate_mat.shape[1]
    loads = []
    for at, (source, target) in enumerate(
        ((cot_own, cot), (down_weight, down_mat), (gate_weight, gate_mat), (up_weight, up_mat))
    ):
        load = pltpu.make_async_copy(source, target, load_sems.at[at])
        load.start()
        loads.append(load)
    devices = partners(*sizes)
    part = group // 2
    spreads = [
        Spread(near, far, spread_send.at[at], spread_recv.at[at])
        for at, (near, far) in enumerate(((cot_near, cot_far), (cot_near_late, cot_far_late), (rows_near, rows_far)))
    ]
    late_cots = cot_own.at[pl.ds(part, part)]
    early_rows = rows_landed.at[pl.ds(0, part)]
    greet(devices[1:] + spreads[0].devices)
    copies = {}
    for place in range(group):
        if place == 0:
            copy = pltpu.make_async_copy(rows_sent.at[0], rows_landed.at[0], own_sems.at[0])
        else:
            copy = remote(
                rows_sent.at[place],
                rows_landed.at[place],
                send_sems.at[0, place - 1],
                recv_sems.at[0, place - 1],
                devices[place],
            )
        copy.start()
        copies[0, place] = copy
    start_all(spreads[0].second())
    start_all(spreads[1].first(late_cots))
    tiles = hidden_width // tile
    loads[0].wait()
    loads[1].wait()
    cot_rows = cot[...].reshape(group * room, width)

    def early(at, carry):
        cut = pl.ds(pl.multiple_of(at * tile, tile), tile)
        down_rows[:, cut] = product_back(cot_rows, down_mat[cut, :]).astype(jnp.bfloat16)
        return carry

    lax.fori_loop(0, tiles, early, 0)
    loads[2].wait()
    loads[3].wait()
    for half in range(2):
        places = range(half * part, (half + 1) * part)
        for place in places:
            copies[0, place].wait()
        if half == 0:
            start_all(spreads[2].first(early_rows))
        held = slice(half * part, (half + 1) * part)
        strip = slice(half * part * room, (half + 1) * part * room)
        rows = rows_landed[held, :, :width].reshape(part * room, width)
        panel = rows_landed[held, :, width:].reshape(part * room, LANES)
        picks = panel[:, 0:1].astype(jnp.float32) + panel[:, 1:2].astype(jnp.float32)
        total[...] = jnp.zeros_like(total)
        picks_back[...] = jnp.zeros_like(picks_back)

        def middle(at, carry):
            cut = pl.ds(pl.multiple_of(at * tile, tile), tile)
            value, slope = gelu_parts(product(rows, gate_mat[:, cut]))
            up_part = product(rows, up_mat[:, cut])
            hidden = value * up_part
            hidden_all[strip, cut] = hidden.astype(jnp.bfloat16)
            back = down_rows[strip, cut].astype(jnp.float32)
            weighed = hidden * back
            picks_back[...] += sum(weighed[:, at : at + LANES] for at in range(0, tile, LANES))
            back = back * picks
            gate_back = (back * up_part * slope).astype(jnp.bfloat16)
            up_back = (back * value).astype(jnp.bfloat16)
            gate_back_all[strip, cut] = gate_back
            up_back_all[strip, cut] = up_back
            total[...] += product_back(gate_back, gate_mat[:, cut]) + product_back(up_back, up_mat[:, cut])
            return carry

        lax.fori_loop(0, tiles, middle, 0)
        back_sent[held, :, :width] = total[...].astype(jnp.bfloat16).reshape(part, room, width)
        pick = jnp.sum(picks_back[...], axis=1, keepdims=True)
        high = pick.astype(jnp.bfloat16)
        low = (pick - high.astype(jnp.float32)).astype(jnp.bfloat16)
        lane = iota((part * room, LANES), 1)
        parts = jnp.where(lane == 0, high, jnp.where(lane == 1, low, jnp.zeros_like(low)))
        back_sent[held, :, width:] = parts.reshape(part, room, LANES)
        for place in places:
            if place == 0:
                copy = pltpu.make_async_copy(back_sent.at[0], back_landed.at[0], own_sems.at[1])
            else:
                copy = remote(
                    back_sent.at[place],
                    back_landed.at[place],
                    send_sems.at[1, place - 1],
                    recv_sems.at[1, place - 1],
                    devices[place],
                )
            copy.start()
            copies[1, place] = copy
        if half == 0:
            wait_all(spreads[1].first(late_cots))
            start_all(spreads[1].second())
        else:
            wait_all(spreads[2].first(early_rows))
            start_all(spreads[2].second())

    def outward(at, carry):
        cut = pl.ds(pl.multiple_of(at * tile, tile), tile)
        out = product(hidden_all[...], down_mat[:, cut]).astype(jnp.bfloat16)
        out_rows[:, :, cut] = out.reshape(group, room, tile)
        return carry

    lax.fori_loop(0, width // tile, outward, 0)
    for place in range(group):
        copies[1, place].wait()
    for spread in spreads:
        wait_all(spread.second())


def experts_apply(sizes, number, rows_sent, cot_own, cot_near, gate_weight, up_weight, down_weight):
    group, room, width = cot_own.shape
    hidden_width = gate_weight.shape[1]
    slots = group * room
    half, single = jnp.bfloat16, jnp.float32
    vmem, anywhere = pl.BlockSpec(memory_space=pltpu.VMEM), pl.BlockSpec(memory_space=pl.ANY)
    shapes = [
        rows_sent.shape,
        rows_sent.shape,
        cot_own.shape,
        (slots, hidden_width),
        (slots, hidden_width),
        (slots, hidden_width),
        (group // 2, room, width),
        (2, group // 2, room, width),
        (group // 2, room, width),
        (2, group // 2, room, rows_sent.shape[2]),
        (group // 2, room, rows_sent.shape[2]),
    ]
    return pl.pallas_call(
        functools.partial(expert_kernel, 256, sizes),
        out_shape=[jax.ShapeDtypeStruct(shape, half) for shape in shapes],
        in_specs=[anywhere] * 6,
        out_specs=[anywhere] + [vmem] * 5 + [anywhere] * 5,
        scratch_shapes=[
            pltpu.VMEM((width, hidden_width), half),
            pltpu.VMEM((width, hidden_width), half),
            pltpu.VMEM((hidden_width, width), half),
            pltpu.VMEM((group, room, width), half),
            pltpu.VMEM((slots, hidden_width), half),
            pltpu.VMEM((slots // 2, width), single),
            pltpu.VMEM((slots // 2, LANES), single),
            pltpu.VMEM(rows_sent.shape, half),
            pltpu.SemaphoreType.DMA((4,)),
            pltpu.SemaphoreType.DMA((2,)),
            pltpu.SemaphoreType.DMA((2, group - 1)),
            pltpu.SemaphoreType.DMA((2, group - 1)),
            pltpu.SemaphoreType.DMA((3, 4)),
            pltpu.SemaphoreType.DMA((3, 4)),
        ],
        compiler_params=pltpu.CompilerParams(
            collective_id=number, has_side_effects=True, vmem_limit_bytes=VMEM_LIMIT
        ),
    )(rows_sent, cot_own, cot_near, gate_weight, up_weight, down_weight)


def column_slots(routes, live, experts, room, capacity):
    tok = live.shape[0]
    names = iota((tok, experts), 1)
    hot = [(routes[:, k : k + 1] == names) & live for k in range(2)]
    both = jnp.where(hot[0] | hot[1], 1.0, 0.0).astype(jnp.bfloat16)
    before = jnp.where(iota((tok, tok), 1) < iota((tok, tok), 0), 1.0, 0.0).astype(jnp.bfloat16)
    earlier = product(before, both)
    slots = []
    for k in range(2):
        place = jnp.sum(jnp.where(hot[k], earlier, 0.0), axis=1, keepdims=True)
        slot = routes[:, k : k + 1].astype(jnp.float32) * room + place
        slots.append(jnp.where(live & (place < capacity), slot, -1.0))
    return slots


def halves(values):
    high = values.astype(jnp.bfloat16)
    return high, (values - high.astype(jnp.float32)).astype(jnp.bfloat16)


def back_kernel(
    dims,
    lengths,
    tokens,
    cotangent,
    near_col,
    routes_col,
    attn_gain,
    moe_gain,
    router,
    residual_in,
    gates_in,
    mixed,
    probs_in,
    queries_in,
    both,
    back_in,
    out_sent,
    rows_own,
    query_weight,
    key_weight,
    value_weight,
    out_weight,
    output,
    token_grad,
    branch_grad,
    query_grad,
    key_grad,
    value_grad,
    small,
    rows_near,
    rows_far,
    back,
    out_landed,
    held_weights,
    mixed_back,
    residual_grad,
    far_sent,
    far_landed,
    near_sum,
    diagonals,
    load_sems,
    own_sem,
    send_sems,
    recv_sems,
    row_send,
    row_recv,
    near_send,
    near_recv,
):
    heads, experts, room, capacity, n_row, n_col, share, depth = dims
    tok, width = tokens.shape
    pair_width = 2 * width // heads
    member_width = pair_width // 2
    slots_count = experts * room
    loads = []
    for at, (source, target) in enumerate(
        ((back_in, back), (out_weight, held_weights.at[0]))
        + tuple((w, held_weights.at[1 + k]) for k, w in enumerate((query_weight, key_weight, value_weight)))
    ):
        load = pltpu.make_async_copy(source, target, load_sems.at[at])
        load.start()
        loads.append(load)
    devices = partners(n_row, n_col)
    spread = Spread(rows_near, rows_far, near_send, near_recv)
    part = len(devices) // 2
    late_rows = rows_own.at[pl.ds(part, part)]
    greet(devices[1:] + spread.devices)
    start_all(spread.first(late_rows))
    copies = [pltpu.make_async_copy(out_sent.at[0], out_landed.at[0], own_sem)]
    for place in range(1, len(devices)):
        copies.append(
            remote(
                out_sent.at[place],
                out_landed.at[place],
                send_sems.at[place - 1],
                recv_sems.at[place - 1],
                devices[place],
            )
        )
    for copy in copies:
        copy.start()

    piece = lax.axis_index("erow")
    live = iota((tok, 1), 0) + piece * tok < lengths[0]
    slots = column_slots(near_col[...], live, experts, room, capacity)
    names = iota((tok, slots_count), 1).astype(jnp.float32)
    hot = [jnp.where(names == slot, 1.0, 0.0).astype(jnp.bfloat16) for slot in slots]
    lane = iota((tok, LANES), 1)
    chosen = [routes_col[:, k : k + 1] == lane for k in range(2)]
    gates = gates_in[...]

    residual = residual_in[...]
    scale = lax.rsqrt(jnp.mean(residual * residual, axis=1, keepdims=True) + epsilon)
    moe_in = (residual * scale * moe_gain[...]).astype(jnp.bfloat16)
    loads[0].wait()
    panel = back[:, :, width:].reshape(slots_count, LANES)
    prob_back = jnp.zeros((tok, LANES), jnp.float32)
    for k in range(2):
        parts = product(hot[k], panel)
        prob_back = prob_back + jnp.where(chosen[k], parts[:, 0:1] + parts[:, 1:2], 0.0)
    logit_back = gates * (prob_back - jnp.sum(gates * prob_back, axis=1, keepdims=True))
    logit_high, logit_low = halves(logit_back)
    router_high, router_low = halves(router[...])
    moe_back = (
        product(hot[0] + hot[1], back[:, :, :width].reshape(slots_count, width))
        + product_back(logit_high, router_high)
        + product_back(logit_low, router_high)
        + product_back(logit_high, router_low)
    )
    left = moe_in.T
    router_grad = product(left, logit_high) + product(left, logit_low)
    moe_gain_grad = jnp.sum(residual * scale * moe_back, axis=0, keepdims=True)
    pulled = moe_gain[...] * moe_back
    total = (
        cotangent[...].astype(jnp.float32)
        + scale * pulled
        - residual * (scale * scale * scale * jnp.mean(residual * pulled, axis=1, keepdims=True))
    )
    residual_grad[...] = total
    branch = total.astype(jnp.bfloat16)
    branch_grad[...] = branch
    loads[1].wait()
    mixed_back[...] = product_back(branch, held_weights[0]).astype(jnp.bfloat16)
    reversal = jnp.where(iota((tok, tok), 0) + iota((tok, tok), 1) == tok - 1, 1.0, 0.0).astype(jnp.bfloat16)
    low_half = iota((tok, pair_width), 1) < member_width

    def unattend(pair, carry):
        lanes = pl.ds(pl.multiple_of(pair * pair_width, pair_width), pair_width)
        value_lanes = pl.ds(pl.multiple_of(width + pair * pair_width, pair_width), pair_width)
        keys, values = both[:, lanes], both[:, value_lanes]
        grads = mixed_back[:, lanes]

        @pl.when(pair == heads // 2 - 2)
        def _():
            wait_all(spread.first(late_rows))
            start_all(spread.second())

        queries_left, grads_left = queries_in[:, lanes].T, grads.T
        query_parts, key_parts, value_parts = [], [], []
        for member in range(2):
            head = 2 * pair + member
            mask = low_half if member == 0 else jnp.logical_not(low_half)
            low = probs_in[pl.ds(head, 1)][0]
            probs = low.astype(jnp.float32)
            part = product_back(jnp.where(mask, grads, jnp.zeros_like(grads)), values)
            weighed = probs * part
            score = (weighed - probs * jnp.sum(weighed, axis=1, keepdims=True)).astype(jnp.bfloat16)
            query_parts.append(product(score, keys))
            span = slice(member * member_width, (member + 1) * member_width)
            key_parts.append(product(queries_left[span], score))
            value_parts.append(product(grads_left[span], low))
            exact = product(reversal, score)
            empty = jnp.zeros((tok, tok), jnp.float32)
            padded = jnp.concatenate([exact[:, :tok], empty, exact[:, tok:], empty], axis=1)
            turned = pltpu.roll(padded, 3 * tok + 1, 1, stride=1, stride_axis=0)
            diagonals[pl.ds(head, 1)] = jnp.sum(turned, axis=0, keepdims=True)
        query_grad[:, lanes] = (jnp.where(low_half, query_parts[0], query_parts[1]) * 0.125).astype(jnp.bfloat16)
        key_part = jnp.concatenate(key_parts, axis=0).T
        value_part = jnp.concatenate(value_parts, axis=0).T
        near_sum[:, lanes] = key_part[:tok]
        near_sum[:, value_lanes] = value_part[:tok]
        far_sent[:, lanes] = key_part[tok:].astype(jnp.bfloat16)
        far_sent[:, value_lanes] = value_part[tok:].astype(jnp.bfloat16)
        return carry

    lax.fori_loop(0, heads // 2, unattend, 0)
    pair_copy = remote(far_sent, far_landed, row_send, row_recv, devices[1])
    pair_copy.start()

    segment = width // heads
    table = 4 * tok
    entry = iota((table, LANES), 0)
    other = entry >= table // 4
    other = other & (entry < 3 * table // 4)
    distance = jnp.where(
        other,
        entry - table // 2 + tok * (1 - 2 * piece),
        jnp.where(entry < table // 2, entry, entry - table),
    )
    bucket = bucket_of(distance)
    place = depth * lax.div(bucket, share) + lax.rem(bucket, share)
    target = lax.rem(iota((table, LANES), 1), segment)
    sorted_hot = jnp.where(place == target, 1.0, 0.0).astype(jnp.bfloat16)
    diagonal_high, diagonal_low = halves(diagonals[...])
    bias_rows = product(diagonal_high, sorted_hot) + product(diagonal_low, sorted_hot)
    bias_wide = jnp.concatenate([bias_rows] * (width // LANES), axis=1)
    mine = lax.div(iota((heads, width), 1), segment) == iota((heads, width), 0)
    bias_row = jnp.sum(jnp.where(mine, bias_wide, 0.0), axis=0, keepdims=True)

    loads[2].wait()
    normed_back = product_back(query_grad[...], held_weights[1])
    pair_copy.wait()
    key_total = (near_sum[:, :width] + far_landed[:, :width].astype(jnp.float32)).astype(jnp.bfloat16)
    value_total = (near_sum[:, width:] + far_landed[:, width:].astype(jnp.float32)).astype(jnp.bfloat16)
    key_grad[...] = key_total
    value_grad[...] = value_total
    loads[3].wait()
    loads[4].wait()
    normed_back = normed_back + product_back(key_total, held_weights[2]) + product_back(value_total, held_weights[3])
    inputs = tokens[...].astype(jnp.float32)
    scale = lax.rsqrt(jnp.mean(inputs * inputs, axis=1, keepdims=True) + epsilon)
    attn_gain_grad = jnp.sum(inputs * scale * normed_back, axis=0, keepdims=True)
    pulled = attn_gain[...] * normed_back
    token_grad[...] = (
        residual_grad[...]
        + scale * pulled
        - inputs * (scale * scale * scale * jnp.mean(inputs * pulled, axis=1, keepdims=True))
    )
    empty = jnp.zeros((LANES - 3, width), jnp.float32)
    small[...] = jnp.concatenate([empty, attn_gain_grad, moe_gain_grad, bias_row], axis=0).T + router_grad

    for copy in copies:
        copy.wait()
    results = out_landed[...].reshape(slots_count, width)
    total = residual
    for k in range(2):
        pick = jnp.sum(jnp.where(chosen[k], gates, 0.0), axis=1, keepdims=True)
        total = total + pick * product(hot[k], results)
    output[...] = total.astype(jnp.bfloat16)
    wait_all(spread.second())


def backward(dims, number, *operands):
    heads, experts, room, capacity, n_row, n_col, share, depth = dims
    tokens, back_in, out_sent, rows_own = operands[1], operands[14], operands[15], operands[16]
    tok, width = tokens.shape
    group = n_row * n_col
    half, single = jnp.bfloat16, jnp.float32
    vmem, anywhere = pl.BlockSpec(memory_space=pltpu.VMEM), pl.BlockSpec(memory_space=pl.ANY)
    shapes = [((tok, width), half), ((tok, width), single)] + [((tok, width), half)] * 4 + [((width, LANES), single)]
    shapes += [((2, group // 2) + rows_own.shape[1:], half), ((group // 2,) + rows_own.shape[1:], half)]
    return pl.pallas_call(
        functools.partial(back_kernel, dims),
        out_shape=[jax.ShapeDtypeStruct(shape, kind) for shape, kind in shapes],
        in_specs=[pl.BlockSpec(memory_space=pltpu.SMEM)] + [vmem] * 13 + [anywhere] * 7,
        out_specs=[vmem] * 7 + [anywhere] * 2,
        scratch_shapes=[
            pltpu.VMEM(back_in.shape, half),
            pltpu.VMEM(out_sent.shape, half),
            pltpu.VMEM((4, width, width), half),
            pltpu.VMEM((tok, width), half),
            pltpu.VMEM((tok, width), single),
            pltpu.VMEM((tok, 2 * width), half),
            pltpu.VMEM((tok, 2 * width), half),
            pltpu.VMEM((tok, 2 * width), single),
            pltpu.VMEM((heads, 4 * tok), single),
            pltpu.SemaphoreType.DMA((5,)),
            pltpu.SemaphoreType.DMA,
            pltpu.SemaphoreType.DMA((group - 1,)),
            pltpu.SemaphoreType.DMA((group - 1,)),
            pltpu.SemaphoreType.DMA,
            pltpu.SemaphoreType.DMA,
            pltpu.SemaphoreType.DMA((4,)),
            pltpu.SemaphoreType.DMA((4,)),
        ],
        compiler_params=pltpu.CompilerParams(
            collective_id=number, has_side_effects=True, vmem_limit_bytes=VMEM_LIMIT
        ),
    )(*operands)


def last_kernel(tile, sizes, depth, *refs):
    pieces = 5
    (normed, query_grad, key_grad, value_grad, mixed, branch_grad, small), refs = refs[:7], refs[7:]
    rows_in, refs = refs[:pieces], refs[pieces:]
    cots_in, refs = refs[:pieces], refs[pieces:]
    (own_in, weights, sums), refs = (refs[:3], refs[3:6], refs[6:11]), refs[11:]
    (gate_out, up_out, down_out), refs = refs[:3], refs[3:]
    (rows, cots, rows_left, mats, own_tiles, tiles_of, own_mats, out_tiles, down_tiles), refs = refs[:9], refs[9:]
    grads, refs = refs[:4], refs[4:]
    held, refs = [refs[5 * at : 5 * at + 5] for at in range(5)], refs[25:]
    load_sems, weight_sems, own_sems, out_sems, down_sem, send_sems, recv_sems = refs
    width, strip = normed.shape[1], grads[0].shape[3]
    hidden_width = weights[0].shape[1]
    tiles = hidden_width // tile
    slots = own_in[0].shape[0]
    total_rows = rows.shape[0]
    share = width // 4
    hidden_share = hidden_width // 4
    replica = lax.axis_index("dp")
    summed = ShareSum(sizes, depth, list(grads) + [small], sums, held, send_sems, recv_sems)
    barrier = pltpu.get_barrier_semaphore()
    for device in summed.devices:
        pl.semaphore_signal(barrier, 1, device_id=device, device_id_type=MESH)
    loads, start = [], 0
    for at, (row_piece, cot_piece) in enumerate(zip(rows_in, cots_in)):
        size = row_piece.shape[0]
        for number, (piece, target) in enumerate(((row_piece, rows), (cot_piece, cots))):
            load = pltpu.make_async_copy(piece, target.at[pl.ds(start, size)], load_sems.at[number, at])
            load.start()
            loads.append(load)
        start += size

    def weight_loads(at, slot):
        cut = pl.ds(pl.multiple_of(at * tile, tile), tile)
        return [
            pltpu.make_async_copy(source, mats.at[number, slot], weight_sems.at[number, slot])
            for number, source in enumerate((weights[0].at[:, cut], weights[1].at[:, cut]))
        ] + [pltpu.make_async_copy(weights[2].at[cut], own_mats.at[slot], weight_sems.at[2, slot])]

    def own_loads(at, slot):
        cut = pl.ds(pl.multiple_of(at * tile, tile), tile)
        return [
            pltpu.make_async_copy(
                source.at[:, cut], own_tiles.at[number, slot], own_sems.at[number, slot]
            )
            for number, source in enumerate(own_in)
        ]

    def out_copies(at, slot):
        cut = pl.ds(pl.multiple_of(at * tile, tile), tile)
        return [
            pltpu.make_async_copy(out_tiles.at[number, slot], target.at[:, cut], out_sems.at[number, slot])
            for number, target in enumerate((gate_out, up_out))
        ]

    for load in weight_loads(0, 0) + own_loads(0, 0):
        load.start()
    left = mixed[...].T
    shape = grads[0].shape
    grads[0][...] = product(left, branch_grad[...]).astype(jnp.bfloat16).reshape(shape)
    left = normed[...].T
    pl.semaphore_wait(barrier, len(summed.devices))
    summed.turn(0)
    grads[1][...] = product(left, query_grad[...]).astype(jnp.bfloat16).reshape(shape)
    grads[2][...] = product(left, key_grad[...]).astype(jnp.bfloat16).reshape(shape)
    grads[3][...] = product(left, value_grad[...]).astype(jnp.bfloat16).reshape(shape)
    summed.turn(1)
    for load in loads:
        load.wait()

    def weigh(at, carry):
        cut = pl.ds(pl.multiple_of(at * 256, 256), 256)
        panel = rows[cut, width:]
        picks = panel[:, 0:1].astype(jnp.float32) + panel[:, 1:2].astype(jnp.float32)
        cots[cut] = (cots[cut].astype(jnp.float32) * picks).astype(jnp.bfloat16)
        lanes = pl.ds(pl.multiple_of(replica * share, share), share)
        rows_left[:, cut] = rows[cut, lanes].T
        return carry

    lax.fori_loop(0, total_rows // 256, weigh, 0)
    first = lax.div(replica * hidden_share, tile)
    last = lax.div((replica + 1) * hidden_share - 1, tile)

    def each_tile(at, carry):
        slot = lax.rem(at, 2)
        for load in weight_loads(at, slot) + own_loads(at, slot):
            load.wait()

        @pl.when(at + 1 < tiles)
        def _():
            for load in weight_loads(at + 1, 1 - slot) + own_loads(at + 1, 1 - slot):
                load.start()

        for number in range(2, summed.turns):
            @pl.when(at == number - 2)
            def _(number=number):
                summed.turn(number)

        def each_block(block, carry):
            cut = pl.ds(pl.multiple_of(block * slots, slots), slots)
            value, slope = gelu_parts(product(rows[cut, :width], mats[0, slot]))
            up_part = product(rows[cut, :width], mats[1, slot])
            back = product_back(cots[cut], own_mats[slot])
            place = pl.ds(pl.multiple_of((block - 1) * slots, slots), slots)
            tiles_of[0, place] = (value * up_part).astype(jnp.bfloat16)
            tiles_of[1, place] = (back * up_part * slope).astype(jnp.bfloat16)
            tiles_of[2, place] = (back * value).astype(jnp.bfloat16)
            return carry

        lax.fori_loop(1, total_rows // slots, each_block, 0)

        @pl.when(at >= 2)
        def _():
            for copy in out_copies(at - 2, slot):
                copy.wait()

        for number in range(2):
            out_tiles[number, slot] = product(rows_left[:, :slots], own_tiles[number + 1, slot]) + product(
                rows_left[:, slots:], tiles_of[number + 1]
            )
        for copy in out_copies(at, slot):
            copy.start()

        @pl.when((at >= first) & (at <= last))
        def _():
            place = pl.ds(pl.multiple_of((at - first) * tile, tile), tile)
            down_tiles[place] = product_left(own_tiles[0, slot], cots[:slots]) + product_left(
                tiles_of[0], cots[slots:]
            )

        return carry

    lax.fori_loop(0, tiles, each_tile, 0)
    offset = pl.multiple_of(replica * hidden_share - first * tile, 8)
    down_copy = pltpu.make_async_copy(down_tiles.at[pl.ds(offset, hidden_share)], down_out, down_sem)
    down_copy.start()
    for at in (tiles - 2, tiles - 1):
        for copy in out_copies(at, at % 2):
            copy.wait()
    for number in range(tiles + 2, summed.turns):
        summed.turn(number)
    down_copy.wait()


def last(sizes, number, shared, small, rows_in, cots_in, own_in, weights):
    n_dp, n_row, n_col = sizes
    normed = shared[0]
    tok, width = normed.shape
    hidden_width = weights[0].shape[1]
    slots = own_in[0].shape[0]
    total_rows = n_dp * slots
    tile = 256
    depth = width // (n_dp * n_row * n_col)
    strip = n_col * depth
    half, single = jnp.bfloat16, jnp.float32
    vmem, anywhere = pl.BlockSpec(memory_space=pltpu.VMEM), pl.BlockSpec(memory_space=pl.ANY)
    small = small.reshape(2, 2, n_row, strip, small.shape[1])
    hidden_share = hidden_width // n_dp
    spans = -(-hidden_share // tile) + 1
    scratch = [
        pltpu.VMEM((total_rows, width + LANES), half),
        pltpu.VMEM((total_rows, width), half),
        pltpu.VMEM((width // n_dp, total_rows), half),
        pltpu.VMEM((2, 2, width, tile), half),
        pltpu.VMEM((3, 2, slots, tile), half),
        pltpu.VMEM((3, total_rows - slots, tile), half),
        pltpu.VMEM((2, tile, width), half),
        pltpu.VMEM((2, 2, width // n_dp, tile), single),
        pltpu.VMEM((spans * tile, width), single),
    ]
    scratch += [pltpu.VMEM((2, 2, n_row, strip, width), half)] * 4
    for _ in range(4):
        scratch += share_scratch((n_row, n_col), depth, width, half)
    scratch += share_scratch((n_row, n_col), depth, LANES, single)
    sems = (5, 4 + n_col)
    scratch += [
        pltpu.SemaphoreType.DMA((2, 5)),
        pltpu.SemaphoreType.DMA((3, 2)),
        pltpu.SemaphoreType.DMA((3, 2)),
        pltpu.SemaphoreType.DMA((2, 2)),
        pltpu.SemaphoreType.DMA,
        pltpu.SemaphoreType.DMA(sems),
        pltpu.SemaphoreType.DMA(sems),
    ]
    out_shape = [jax.ShapeDtypeStruct((depth, width), single)] * 4
    out_shape += [jax.ShapeDtypeStruct((depth, LANES), single)]
    out_shape += [jax.ShapeDtypeStruct((width // n_dp, hidden_width), single)] * 2
    out_shape += [jax.ShapeDtypeStruct((hidden_share, width), single)]
    return pl.pallas_call(
        functools.partial(last_kernel, tile, (n_row, n_col), depth),
        out_shape=out_shape,
        in_specs=[vmem] * 7 + [anywhere] * 16,
        out_specs=[vmem] * 5 + [anywhere] * 3,
        scratch_shapes=scratch,
        compiler_params=pltpu.CompilerParams(
            collective_id=number, has_side_effects=True, vmem_limit_bytes=VMEM_LIMIT
        ),
    )(*shared, small, *rows_in, *cots_in, *own_in, *weights)


def gelu_parts(gate_part):
    square = gate_part * gate_part
    inner = gate_part * (0.7978845608028654 + 0.035677408136300125 * square)
    half = 0.5 + 0.5 * jnp.tanh(inner)
    value = gate_part * half
    slope = half + value * (1.0 - half) * (1.5957691216057308 + 0.21406444881780075 * square)
    return value, slope


def flat(*pieces):
    return [piece.reshape(-1, piece.shape[-1]) for piece in pieces]


def body(
    tokens,
    lengths,
    routes,
    attn_gain,
    query_weight,
    key_weight,
    value_weight,
    out_weight,
    relative_bias,
    moe_gain,
    router_weight,
    gate_weight,
    up_weight,
    down_weight,
    cotangent,
):
    tok_rows, width = tokens.shape[1:]
    head_count, bucket_count = relative_bias.shape
    expert_count = router_weight.shape[1]
    capacity = 5 * tok_rows // (2 * expert_count)
    room = -(-capacity // 16) * 16
    n_dp, n_row, n_col = (lax.axis_size(name) for name in ("dp", "erow", "ecol"))
    device_count = n_dp * n_row * n_col
    slot_count = expert_count * room
    gate_mat, up_mat, down_mat = gate_weight[0], up_weight[0], down_weight[0]
    near_routes = ((routes[0] % n_col) ^ lax.axis_index("ecol")) * n_row + (
        (routes[0] // n_col) ^ lax.axis_index("erow")
    )
    router = jnp.pad(router_weight, ((0, 0), (0, LANES - expert_count)))
    dims = (head_count, expert_count, room, capacity, n_row, n_col)
    normed, queries, both, probs, mixed, residual, gates, slot_rows, got_grads, near_grads = front(
        dims,
        0,
        lengths,
        tokens[0],
        cotangent[0],
        near_routes.T,
        routes[0],
        attn_gain[None],
        moe_gain[None],
        relative_bias,
        router,
        query_weight,
        key_weight,
        value_weight,
        out_weight,
    )
    (
        back,
        got,
        expert_out,
        own_hidden,
        own_gate_back,
        own_up_back,
        far_grads,
        near_grads_late,
        far_grads_late,
        near_rows,
        far_rows,
    ) = experts_apply((n_row, n_col), 1, slot_rows, got_grads, near_grads, gate_mat, up_mat, down_mat)
    depth = width // device_count
    bias_share = head_count * bucket_count // device_count
    output, token_grad, branch_grad, query_grad, key_grad, value_grad, small, near_rows_late, far_rows_late = backward(
        dims + (bias_share, depth),
        2,
        lengths,
        tokens[0],
        cotangent[0],
        near_routes,
        routes[0],
        attn_gain[None],
        moe_gain[None],
        router,
        residual,
        gates,
        mixed,
        probs,
        queries,
        both,
        back,
        expert_out,
        got,
        query_weight,
        key_weight,
        value_weight,
        out_weight,
    )
    out_sum, query_sum, key_sum, value_sum, small_sum, gate_total, up_total, down_total = last(
        (n_dp, n_row, n_col),
        3,
        (normed, query_grad, key_grad, value_grad, mixed, branch_grad),
        small,
        flat(got, near_rows, far_rows, near_rows_late, far_rows_late),
        flat(got_grads, near_grads, far_grads, near_grads_late, far_grads_late),
        (own_hidden, own_gate_back, own_up_back),
        (gate_mat, up_mat, down_mat),
    )
    return (
        output[None],
        token_grad[None],
        small_sum[:, LANES - 3],
        query_sum,
        key_sum,
        value_sum,
        out_sum,
        small_sum[:bias_share, LANES - 1],
        small_sum[:, LANES - 2],
        small_sum[:, :expert_count],
        gate_total[None],
        up_total[None],
        down_total[None],
    )


def solution(mesh):
    rows = P(("dp", "ecol"), "erow", None)
    experts = P(("erow", "ecol"), None, None)
    every = ("dp", "erow", "ecol")
    shares = P(("erow", "ecol"), "dp", None)
    return jax.shard_map(
        body,
        mesh=mesh,
        in_specs=(
            (rows, P(("dp", "ecol")), rows) + (P(),) * 8 + (experts, experts, experts, rows)
        ),
        out_specs=(rows, rows, P(every))
        + (P(every, None),) * 4
        + (P(every), P(every), P(every, None), shares, shares, shares),
        check_vma=False,
    )
```

```python
import functools

import jax
import jax.numpy as jnp
from jax import lax
from jax.experimental import pallas as pl
from jax.experimental.pallas import tpu as pltpu
from jax.sharding import PartitionSpec as P

epsilon = 1e-06
highest = lax.Precision.HIGHEST
thresholds = (12, 16, 23, 32, 46, 64, 91)
MESH = pl.DeviceIdType.MESH
LANES = 128
VMEM_LIMIT = 60 * 1024 * 1024


def bucket_of(offset):
    distance = jnp.abs(offset)
    larger = 8 + sum(((distance >= bound_at).astype(jnp.int32) for bound_at in thresholds))
    return jnp.where(offset > 0, 16, 0) + jnp.where(distance < 8, distance, larger)


def product(left_side, right_side):
    return jnp.dot(left_side, right_side, preferred_element_type=jnp.float32)


def product_back(left_side, right_side):
    return lax.dot_general(
        left_side, right_side, (((1,), (1,)), ((), ())), preferred_element_type=jnp.float32
    )


def product_left(left_side, right_side):
    return lax.dot_general(
        left_side, right_side, (((0,), (0,)), ((), ())), preferred_element_type=jnp.float32
    )


def greet(devices):
    barrier = pltpu.get_barrier_semaphore()
    for device in devices:
        pl.semaphore_signal(barrier, 1, device_id=device, device_id_type=MESH)
    pl.semaphore_wait(barrier, len(devices))


def remote(source, target, send_sem, recv_sem, device):
    return pltpu.make_async_remote_copy(
        src_ref=source,
        dst_ref=target,
        send_sem=send_sem,
        recv_sem=recv_sem,
        device_id=device,
        device_id_type=MESH,
    )


def flipped(index, mask, size):
    bit = 1
    while bit < size:
        if mask & bit:
            index = index + bit * (1 - 2 * lax.rem(lax.div(index, bit), 2))
        bit *= 2
    return index


def mirrored(value, size):
    result, bit = value * 0, 1
    while bit < size:
        result = result * 2 + (value // bit) % 2
        bit *= 2
    return result


def partners(n_row, n_col):
    row, col = lax.axis_index("erow"), lax.axis_index("ecol")
    return [
        {
            "erow": flipped(row, place % n_row, n_row),
            "ecol": flipped(col, mirrored(place // n_row, n_col), n_col),
        }
        for place in range(n_row * n_col)
    ]


class Spread:
    def __init__(self, near, far, send_sems, recv_sems):
        dp = lax.axis_index("dp")
        slow, fast = lax.div(dp, 2), lax.rem(dp, 2)
        self.devices = [{"dp": slow * 2 + 1 - fast}, {"dp": (1 - slow) * 2 + fast}]
        self.near, self.far, self.send_sems, self.recv_sems = near, far, send_sems, recv_sems

    def first(self, source):
        return [
            remote(source, self.near.at[k], self.send_sems.at[k], self.recv_sems.at[k], self.devices[k])
            for k in range(2)
        ]

    def second(self, near=None):
        near = self.near if near is None else near
        half = self.far.shape[0] // 2
        return [
            remote(
                near.at[k, pl.ds(k * half, half)],
                self.far.at[pl.ds(k * half, half)],
                self.send_sems.at[2 + k],
                self.recv_sems.at[2 + k],
                self.devices[1 - k],
            )
            for k in range(2)
        ]


def start_all(copies):
    for copy in copies:
        copy.start()


def wait_all(copies):
    for copy in copies:
        copy.wait()


class ShareSum:
    stages = 5

    def __init__(self, sizes, depth, grads, totals, held, send_sems, recv_sems):
        self.n_row, self.n_col = sizes
        self.depth, self.grads, self.totals, self.held = depth, grads, totals, held
        self.send_sems, self.recv_sems = send_sems, recv_sems
        dp, self.row, self.col = (lax.axis_index(name) for name in ("dp", "erow", "ecol"))
        self.slow, self.fast = lax.div(dp, 2), lax.rem(dp, 2)
        self.over_row = {"erow": 1 - self.row}
        self.over_fast = {"dp": self.slow * 2 + 1 - self.fast}
        self.over_slow = {"dp": (1 - self.slow) * 2 + self.fast}
        self.over_col = [{"ecol": flipped(self.col, mask, self.n_col)} for mask in range(1, self.n_col)]
        self.devices = [self.over_row, self.over_fast, self.over_slow] + self.over_col

    def parts(self, at):
        width = self.grads[at].shape[-1]
        if width >= 2 * LANES:
            return ((0, pl.ds(0, width // 2)), (1, pl.ds(width // 2, width // 2)))
        return ((0, pl.ds(0, width)),)

    def copy(self, at, number):
        from_row, from_near, from_far, late_sum, from_col = self.held[at]
        sems = (self.send_sems.at[at, number], self.recv_sems.at[at, number])
        if number == 0:
            return remote(self.grads[at].at[:, :, 1 - self.row], from_row, *sems, self.over_row)
        if number <= 4:
            which, cut = self.parts(at)[(number - 1) % 2]
            if number == 1:
                return remote(from_row.at[:, 1 - self.fast, :, cut], from_near.at[:, :, cut], *sems, self.over_fast)
            if number == 2:
                return remote(from_row.at[1 - self.slow, :, :, cut], from_near.at[:, :, cut], *sems, self.over_slow)
            if number == 3:
                return remote(from_near.at[1 - self.slow, :, cut], from_far.at[:, cut], *sems, self.over_slow)
            return remote(from_near.at[1 - self.fast, :, cut], from_far.at[:, cut], *sems, self.over_fast)
        mask = number - 4
        peer = flipped(self.col, mask, self.n_col)
        return remote(late_sum.at[peer], from_col.at[mask - 1], *sems, self.over_col[mask - 1])

    def step(self, at, stage):
        from_row, from_near, from_far, late_sum, from_col = self.held[at]
        if stage == 0:
            self.copy(at, 0).start()
        elif stage == 1:
            self.copy(at, 0).wait()
            for high in range(2):
                for low in range(2):
                    from_row[high, low] = (
                        self.grads[at][high, low, self.row].astype(jnp.float32)
                        + from_row[high, low].astype(jnp.float32)
                    ).astype(from_row.dtype)
            for which, _ in self.parts(at):
                self.copy(at, 1 + which).start()
        elif stage == 2:
            for which, cut in self.parts(at):
                self.copy(at, 1 + which).wait()
                for place in range(2):
                    kept = from_row[place, self.fast, :, cut] if which == 0 else from_row[self.slow, place, :, cut]
                    from_near[place, :, cut] = (
                        kept.astype(jnp.float32) + from_near[place, :, cut].astype(jnp.float32)
                    ).astype(from_near.dtype)
                self.copy(at, 3 + which).start()
        elif stage == 3:
            for which, cut in self.parts(at):
                self.copy(at, 3 + which).wait()
                kept = from_near[self.slow if which == 0 else self.fast, :, cut]
                total = kept.astype(jnp.float32) + from_far[:, cut].astype(jnp.float32)
                late_sum[:, :, cut] = total.reshape(self.n_col, self.depth, -1).astype(late_sum.dtype)
            for mask in range(1, self.n_col):
                self.copy(at, 4 + mask).start()
        else:
            total = late_sum[self.col].astype(jnp.float32)
            for mask in range(1, self.n_col):
                self.copy(at, 4 + mask).wait()
                total = total + from_col[mask - 1].astype(jnp.float32)
            self.totals[at][...] = total

    def turn(self, number):
        for at in range(len(self.grads)):
            if 0 <= number - at < self.stages:
                self.step(at, number - at)

    @property
    def turns(self):
        return len(self.grads) + self.stages - 1


def share_scratch(sizes, depth, width, kind):
    n_row, n_col = sizes
    strip = n_col * depth
    late = kind if depth % 16 == 0 else jnp.float32
    return [
        pltpu.VMEM((2, 2, strip, width), kind),
        pltpu.VMEM((2, strip, width), kind),
        pltpu.VMEM((strip, width), kind),
        pltpu.VMEM((n_col, depth, width), late),
        pltpu.VMEM((n_col - 1, depth, width), late),
    ]


def iota(shape, dimension):
    return lax.broadcasted_iota(jnp.int32, shape, dimension)


def columns_of(rows, count):
    padded = jnp.concatenate([rows.astype(jnp.float32), jnp.zeros((8 - count, rows.shape[1]), jnp.float32)], axis=0)
    return padded.T


def row_slots(routes, live, experts, room, capacity):
    tok = live.shape[1]
    names = iota((experts, tok), 0)
    hot = [(routes[k : k + 1] == names) & live for k in range(2)]
    both = jnp.where(hot[0] | hot[1], 1.0, 0.0).astype(jnp.bfloat16)
    before = jnp.where(iota((tok, tok), 0) < iota((tok, tok), 1), 1.0, 0.0).astype(jnp.bfloat16)
    earlier = product(both, before)
    slots = []
    for k in range(2):
        place = jnp.sum(jnp.where(hot[k], earlier, 0.0), axis=0, keepdims=True)
        slot = routes[k : k + 1].astype(jnp.float32) * room + place
        slots.append(jnp.where(live & (place < capacity), slot, -1.0))
    return slots


def bias_tables(relative_bias, table_width, offset):
    buckets = relative_bias.shape[1]
    place = iota((buckets, table_width), 1)
    distance = jnp.where(place < table_width // 2, place, place - table_width) + offset
    hot = jnp.where(bucket_of(distance) == iota((buckets, table_width), 0), 1.0, 0.0)
    return jnp.dot(relative_bias, hot, precision=highest, preferred_element_type=jnp.float32)


def skewed(row, rows):
    width = row.shape[1]
    full = pltpu.roll(jnp.broadcast_to(row, (rows, width)), 0, 1, stride=1, stride_axis=0)
    return full[:, : width // 2]


def front_kernel(
    dims,
    lengths,
    tokens,
    cotangent,
    routes_row,
    routes_true,
    attn_gain,
    moe_gain,
    relative_bias,
    router,
    query_weight,
    key_weight,
    value_weight,
    out_weight,
    normed_out,
    query_out,
    both_out,
    probs_out,
    mixed_out,
    residual_out,
    gates_out,
    rows_out,
    cot_landed,
    cot_near,
    cot_far,
    select,
    cot_slots,
    tables,
    held_weights,
    weight_sems,
    own_sem,
    send_sems,
    recv_sems,
    row_send,
    row_recv,
    near_send,
    near_recv,
):
    heads, experts, room, capacity, n_row, n_col = dims
    tok, width = tokens.shape
    pair_width = 2 * width // heads
    loads = []
    for at, source in enumerate((key_weight, value_weight, query_weight, out_weight)):
        load = pltpu.make_async_copy(source, held_weights.at[at], weight_sems.at[at])
        load.start()
        loads.append(load)
    devices = partners(n_row, n_col)
    spread = Spread(cot_near, cot_far, near_send, near_recv)
    part = len(devices) // 4
    barrier = pltpu.get_barrier_semaphore()
    for device in devices[1:] + spread.devices:
        pl.semaphore_signal(barrier, 1, device_id=device, device_id_type=MESH)

    piece = lax.axis_index("erow")
    length = lengths[0]
    live = iota((1, tok), 1) + piece * tok < length
    slots = row_slots(routes_row[...], live, experts, room, capacity)
    names = iota((experts * room, tok), 0).astype(jnp.float32)
    hot = [jnp.where(names == slot, 1.0, 0.0).astype(jnp.bfloat16) for slot in slots]
    select[...] = hot[0] + hot[1]
    cot_slots[...] = product(select[...], cotangent[...]).astype(jnp.bfloat16).reshape(cot_slots.shape)
    pl.semaphore_wait(barrier, len(devices) + 1)
    own = pltpu.make_async_copy(cot_slots.at[0], cot_landed.at[0], own_sem)
    own.start()
    copies = []
    for place in range(1, len(devices)):
        copy = remote(
            cot_slots.at[place],
            cot_landed.at[place],
            send_sems.at[place - 1],
            recv_sems.at[place - 1],
            devices[place],
        )
        copy.start()
        copies.append(copy)

    inputs = tokens[...].astype(jnp.float32)
    scale = lax.rsqrt(jnp.mean(inputs * inputs, axis=1, keepdims=True) + epsilon)
    normed = (inputs * scale * attn_gain[...]).astype(jnp.bfloat16)
    normed_out[...] = normed
    loads[0].wait()
    both_out[:tok, :width] = product(normed, held_weights[0]).astype(jnp.bfloat16)
    loads[1].wait()
    both_out[:tok, width:] = product(normed, held_weights[1]).astype(jnp.bfloat16)
    pair_copy = remote(both_out.at[pl.ds(0, tok)], both_out.at[pl.ds(tok, tok)], row_send, row_recv, devices[1])
    pair_copy.start()
    loads[2].wait()
    query_out[...] = (product(normed, held_weights[2]) * 0.125).astype(jnp.bfloat16)
    offset = tok * (1 - 2 * piece)
    tables[:, : 2 * tok] = bias_tables(relative_bias[...], 2 * tok, 0)
    tables[:, 2 * tok :] = bias_tables(relative_bias[...], 2 * tok, offset)
    place = iota((1, 2 * tok), 1)
    position = jnp.where(place < tok, place + piece * tok, place - tok + (1 - piece) * tok)
    dead = jnp.where(position < length, 0.0, -1000000000.0)
    low_half = iota((tok, pair_width), 1) < pair_width // 2
    pair_copy.wait()

    def attend(pair, carry):
        lanes = pl.ds(pl.multiple_of(pair * pair_width, pair_width), pair_width)
        value_lanes = pl.ds(pl.multiple_of(width + pair * pair_width, pair_width), pair_width)
        queries, keys, values = query_out[:, lanes], both_out[:, lanes], both_out[:, value_lanes]

        @pl.when(pair == 0)
        def _():
            wait_all([own] + copies[: part - 1])
            start_all(spread.first(cot_landed.at[pl.ds(0, part)]))

        @pl.when(pair == heads // 4)
        def _():
            wait_all(spread.first(cot_landed.at[pl.ds(0, part)]))
            start_all(spread.second())

        results = []
        for member in range(2):
            mask = low_half if member == 0 else jnp.logical_not(low_half)
            head = 2 * pair + member
            scores = product_back(jnp.where(mask, queries, jnp.zeros_like(queries)), keys)
            table = tables[pl.ds(head, 1)]
            bias = jnp.concatenate([skewed(table[:, : 2 * tok], tok), skewed(table[:, 2 * tok :], tok)], axis=1)
            scores = scores + bias + dead
            powers = jnp.exp(scores - jnp.max(scores, axis=1, keepdims=True))
            probs = (powers * (1.0 / jnp.sum(powers, axis=1, keepdims=True))).astype(jnp.bfloat16)
            probs_out[pl.ds(head, 1)] = probs[None]
            results.append(product(probs, values))
        mixed_out[:, lanes] = jnp.where(low_half, results[0], results[1]).astype(jnp.bfloat16)
        return carry

    lax.fori_loop(0, heads // 2, attend, 0)
    loads[3].wait()
    residual = inputs + product(mixed_out[...], held_weights[3])
    residual_out[...] = residual
    scale = lax.rsqrt(jnp.mean(residual * residual, axis=1, keepdims=True) + epsilon)
    moe_in = residual * scale * moe_gain[...]
    logits = lax.dot_general(
        moe_in, router[...], (((1,), (1,)), ((), ())), precision=highest, preferred_element_type=jnp.float32
    )
    logits = jnp.concatenate([logits, jnp.full((tok, LANES - experts), -1e30, jnp.float32)], axis=1)
    lane = iota(logits.shape, 1)
    columns = columns_of(routes_true[...], 2)
    powers = jnp.exp(logits - jnp.max(logits, axis=1, keepdims=True))
    gates = powers / jnp.sum(powers, axis=1, keepdims=True)
    gates_out[...] = gates
    panel = jnp.zeros((experts * room, LANES), jnp.float32)
    for k in range(2):
        pick = jnp.sum(jnp.where(columns[:, k : k + 1] == lane.astype(jnp.float32), gates, 0.0), axis=1, keepdims=True)
        high = pick.astype(jnp.bfloat16)
        low = (pick - high.astype(jnp.float32)).astype(jnp.bfloat16)
        parts = jnp.where(lane == 0, high, jnp.where(lane == 1, low, jnp.zeros_like(low)))
        panel = panel + product(hot[k], parts)
    rows = product(select[...], moe_in.astype(jnp.bfloat16))
    rows_out[:, :, :width] = rows.astype(jnp.bfloat16).reshape(rows_out.shape[0], -1, width)
    rows_out[:, :, width:] = panel.astype(jnp.bfloat16).reshape(rows_out.shape[0], -1, LANES)
    wait_all(copies[part - 1 :])
    wait_all(spread.second())


def front(dims, number, lengths, tokens, cotangent, routes_row, routes_col, *params):
    heads, experts, room, capacity, n_row, n_col = dims
    tok, width = tokens.shape
    group = n_row * n_col
    blocks = experts * room // group
    half, single = jnp.bfloat16, jnp.float32
    vmem, anywhere = pl.BlockSpec(memory_space=pltpu.VMEM), pl.BlockSpec(memory_space=pl.ANY)
    shapes = [
        ((tok, width), half),
        ((tok, width), half),
        ((2 * tok, 2 * width), half),
        ((heads, tok, 2 * tok), half),
        ((tok, width), half),
        ((tok, width), single),
        ((tok, LANES), single),
        ((group, blocks, width + LANES), half),
        ((group, blocks, width), half),
        ((2, group // 4, blocks, width), half),
        ((group // 4, blocks, width), half),
    ]
    return pl.pallas_call(
        functools.partial(front_kernel, dims),
        out_shape=[jax.ShapeDtypeStruct(shape, kind) for shape, kind in shapes],
        in_specs=[pl.BlockSpec(memory_space=pltpu.SMEM)] + [vmem] * 8 + [anywhere] * 4,
        out_specs=[vmem] * 8 + [anywhere] * 3,
        scratch_shapes=[
            pltpu.VMEM((experts * room, tok), half),
            pltpu.VMEM((group, blocks, width), half),
            pltpu.VMEM((heads, 4 * tok), single),
            pltpu.VMEM((4, width, width), half),
            pltpu.SemaphoreType.DMA((4,)),
            pltpu.SemaphoreType.DMA,
            pltpu.SemaphoreType.DMA((group - 1,)),
            pltpu.SemaphoreType.DMA((group - 1,)),
            pltpu.SemaphoreType.DMA,
            pltpu.SemaphoreType.DMA,
            pltpu.SemaphoreType.DMA((4,)),
            pltpu.SemaphoreType.DMA((4,)),
        ],
        compiler_params=pltpu.CompilerParams(
            collective_id=number, has_side_effects=True, vmem_limit_bytes=VMEM_LIMIT
        ),
    )(lengths, tokens, cotangent, routes_row, routes_col, *params)


def panel_sum(panel):
    return panel[:, 0:1].astype(jnp.float32) + panel[:, 1:2].astype(jnp.float32)


def expert_kernel(
    tile,
    sizes,
    rows_sent,
    cot_own,
    cot_near0,
    cot_far0,
    gate_weight,
    up_weight,
    down_weight,
    back_landed,
    rows_landed,
    out_rows,
    parts_out,
    cot_near1,
    cot_far1,
    cot_near2,
    cot_far2,
    cot_near3,
    cot_far3,
    rows_near0,
    rows_far0,
    rows_near1,
    rows_far1,
    gate_mat,
    up_mat,
    down_mat,
    cot,
    down_rows,
    hidden_all,
    total,
    picks_back,
    back_sent,
    other_rows,
    other_cots,
    staged,
    load_sems,
    own_sems,
    send_sems,
    recv_sems,
    spread_send,
    spread_recv,
    stage_sems,
    other_sems,
):
    group, room, width = cot_own.shape
    hidden_width = gate_mat.shape[1]
    tiles = hidden_width // tile
    loads = []
    for at, (source, target) in enumerate(
        ((cot_own, cot), (down_weight, down_mat), (gate_weight, gate_mat), (up_weight, up_mat))
    ):
        load = pltpu.make_async_copy(source, target, load_sems.at[at])
        load.start()
        loads.append(load)
    devices = partners(*sizes)
    part, quarter = group // 2, group // 4
    strip = part * room
    cot_spreads = [None] + [
        Spread(near, far, spread_send.at[at], spread_recv.at[at])
        for at, (near, far) in enumerate(((cot_near1, cot_far1), (cot_near2, cot_far2), (cot_near3, cot_far3)))
    ]
    row_spreads = [
        Spread(near, far, spread_send.at[3 + at], spread_recv.at[3 + at])
        for at, (near, far) in enumerate(((rows_near0, rows_far0), (rows_near1, rows_far1)))
    ]
    greet(devices[1:] + row_spreads[0].devices)

    def cots_first(piece):
        return cot_spreads[piece].first(cot_own.at[pl.ds(piece * quarter, quarter)])

    def rows_first(piece):
        return row_spreads[piece].first(rows_landed.at[pl.ds(piece * quarter, quarter)])

    def row_copy(way, place):
        source, target = ((rows_sent, rows_landed), (back_sent, back_landed))[way]
        if place == 0:
            return pltpu.make_async_copy(source.at[0], target.at[0], own_sems.at[way])
        sems = (send_sems.at[way, place - 1], recv_sems.at[way, place - 1])
        return remote(source.at[place], target.at[place], *sems, devices[place])

    def stage_copy(at, slot, start, size):
        return pltpu.make_async_copy(
            staged.at[slot, :, pl.ds(0, size)], parts_out.at[at, :, pl.ds(start, size)], stage_sems.at[slot]
        )

    def stage_free(at, start, size):
        @pl.when(at >= 2)
        def _():
            stage_copy(at - 2, lax.rem(at, 2), start, size).wait()

    def stage(at, start, size, hidden, gate_back, up_back):
        slot = lax.rem(at, 2)
        for number, values in enumerate((hidden, gate_back, up_back)):
            staged[slot, number, pl.ds(0, size)] = values
        return stage_copy(at, slot, start, size)

    def stage_end(start, size):
        for at in (tiles - 2, tiles - 1):
            stage_copy(at, at % 2, start, size).wait()

    def own_half(half):
        held = slice(half * part, (half + 1) * part)
        cut_rows = pl.ds(half * strip, strip)
        rows = rows_landed[held, :, :width].reshape(strip, width)
        picks = panel_sum(rows_landed[held, :, width:].reshape(strip, LANES))
        total[...] = jnp.zeros_like(total)
        picks_back[...] = jnp.zeros_like(picks_back)

        def middle(at, carry):
            stage_free(at, half * strip, strip)
            cut = pl.ds(pl.multiple_of(at * tile, tile), tile)
            value, slope = gelu_parts(product(rows, gate_mat[:, cut]))
            up_part = product(rows, up_mat[:, cut])
            hidden = value * up_part
            hidden_low = hidden.astype(jnp.bfloat16)
            hidden_all[cut_rows, cut] = hidden_low
            back = down_rows[cut_rows, cut].astype(jnp.float32)
            weighed = hidden * back
            picks_back[...] += sum(weighed[:, lane : lane + LANES] for lane in range(0, tile, LANES))
            back = back * picks
            gate_back = (back * up_part * slope).astype(jnp.bfloat16)
            up_back = (back * value).astype(jnp.bfloat16)
            store = stage(at, half * strip, strip, hidden_low, gate_back, up_back)
            total[...] += product_back(
                jnp.concatenate([gate_back, up_back], axis=1),
                jnp.concatenate([gate_mat[:, cut], up_mat[:, cut]], axis=1),
            )
            store.start()
            return carry

        lax.fori_loop(0, tiles, middle, 0)
        back_sent[held, :, :width] = total[...].astype(jnp.bfloat16).reshape(part, room, width)
        high, low = halves(jnp.sum(picks_back[...], axis=1, keepdims=True))
        lane = iota((strip, LANES), 1)
        panel = jnp.where(lane == 0, high, jnp.where(lane == 1, low, jnp.zeros_like(low)))
        back_sent[held, :, width:] = panel.reshape(part, room, LANES)
        start_all([row_copy(1, place) for place in range(half * part, (half + 1) * part)])
        stage_end(half * strip, strip)

    def others(start, sources):
        at, copies = 0, []
        for number, (row_source, cot_source) in enumerate(sources):
            size = row_source.shape[0]
            place = pl.ds(at, size)
            copies += [
                pltpu.make_async_copy(row_source, other_rows.at[place], other_sems.at[0, number]),
                pltpu.make_async_copy(cot_source, other_cots.at[place], other_sems.at[1, number]),
            ]
            at += size
        size = at
        start_all(copies)
        wait_all(copies)
        rows = other_rows[:size, :, :width].reshape(size * room, width)
        picks = panel_sum(other_rows[:size, :, width:].reshape(size * room, LANES))
        cots = (other_cots[:size].reshape(size * room, width).astype(jnp.float32) * picks).astype(jnp.bfloat16)
        size = size * room

        def middle(at, carry):
            stage_free(at, start, size)
            cut = pl.ds(pl.multiple_of(at * tile, tile), tile)
            value, slope = gelu_parts(product(rows, gate_mat[:, cut]))
            up_part = product(rows, up_mat[:, cut])
            back = product_back(cots, down_mat[cut, :])
            store = stage(
                at,
                start,
                size,
                (value * up_part).astype(jnp.bfloat16),
                (back * up_part * slope).astype(jnp.bfloat16),
                (back * value).astype(jnp.bfloat16),
            )
            store.start()
            return carry

        lax.fori_loop(0, tiles, middle, 0)
        stage_end(start, size)

    start_all([row_copy(0, place) for place in range(part)])
    start_all(cots_first(1))
    wait_all(loads[:2])
    cot_rows = cot[...].reshape(group * room, width)

    def early(at, carry):
        cut = pl.ds(pl.multiple_of(at * tile, tile), tile)
        down_rows[:, cut] = product_back(cot_rows, down_mat[cut, :]).astype(jnp.bfloat16)
        return carry

    lax.fori_loop(0, tiles, early, 0)
    wait_all(loads[2:])
    wait_all([row_copy(0, place) for place in range(quarter)])
    start_all(rows_first(0))
    wait_all([row_copy(0, place) for place in range(quarter, part)])
    start_all([row_copy(0, place) for place in range(part, group)])
    start_all(rows_first(1))
    own_half(0)
    wait_all(cots_first(1) + rows_first(0))
    start_all(cot_spreads[1].second() + row_spreads[0].second() + cots_first(2))
    others(2 * strip, [(rows_near0.at[k], cot_near0.at[k]) for k in range(2)])
    wait_all(rows_first(1))
    start_all(row_spreads[1].second() + cots_first(3))
    wait_all([row_copy(0, place) for place in range(part, group)])
    own_half(1)
    wait_all(cots_first(2) + cots_first(3))
    start_all(cot_spreads[2].second() + cot_spreads[3].second())
    wait_all(cot_spreads[1].second() + row_spreads[0].second() + row_spreads[1].second())
    others(
        3 * strip,
        [(rows_near1.at[k], cot_near1.at[k]) for k in range(2)] + [(rows_far0, cot_far0), (rows_far1, cot_far1)],
    )

    def outward(at, carry):
        cut = pl.ds(pl.multiple_of(at * tile, tile), tile)
        out = product(hidden_all[...], down_mat[:, cut]).astype(jnp.bfloat16)
        out_rows[:, :, cut] = out.reshape(group, room, tile)
        return carry

    lax.fori_loop(0, width // tile, outward, 0)
    wait_all([row_copy(1, place) for place in range(group)])
    wait_all(cot_spreads[2].second() + cot_spreads[3].second())


def experts_apply(sizes, number, tile, *operands):
    rows_sent, cot_own = operands[:2]
    group, room, width = cot_own.shape
    hidden_width = operands[4].shape[1]
    slots = group * room
    quarter = group // 4
    half, single = jnp.bfloat16, jnp.float32
    vmem, anywhere = pl.BlockSpec(memory_space=pltpu.VMEM), pl.BlockSpec(memory_space=pl.ANY)
    wide = rows_sent.shape[2]
    shapes = [rows_sent.shape, rows_sent.shape, cot_own.shape, (hidden_width // tile, 3, 5 * slots // 2, tile)]
    shapes += [(2, quarter, room, width), (quarter, room, width)] * 3
    shapes += [(2, quarter, room, wide), (quarter, room, wide)] * 2
    return pl.pallas_call(
        functools.partial(expert_kernel, tile, sizes),
        out_shape=[jax.ShapeDtypeStruct(shape, half) for shape in shapes],
        in_specs=[anywhere] * 7,
        out_specs=[anywhere] + [vmem] * 2 + [anywhere] * 11,
        scratch_shapes=[
            pltpu.VMEM((width, hidden_width), half),
            pltpu.VMEM((width, hidden_width), half),
            pltpu.VMEM((hidden_width, width), half),
            pltpu.VMEM((group, room, width), half),
            pltpu.VMEM((slots, hidden_width), half),
            pltpu.VMEM((slots, hidden_width), half),
            pltpu.VMEM((slots // 2, width), single),
            pltpu.VMEM((slots // 2, LANES), single),
            pltpu.VMEM(rows_sent.shape, half),
            pltpu.VMEM((4 * quarter, room, wide), half),
            pltpu.VMEM((4 * quarter, room, width), half),
            pltpu.VMEM((2, 3, slots, tile), half),
            pltpu.SemaphoreType.DMA((4,)),
            pltpu.SemaphoreType.DMA((2,)),
            pltpu.SemaphoreType.DMA((2, group - 1)),
            pltpu.SemaphoreType.DMA((2, group - 1)),
            pltpu.SemaphoreType.DMA((5, 4)),
            pltpu.SemaphoreType.DMA((5, 4)),
            pltpu.SemaphoreType.DMA((2,)),
            pltpu.SemaphoreType.DMA((2, 4)),
        ],
        compiler_params=pltpu.CompilerParams(
            collective_id=number, has_side_effects=True, vmem_limit_bytes=VMEM_LIMIT
        ),
    )(*operands)


def column_slots(routes, live, experts, room, capacity):
    tok = live.shape[0]
    names = iota((tok, experts), 1).astype(jnp.float32)
    hot = [(routes[:, k : k + 1] == names) & live for k in range(2)]
    both = jnp.where(hot[0] | hot[1], 1.0, 0.0).astype(jnp.bfloat16)
    before = jnp.where(iota((tok, tok), 1) < iota((tok, tok), 0), 1.0, 0.0).astype(jnp.bfloat16)
    earlier = product(before, both)
    slots = []
    for k in range(2):
        place = jnp.sum(jnp.where(hot[k], earlier, 0.0), axis=1, keepdims=True)
        slot = routes[:, k : k + 1] * room + place
        slots.append(jnp.where(live & (place < capacity), slot, -1.0))
    return slots


def halves(values):
    high = values.astype(jnp.bfloat16)
    return high, (values - high.astype(jnp.float32)).astype(jnp.bfloat16)


def back_kernel(
    dims,
    lengths,
    tokens,
    cotangent,
    near_row,
    routes_true,
    attn_gain,
    moe_gain,
    router,
    residual_in,
    gates_in,
    mixed,
    probs_in,
    queries_in,
    both,
    back_in,
    rows_own,
    query_weight,
    key_weight,
    value_weight,
    out_weight,
    token_grad,
    query_grad,
    key_grad,
    value_grad,
    small,
    rows_near2,
    rows_far2,
    rows_near3,
    rows_far3,
    out_total,
    back,
    held_weights,
    mixed_back,
    residual_grad,
    far_sent,
    far_landed,
    near_sum,
    diagonals,
    load_sems,
    row_send,
    row_recv,
    near_send,
    near_recv,
    out_wgrad,
    *shared,
):
    *held, sum_send, sum_recv = shared
    heads, experts, room, capacity, n_row, n_col, share, depth = dims
    tok, width = tokens.shape
    pair_width = 2 * width // heads
    member_width = pair_width // 2
    slots_count = experts * room
    loads = []
    for at, (source, target) in enumerate(
        ((back_in, back), (out_weight, held_weights.at[0]))
        + tuple((w, held_weights.at[1 + k]) for k, w in enumerate((query_weight, key_weight, value_weight)))
    ):
        load = pltpu.make_async_copy(source, target, load_sems.at[at])
        load.start()
        loads.append(load)
    devices = partners(n_row, n_col)
    spreads = [
        Spread(near, far, near_send.at[at], near_recv.at[at])
        for at, (near, far) in enumerate(((rows_near2, rows_far2), (rows_near3, rows_far3)))
    ]
    quarter = len(devices) // 4
    summed = ShareSum((n_row, n_col), depth, [out_wgrad], [out_total], [held], sum_send, sum_recv)
    greet(devices[1:] + spreads[0].devices)

    def rows_first(at):
        return spreads[at].first(rows_own.at[pl.ds((2 + at) * quarter, quarter)])

    start_all(rows_first(0))
    piece = lax.axis_index("erow")
    live = iota((tok, 1), 0) + piece * tok < lengths[0]
    slots = column_slots(columns_of(near_row[...], 2), live, experts, room, capacity)
    names = iota((tok, slots_count), 1).astype(jnp.float32)
    hot = [jnp.where(names == slot, 1.0, 0.0).astype(jnp.bfloat16) for slot in slots]
    lane = iota((tok, LANES), 1)
    columns = columns_of(routes_true[...], 2)
    chosen = [columns[:, k : k + 1] == lane.astype(jnp.float32) for k in range(2)]
    gates = gates_in[...]

    residual = residual_in[...]
    scale = lax.rsqrt(jnp.mean(residual * residual, axis=1, keepdims=True) + epsilon)
    moe_in = (residual * scale * moe_gain[...]).astype(jnp.bfloat16)
    loads[0].wait()
    panel = back[:, :, width:].reshape(slots_count, LANES)
    prob_back = jnp.zeros((tok, LANES), jnp.float32)
    for k in range(2):
        parts = product(hot[k], panel)
        prob_back = prob_back + jnp.where(chosen[k], parts[:, 0:1] + parts[:, 1:2], 0.0)
    logit_back = gates * (prob_back - jnp.sum(gates * prob_back, axis=1, keepdims=True))
    logit_high, logit_low = halves(logit_back)
    router_high, router_low = halves(router[...])
    few = slice(0, experts)
    moe_back = (
        product(hot[0] + hot[1], back[:, :, :width].reshape(slots_count, width))
        + product(logit_high[:, few], router_high)
        + product(logit_low[:, few], router_high)
        + product(logit_high[:, few], router_low)
    )
    left = moe_in.T
    router_grad = product(left, logit_high) + product(left, logit_low)
    moe_gain_grad = jnp.sum(residual * scale * moe_back, axis=0, keepdims=True)
    pulled = moe_gain[...] * moe_back
    total = (
        cotangent[...].astype(jnp.float32)
        + scale * pulled
        - residual * (scale * scale * scale * jnp.mean(residual * pulled, axis=1, keepdims=True))
    )
    residual_grad[...] = total
    branch = total.astype(jnp.bfloat16)
    loads[1].wait()
    mixed_back[...] = product_back(branch, held_weights[0]).astype(jnp.bfloat16)
    out_wgrad[...] = product(mixed[...].T, branch).astype(jnp.bfloat16).reshape(out_wgrad.shape)
    summed.turn(0)
    reversal = jnp.where(iota((tok, tok), 0) + iota((tok, tok), 1) == tok - 1, 1.0, 0.0).astype(jnp.bfloat16)
    low_half = iota((tok, pair_width), 1) < member_width

    def unattend(pair, carry):
        lanes = pl.ds(pl.multiple_of(pair * pair_width, pair_width), pair_width)
        value_lanes = pl.ds(pl.multiple_of(width + pair * pair_width, pair_width), pair_width)
        keys, values = both[:, lanes], both[:, value_lanes]
        grads = mixed_back[:, lanes]

        @pl.when(pair == 1)
        def _():
            summed.turn(1)

        @pl.when(pair == 3)
        def _():
            wait_all(rows_first(0))
            start_all(spreads[0].second() + rows_first(1))

        @pl.when(pair == 5)
        def _():
            summed.turn(2)

        @pl.when(pair == heads // 2 - 1)
        def _():
            summed.turn(3)

        queries_left, grads_left = queries_in[:, lanes].T, grads.T
        query_parts, key_parts, value_parts = [], [], []
        for member in range(2):
            head = 2 * pair + member
            mask = low_half if member == 0 else jnp.logical_not(low_half)
            low = probs_in[pl.ds(head, 1)][0]
            probs = low.astype(jnp.float32)
            part = product_back(jnp.where(mask, grads, jnp.zeros_like(grads)), values)
            weighed = probs * part
            score = (weighed - probs * jnp.sum(weighed, axis=1, keepdims=True)).astype(jnp.bfloat16)
            query_parts.append(product(score, keys))
            span = slice(member * member_width, (member + 1) * member_width)
            key_parts.append(product(queries_left[span], score))
            value_parts.append(product(grads_left[span], low))
            exact = product(reversal, score)
            empty = jnp.zeros((tok, tok), jnp.float32)
            padded = jnp.concatenate([exact[:, :tok], empty, exact[:, tok:], empty], axis=1)
            turned = pltpu.roll(padded, 3 * tok + 1, 1, stride=1, stride_axis=0)
            diagonals[pl.ds(head, 1)] = jnp.sum(turned, axis=0, keepdims=True)
        query_grad[:, lanes] = (jnp.where(low_half, query_parts[0], query_parts[1]) * 0.125).astype(jnp.bfloat16)
        key_part = jnp.concatenate(key_parts, axis=0).T
        value_part = jnp.concatenate(value_parts, axis=0).T
        near_sum[:, lanes] = key_part[:tok]
        near_sum[:, value_lanes] = value_part[:tok]
        far_sent[:, lanes] = key_part[tok:].astype(jnp.bfloat16)
        far_sent[:, value_lanes] = value_part[tok:].astype(jnp.bfloat16)
        return carry

    lax.fori_loop(0, heads // 2, unattend, 0)
    pair_copy = remote(far_sent, far_landed, row_send, row_recv, devices[1])
    pair_copy.start()

    segment = width // heads
    table = 4 * tok
    entry = iota((table, LANES), 0)
    other = entry >= table // 4
    other = other & (entry < 3 * table // 4)
    distance = jnp.where(
        other,
        entry - table // 2 + tok * (1 - 2 * piece),
        jnp.where(entry < table // 2, entry, entry - table),
    )
    bucket = bucket_of(distance)
    place = depth * lax.div(bucket, share) + lax.rem(bucket, share)
    target = lax.rem(iota((table, LANES), 1), segment)
    sorted_hot = jnp.where(place == target, 1.0, 0.0).astype(jnp.bfloat16)
    diagonal_high, diagonal_low = halves(diagonals[...])
    bias_rows = product(diagonal_high, sorted_hot) + product(diagonal_low, sorted_hot)
    bias_wide = jnp.concatenate([bias_rows] * (width // LANES), axis=1)
    mine = lax.div(iota((heads, width), 1), segment) == iota((heads, width), 0)
    bias_row = jnp.sum(jnp.where(mine, bias_wide, 0.0), axis=0, keepdims=True)

    loads[2].wait()
    normed_back = product_back(query_grad[...], held_weights[1])
    pair_copy.wait()
    key_total = (near_sum[:, :width] + far_landed[:, :width].astype(jnp.float32)).astype(jnp.bfloat16)
    value_total = (near_sum[:, width:] + far_landed[:, width:].astype(jnp.float32)).astype(jnp.bfloat16)
    wait_all(rows_first(1))
    start_all(spreads[1].second())
    key_grad[...] = key_total
    value_grad[...] = value_total
    loads[3].wait()
    loads[4].wait()
    normed_back = normed_back + product_back(key_total, held_weights[2]) + product_back(value_total, held_weights[3])
    inputs = tokens[...].astype(jnp.float32)
    scale = lax.rsqrt(jnp.mean(inputs * inputs, axis=1, keepdims=True) + epsilon)
    attn_gain_grad = jnp.sum(inputs * scale * normed_back, axis=0, keepdims=True)
    pulled = attn_gain[...] * normed_back
    token_grad[...] = (
        residual_grad[...]
        + scale * pulled
        - inputs * (scale * scale * scale * jnp.mean(inputs * pulled, axis=1, keepdims=True))
    )
    empty = jnp.zeros((LANES - 3, width), jnp.float32)
    small[...] = jnp.concatenate([empty, attn_gain_grad, moe_gain_grad, bias_row], axis=0).T + router_grad
    wait_all(spreads[0].second() + spreads[1].second())
    summed.turn(4)


def backward(dims, number, *operands):
    heads, experts, room, capacity, n_row, n_col, share, depth = dims
    tokens, back_in, rows_own = operands[1], operands[14], operands[15]
    tok, width = tokens.shape
    group = n_row * n_col
    half, single = jnp.bfloat16, jnp.float32
    vmem, anywhere = pl.BlockSpec(memory_space=pltpu.VMEM), pl.BlockSpec(memory_space=pl.ANY)
    shapes = [((tok, width), single)] + [((tok, width), half)] * 3 + [((width, LANES), single)]
    shapes += [((2, group // 4) + rows_own.shape[1:], half), ((group // 4,) + rows_own.shape[1:], half)] * 2
    shapes += [((depth, width), single)]
    sems = (1, 4 + n_col)
    return pl.pallas_call(
        functools.partial(back_kernel, dims),
        out_shape=[jax.ShapeDtypeStruct(shape, kind) for shape, kind in shapes],
        in_specs=[pl.BlockSpec(memory_space=pltpu.SMEM)] + [vmem] * 13 + [anywhere] * 6,
        out_specs=[vmem] * 5 + [anywhere] * 4 + [vmem],
        scratch_shapes=[
            pltpu.VMEM(back_in.shape, half),
            pltpu.VMEM((4, width, width), half),
            pltpu.VMEM((tok, width), half),
            pltpu.VMEM((tok, width), single),
            pltpu.VMEM((tok, 2 * width), half),
            pltpu.VMEM((tok, 2 * width), half),
            pltpu.VMEM((tok, 2 * width), single),
            pltpu.VMEM((heads, 4 * tok), single),
            pltpu.SemaphoreType.DMA((5,)),
            pltpu.SemaphoreType.DMA,
            pltpu.SemaphoreType.DMA,
            pltpu.SemaphoreType.DMA((2, 4)),
            pltpu.SemaphoreType.DMA((2, 4)),
            pltpu.VMEM((2, 2, n_row, n_col * depth, width), half),
        ]
        + share_scratch((n_row, n_col), depth, width, half)
        + [pltpu.SemaphoreType.DMA(sems), pltpu.SemaphoreType.DMA(sems)],
        compiler_params=pltpu.CompilerParams(
            collective_id=number, has_side_effects=True, vmem_limit_bytes=VMEM_LIMIT
        ),
    )(*operands)


def last_kernel(tile, sizes, depth, slot_sizes, *refs):
    pieces = 9
    (lengths, near_row, routes_true, residual, gates_in), refs = refs[:5], refs[5:]
    (normed, query_grad, key_grad, value_grad, small), refs = refs[:5], refs[5:]
    rows_in, refs = refs[:pieces], refs[pieces:]
    cots_in, refs = refs[:pieces], refs[pieces:]
    parts_in, out_sent, weights, sums, refs = refs[0], refs[1], refs[2:5], refs[5:9], refs[9:]
    (gate_out, up_out, down_out, output), refs = refs[:4], refs[4:]
    (out_landed, out_own, out_send, out_recv), refs = refs[:4], refs[4:]
    (rows, cots, rows_left, mats, tiles_of, own_mats, out_tiles, down_tiles), refs = refs[:8], refs[8:]
    grads, refs = refs[:3], refs[3:]
    held, refs = [refs[5 * at : 5 * at + 5] for at in range(4)], refs[20:]
    load_sems, weight_sems, own_sems, out_sems, down_sem, send_sems, recv_sems = refs
    width, strip = normed.shape[1], grads[0].shape[3]
    hidden_width = weights[0].shape[1]
    tiles = hidden_width // tile
    ready = parts_in.shape[2]
    total_rows = rows.shape[0]
    chunk = (total_rows - ready) // 2
    share = width // 4
    hidden_share = hidden_width // 4
    replica = lax.axis_index("dp")
    summed = ShareSum(sizes, depth, list(grads) + [small], sums, held, send_sems, recv_sems)
    barrier = pltpu.get_barrier_semaphore()
    devices = partners(*sizes)
    for device in devices[1:] + summed.devices[1:3]:
        pl.semaphore_signal(barrier, 1, device_id=device, device_id_type=MESH)
    loads, start = [], 0
    for at, (row_piece, cot_piece) in enumerate(zip(rows_in, cots_in)):
        size = row_piece.shape[0]
        for number, (piece, target) in enumerate(((row_piece, rows), (cot_piece, cots))):
            load = pltpu.make_async_copy(piece, target.at[pl.ds(start, size)], load_sems.at[number, at])
            load.start()
            loads.append(load)
        start += size

    def weight_loads(at, slot):
        cut = pl.ds(pl.multiple_of(at * tile, tile), tile)
        return [
            pltpu.make_async_copy(source, mats.at[number, slot], weight_sems.at[number, slot])
            for number, source in enumerate((weights[0].at[:, cut], weights[1].at[:, cut]))
        ] + [pltpu.make_async_copy(weights[2].at[cut], own_mats.at[slot], weight_sems.at[2, slot])]

    def own_loads(at, slot):
        return [
            pltpu.make_async_copy(parts_in.at[at], tiles_of.at[slot, :, pl.ds(0, ready)], own_sems.at[slot])
        ]

    def out_copies(at, slot):
        cut = pl.ds(pl.multiple_of(at * tile, tile), tile)
        return [
            pltpu.make_async_copy(out_tiles.at[number, slot], target.at[:, cut], out_sems.at[number, slot])
            for number, target in enumerate((gate_out, up_out))
        ]

    first = lax.div(replica * hidden_share, tile)
    spans = lax.div((replica + 1) * hidden_share - 1, tile) - first + 1

    def tile_at(turn):
        return lax.rem(first + turn, tiles)

    start_all(weight_loads(tile_at(0), 0) + own_loads(tile_at(0), 0))
    left = normed[...].T
    shape = grads[0].shape
    grads[0][...] = product(left, query_grad[...]).astype(jnp.bfloat16).reshape(shape)
    pl.semaphore_wait(barrier, len(devices) + 1)
    returns = [pltpu.make_async_copy(out_sent.at[0], out_landed.at[0], out_own)]
    for place in range(1, len(devices)):
        sems = (out_send.at[place - 1], out_recv.at[place - 1])
        returns.append(remote(out_sent.at[place], out_landed.at[place], *sems, devices[place]))
    start_all(returns)
    summed.turn(0)
    grads[1][...] = product(left, key_grad[...]).astype(jnp.bfloat16).reshape(shape)
    grads[2][...] = product(left, value_grad[...]).astype(jnp.bfloat16).reshape(shape)
    summed.turn(1)
    for load in loads:
        load.wait()

    def weigh(at, carry):
        cut = pl.ds(pl.multiple_of(at * 256, 256), 256)
        panel = rows[cut, width:]
        picks = panel[:, 0:1].astype(jnp.float32) + panel[:, 1:2].astype(jnp.float32)
        cots[cut] = (cots[cut].astype(jnp.float32) * picks).astype(jnp.bfloat16)
        lanes = pl.ds(pl.multiple_of(replica * share, share), share)
        rows_left[:, cut] = rows[cut, lanes].T
        return carry

    lax.fori_loop(0, total_rows // 256, weigh, 0)
    turn_tiles = (0, 2, 4, 6, 8, 10)
    blocks = 1 if chunk <= 512 else 2

    def each_tile(turn, carry):
        slot = lax.rem(turn, 2)
        at = tile_at(turn)
        wait_all(weight_loads(at, slot) + own_loads(at, slot))

        @pl.when(turn + 1 < tiles)
        def _():
            start_all(weight_loads(tile_at(turn + 1), 1 - slot) + own_loads(tile_at(turn + 1), 1 - slot))

        for number in range(2, summed.turns):
            @pl.when(turn == turn_tiles[number - 2])
            def _(number=number):
                summed.turn(number)

        @pl.when(turn >= 2)
        def _():
            wait_all(out_copies(tile_at(turn - 2), slot))

        size = 2 * chunk // blocks
        for block in range(blocks):
            cut = pl.ds(ready + block * size, size)
            value, slope = gelu_parts(product(rows[cut, :width], mats[0, slot]))
            up_part = product(rows[cut, :width], mats[1, slot])
            back = product_back(cots[cut], own_mats[slot])
            tiles_of[slot, 0, cut] = (value * up_part).astype(jnp.bfloat16)
            tiles_of[slot, 1, cut] = (back * up_part * slope).astype(jnp.bfloat16)
            tiles_of[slot, 2, cut] = (back * value).astype(jnp.bfloat16)
        for number in range(2):
            out_tiles[number, slot] = product(rows_left[...], tiles_of[slot, number + 1])
        start_all(out_copies(at, slot))

        @pl.when(turn < spans)
        def _():
            place = pl.ds(pl.multiple_of(turn * tile, tile), tile)
            down_tiles[place] = product_left(tiles_of[slot, 0], cots[...])

        return carry

    lax.fori_loop(0, tiles, each_tile, 0)
    offset = pl.multiple_of(replica * hidden_share - first * tile, 8)
    down_copy = pltpu.make_async_copy(down_tiles.at[pl.ds(offset, hidden_share)], down_out, down_sem)
    down_copy.start()
    experts, room, capacity = slot_sizes
    tok = normed.shape[0]
    live = iota((tok, 1), 0) + lax.axis_index("erow") * tok < lengths[0]
    slots = column_slots(columns_of(near_row[...], 2), live, experts, room, capacity)
    names = iota((tok, experts * room), 1).astype(jnp.float32)
    columns = columns_of(routes_true[...], 2)
    lane = iota((tok, LANES), 1).astype(jnp.float32)
    total = residual[...]
    wait_all(returns)
    results = out_landed[...].reshape(experts * room, width)
    for k in range(2):
        hot = jnp.where(names == slots[k], 1.0, 0.0).astype(jnp.bfloat16)
        pick = jnp.sum(jnp.where(columns[:, k : k + 1] == lane, gates_in[...], 0.0), axis=1, keepdims=True)
        total = total + pick * product(hot, results)
    output[...] = total.astype(jnp.bfloat16)
    for turn in (tiles - 2, tiles - 1):
        wait_all(out_copies(tile_at(turn), turn % 2))
    down_copy.wait()


def last(sizes, number, slot_sizes, placing, shared, small, rows_in, cots_in, parts_in, out_sent, weights):
    n_dp, n_row, n_col = sizes
    normed = shared[0]
    tok, width = normed.shape
    hidden_width = weights[0].shape[1]
    total_rows = sum(piece.shape[0] for piece in rows_in)
    tile = parts_in.shape[3]
    depth = width // (n_dp * n_row * n_col)
    strip = n_col * depth
    half, single = jnp.bfloat16, jnp.float32
    vmem, anywhere = pl.BlockSpec(memory_space=pltpu.VMEM), pl.BlockSpec(memory_space=pl.ANY)
    small = small.reshape(2, 2, n_row, strip, small.shape[1])
    hidden_share = hidden_width // n_dp
    spans = -(-hidden_share // tile) + 1
    scratch = [
        pltpu.VMEM(out_sent.shape, half),
        pltpu.SemaphoreType.DMA,
        pltpu.SemaphoreType.DMA((n_row * n_col - 1,)),
        pltpu.SemaphoreType.DMA((n_row * n_col - 1,)),
        pltpu.VMEM((total_rows, width + LANES), half),
        pltpu.VMEM((total_rows, width), half),
        pltpu.VMEM((width // n_dp, total_rows), half),
        pltpu.VMEM((2, 2, width, tile), half),
        pltpu.VMEM((2, 3, total_rows, tile), half),
        pltpu.VMEM((2, tile, width), half),
        pltpu.VMEM((2, 2, width // n_dp, tile), single),
        pltpu.VMEM((spans * tile, width), single),
    ]
    scratch += [pltpu.VMEM((2, 2, n_row, strip, width), half)] * 3
    for _ in range(3):
        scratch += share_scratch((n_row, n_col), depth, width, half)
    scratch += share_scratch((n_row, n_col), depth, LANES, single)
    sems = (4, 4 + n_col)
    scratch += [
        pltpu.SemaphoreType.DMA((2, len(rows_in))),
        pltpu.SemaphoreType.DMA((3, 2)),
        pltpu.SemaphoreType.DMA((2,)),
        pltpu.SemaphoreType.DMA((2, 2)),
        pltpu.SemaphoreType.DMA,
        pltpu.SemaphoreType.DMA(sems),
        pltpu.SemaphoreType.DMA(sems),
    ]
    out_shape = [jax.ShapeDtypeStruct((depth, width), single)] * 3
    out_shape += [jax.ShapeDtypeStruct((depth, LANES), single)]
    out_shape += [jax.ShapeDtypeStruct((width // n_dp, hidden_width), single)] * 2
    out_shape += [jax.ShapeDtypeStruct((hidden_share, width), single), jax.ShapeDtypeStruct((tok, width), half)]
    return pl.pallas_call(
        functools.partial(last_kernel, tile, (n_row, n_col), depth, slot_sizes),
        out_shape=out_shape,
        in_specs=[pl.BlockSpec(memory_space=pltpu.SMEM)] + [vmem] * 9 + [anywhere] * (2 * len(rows_in) + 5),
        out_specs=[vmem] * 4 + [anywhere] * 3 + [vmem],
        scratch_shapes=scratch,
        compiler_params=pltpu.CompilerParams(
            collective_id=number, has_side_effects=True, vmem_limit_bytes=VMEM_LIMIT
        ),
    )(*placing, *shared, small, *rows_in, *cots_in, parts_in, out_sent, *weights)


def finish_kernel(experts, bias_share, small, *refs):
    count = (len(refs) - 5) // 3
    sources, targets, rest = refs[:count], refs[count : 2 * count], refs[2 * count :]
    (attn_out, moe_out, bias_out, router_out), held, sems = rest[:4], rest[4:-1], rest[-1]
    loads = [
        pltpu.make_async_copy(source, place, sems.at[0, at]) for at, (source, place) in enumerate(zip(sources, held))
    ]
    stores = [
        pltpu.make_async_copy(place, target, sems.at[1, at]) for at, (place, target) in enumerate(zip(held, targets))
    ]
    start_all(loads)
    turned = small[...].T
    attn_out[...] = turned[LANES - 3 : LANES - 2]
    moe_out[...] = turned[LANES - 2 : LANES - 1]
    bias_out[...] = turned[LANES - 1 :, :bias_share]
    router_out[...] = turned[:experts]
    for load, store in zip(loads, stores):
        load.wait()
        store.start()
    wait_all(stores)


def finish(experts, bias_share, small, *arrays):
    depth = small.shape[0]
    vmem, anywhere = pl.BlockSpec(memory_space=pltpu.VMEM), pl.BlockSpec(memory_space=pl.ANY)
    shapes = [(array.shape, array.dtype) for array in arrays]
    shapes += [((1, depth), small.dtype)] * 2 + [((1, bias_share), small.dtype), ((experts, depth), small.dtype)]
    return pl.pallas_call(
        functools.partial(finish_kernel, experts, bias_share),
        out_shape=[jax.ShapeDtypeStruct(*shape) for shape in shapes],
        in_specs=[vmem] + [anywhere] * len(arrays),
        out_specs=[anywhere] * len(arrays) + [vmem] * 4,
        scratch_shapes=[pltpu.VMEM(array.shape, array.dtype) for array in arrays]
        + [pltpu.SemaphoreType.DMA((2, len(arrays)))],
        compiler_params=pltpu.CompilerParams(vmem_limit_bytes=VMEM_LIMIT),
    )(small, *arrays)


def gelu_parts(gate_part):
    square = gate_part * gate_part
    inner = gate_part * (0.7978845608028654 + 0.035677408136300125 * square)
    half = 0.5 + 0.5 * jnp.tanh(inner)
    value = gate_part * half
    slope = half + value * (1.0 - half) * (1.5957691216057308 + 0.21406444881780075 * square)
    return value, slope


def paired(own, *pieces):
    blocks = [own]
    for at in range(0, len(pieces), 2):
        blocks += [pieces[at][0], pieces[at + 1][0], pieces[at][1], pieces[at + 1][1]]
    return [block.reshape(-1, block.shape[-1]) for block in blocks]


def body(
    tokens,
    lengths,
    routes,
    attn_gain,
    query_weight,
    key_weight,
    value_weight,
    out_weight,
    relative_bias,
    moe_gain,
    router_weight,
    gate_weight,
    up_weight,
    down_weight,
    cotangent,
):
    tok_rows, width = tokens.shape[1:]
    head_count, bucket_count = relative_bias.shape
    expert_count = router_weight.shape[1]
    capacity = 5 * tok_rows // (2 * expert_count)
    room = -(-capacity // 16) * 16
    n_dp, n_row, n_col = (lax.axis_size(name) for name in ("dp", "erow", "ecol"))
    device_count = n_dp * n_row * n_col
    slot_count = expert_count * room
    gate_mat, up_mat, down_mat = gate_weight[0], up_weight[0], down_weight[0]
    routes_row = routes[0].T
    near_routes = mirrored((routes_row % n_col) ^ lax.axis_index("ecol"), n_col) * n_row + (
        (routes_row // n_col) ^ lax.axis_index("erow")
    )
    router = router_weight.T
    dims = (head_count, expert_count, room, capacity, n_row, n_col)
    normed, queries, both, probs, mixed, residual, gates, slot_rows, got_grads, *cots0 = front(
        dims,
        0,
        lengths,
        tokens[0],
        cotangent[0],
        near_routes,
        routes_row,
        attn_gain[None],
        moe_gain[None],
        relative_bias,
        router,
        query_weight,
        key_weight,
        value_weight,
        out_weight,
    )
    back, got, expert_out, parts, *moved = experts_apply(
        (n_row, n_col), 1, 256 if slot_count <= 768 else LANES, slot_rows, got_grads, *cots0, gate_mat, up_mat, down_mat
    )
    cots1, cots2, cots3, rows0, rows1 = (moved[at : at + 2] for at in range(0, 10, 2))
    depth = width // device_count
    bias_share = head_count * bucket_count // device_count
    token_grad, query_grad, key_grad, value_grad, small, *moved, out_sum = backward(
        dims + (bias_share, depth),
        2,
        lengths,
        tokens[0],
        cotangent[0],
        near_routes,
        routes_row,
        attn_gain[None],
        moe_gain[None],
        router,
        residual,
        gates,
        mixed,
        probs,
        queries,
        both,
        back,
        got,
        query_weight,
        key_weight,
        value_weight,
        out_weight,
    )
    rows2, rows3 = moved[:2], moved[2:]
    query_sum, key_sum, value_sum, small_sum, gate_total, up_total, down_total, output = last(
        (n_dp, n_row, n_col),
        3,
        (expert_count, room, capacity),
        (lengths, near_routes, routes_row, residual, gates),
        (normed, query_grad, key_grad, value_grad),
        small,
        paired(got, rows0, rows1, rows2, rows3),
        paired(got_grads, cots0, cots1, cots2, cots3),
        parts,
        expert_out,
        (gate_mat, up_mat, down_mat),
    )
    handed = finish(
        expert_count,
        bias_share,
        small_sum,
        output,
        token_grad,
        query_sum,
        key_sum,
        value_sum,
        out_sum,
        gate_total,
        up_total,
        down_total,
    )
    output, token_grad, query_sum, key_sum, value_sum, out_sum, gate_total, up_total, down_total = handed[:9]
    attn_sum, moe_sum, bias_sum, router_sum = handed[9:]
    return (
        output[None],
        token_grad[None],
        attn_sum[0],
        query_sum,
        key_sum,
        value_sum,
        out_sum,
        bias_sum[0],
        moe_sum[0],
        router_sum.T,
        gate_total[None],
        up_total[None],
        down_total[None],
    )


def solution(mesh):
    rows = P(("dp", "ecol"), "erow", None)
    experts = P(("erow", "ecol"), None, None)
    every = ("dp", "erow", "ecol")
    shares = P(("erow", "ecol"), "dp", None)
    return jax.shard_map(
        body,
        mesh=mesh,
        in_specs=(
            (rows, P(("dp", "ecol")), rows) + (P(),) * 8 + (experts, experts, experts, rows)
        ),
        out_specs=(rows, rows, P(every))
        + (P(every, None),) * 4
        + (P(every), P(every), P(every, None), shares, shares, shares),
        check_vma=False,
    )
```

```python
import functools

import jax
import jax.numpy as jnp
from jax import lax
from jax.experimental import pallas as pl
from jax.experimental.pallas import tpu as pltpu
from jax.sharding import PartitionSpec as P

epsilon = 1e-06
highest = lax.Precision.HIGHEST
thresholds = (12, 16, 23, 32, 46, 64, 91)
MESH = pl.DeviceIdType.MESH
LANES = 128
VMEM_LIMIT = 60 * 1024 * 1024


def bucket_of(offset):
    distance = jnp.abs(offset)
    larger = 8 + sum(((distance >= bound_at).astype(jnp.int32) for bound_at in thresholds))
    return jnp.where(offset > 0, 16, 0) + jnp.where(distance < 8, distance, larger)


def product(left_side, right_side):
    return jnp.dot(left_side, right_side, preferred_element_type=jnp.float32)


def product_back(left_side, right_side):
    return lax.dot_general(
        left_side, right_side, (((1,), (1,)), ((), ())), preferred_element_type=jnp.float32
    )


def product_left(left_side, right_side):
    return lax.dot_general(
        left_side, right_side, (((0,), (0,)), ((), ())), preferred_element_type=jnp.float32
    )


def greet(devices):
    barrier = pltpu.get_barrier_semaphore()
    for device in devices:
        pl.semaphore_signal(barrier, 1, device_id=device, device_id_type=MESH)
    pl.semaphore_wait(barrier, len(devices))


def remote(source, target, send_sem, recv_sem, device):
    return pltpu.make_async_remote_copy(
        src_ref=source,
        dst_ref=target,
        send_sem=send_sem,
        recv_sem=recv_sem,
        device_id=device,
        device_id_type=MESH,
    )


def flipped(index, mask, size):
    bit = 1
    while bit < size:
        if mask & bit:
            index = index + bit * (1 - 2 * lax.rem(lax.div(index, bit), 2))
        bit *= 2
    return index


def mirrored(value, size):
    result, bit = value * 0, 1
    while bit < size:
        result = result * 2 + (value // bit) % 2
        bit *= 2
    return result


def partners(n_row, n_col):
    row, col = lax.axis_index("erow"), lax.axis_index("ecol")
    return [
        {
            "erow": flipped(row, place % n_row, n_row),
            "ecol": flipped(col, mirrored(place // n_row, n_col), n_col),
        }
        for place in range(n_row * n_col)
    ]


class Spread:
    def __init__(self, near, far, send_sems, recv_sems):
        dp = lax.axis_index("dp")
        slow, fast = lax.div(dp, 2), lax.rem(dp, 2)
        self.devices = [{"dp": slow * 2 + 1 - fast}, {"dp": (1 - slow) * 2 + fast}]
        self.near, self.far, self.send_sems, self.recv_sems = near, far, send_sems, recv_sems

    def first(self, source):
        return [
            remote(source, self.near.at[k], self.send_sems.at[k], self.recv_sems.at[k], self.devices[k])
            for k in range(2)
        ]

    def second(self, near=None):
        near = self.near if near is None else near
        half = self.far.shape[0] // 2
        return [
            remote(
                near.at[k, pl.ds(k * half, half)],
                self.far.at[pl.ds(k * half, half)],
                self.send_sems.at[2 + k],
                self.recv_sems.at[2 + k],
                self.devices[1 - k],
            )
            for k in range(2)
        ]


def start_all(copies):
    for copy in copies:
        copy.start()


def wait_all(copies):
    for copy in copies:
        copy.wait()


class ShareSum:
    stages = 5

    def __init__(self, sizes, depth, grads, totals, held, send_sems, recv_sems):
        self.n_row, self.n_col = sizes
        self.depth, self.grads, self.totals, self.held = depth, grads, totals, held
        self.send_sems, self.recv_sems = send_sems, recv_sems
        dp, self.row, self.col = (lax.axis_index(name) for name in ("dp", "erow", "ecol"))
        self.slow, self.fast = lax.div(dp, 2), lax.rem(dp, 2)
        self.over_row = {"erow": 1 - self.row}
        self.over_fast = {"dp": self.slow * 2 + 1 - self.fast}
        self.over_slow = {"dp": (1 - self.slow) * 2 + self.fast}
        self.over_col = [{"ecol": flipped(self.col, mask, self.n_col)} for mask in range(1, self.n_col)]
        self.devices = [self.over_row, self.over_fast, self.over_slow] + self.over_col

    def parts(self, at):
        width = self.grads[at].shape[-1]
        if width >= 2 * LANES:
            return ((0, pl.ds(0, width // 2)), (1, pl.ds(width // 2, width // 2)))
        return ((0, pl.ds(0, width)),)

    def copy(self, at, number):
        from_row, from_near, from_far, late_sum, from_col = self.held[at]
        sems = (self.send_sems.at[at, number], self.recv_sems.at[at, number])
        if number == 0:
            return remote(self.grads[at].at[:, :, 1 - self.row], from_row, *sems, self.over_row)
        if number <= 4:
            which, cut = self.parts(at)[(number - 1) % 2]
            if number == 1:
                return remote(from_row.at[:, 1 - self.fast, :, cut], from_near.at[:, :, cut], *sems, self.over_fast)
            if number == 2:
                return remote(from_row.at[1 - self.slow, :, :, cut], from_near.at[:, :, cut], *sems, self.over_slow)
            if number == 3:
                return remote(from_near.at[1 - self.slow, :, cut], from_far.at[:, cut], *sems, self.over_slow)
            return remote(from_near.at[1 - self.fast, :, cut], from_far.at[:, cut], *sems, self.over_fast)
        mask = number - 4
        peer = flipped(self.col, mask, self.n_col)
        return remote(late_sum.at[peer], from_col.at[mask - 1], *sems, self.over_col[mask - 1])

    def step(self, at, stage):
        from_row, from_near, from_far, late_sum, from_col = self.held[at]
        if stage == 0:
            self.copy(at, 0).start()
        elif stage == 1:
            self.copy(at, 0).wait()
            for high in range(2):
                for low in range(2):
                    from_row[high, low] = (
                        self.grads[at][high, low, self.row].astype(jnp.float32)
                        + from_row[high, low].astype(jnp.float32)
                    ).astype(from_row.dtype)
            for which, _ in self.parts(at):
                self.copy(at, 1 + which).start()
        elif stage == 2:
            for which, cut in self.parts(at):
                self.copy(at, 1 + which).wait()
                for place in range(2):
                    kept = from_row[place, self.fast, :, cut] if which == 0 else from_row[self.slow, place, :, cut]
                    from_near[place, :, cut] = (
                        kept.astype(jnp.float32) + from_near[place, :, cut].astype(jnp.float32)
                    ).astype(from_near.dtype)
                self.copy(at, 3 + which).start()
        elif stage == 3:
            for which, cut in self.parts(at):
                self.copy(at, 3 + which).wait()
                kept = from_near[self.slow if which == 0 else self.fast, :, cut]
                total = kept.astype(jnp.float32) + from_far[:, cut].astype(jnp.float32)
                late_sum[:, :, cut] = total.reshape(self.n_col, self.depth, -1).astype(late_sum.dtype)
            for mask in range(1, self.n_col):
                self.copy(at, 4 + mask).start()
        else:
            total = late_sum[self.col].astype(jnp.float32)
            for mask in range(1, self.n_col):
                self.copy(at, 4 + mask).wait()
                total = total + from_col[mask - 1].astype(jnp.float32)
            self.totals[at][...] = total

    def turn(self, number):
        for at in range(len(self.grads)):
            if 0 <= number - at < self.stages:
                self.step(at, number - at)

    @property
    def turns(self):
        return len(self.grads) + self.stages - 1


def share_scratch(sizes, depth, width, kind):
    n_row, n_col = sizes
    strip = n_col * depth
    late = kind if depth % 16 == 0 else jnp.float32
    return [
        pltpu.VMEM((2, 2, strip, width), kind),
        pltpu.VMEM((2, strip, width), kind),
        pltpu.VMEM((strip, width), kind),
        pltpu.VMEM((n_col, depth, width), late),
        pltpu.VMEM((n_col - 1, depth, width), late),
    ]


def iota(shape, dimension):
    return lax.broadcasted_iota(jnp.int32, shape, dimension)


def columns_of(rows, count):
    padded = jnp.concatenate([rows.astype(jnp.float32), jnp.zeros((8 - count, rows.shape[1]), jnp.float32)], axis=0)
    return padded.T


def row_slots(routes, live, experts, room, capacity):
    tok = live.shape[1]
    names = iota((experts, tok), 0)
    hot = [(routes[k : k + 1] == names) & live for k in range(2)]
    both = jnp.where(hot[0] | hot[1], 1.0, 0.0).astype(jnp.bfloat16)
    before = jnp.where(iota((tok, tok), 0) < iota((tok, tok), 1), 1.0, 0.0).astype(jnp.bfloat16)
    earlier = product(both, before)
    slots = []
    for k in range(2):
        place = jnp.sum(jnp.where(hot[k], earlier, 0.0), axis=0, keepdims=True)
        slot = routes[k : k + 1].astype(jnp.float32) * room + place
        slots.append(jnp.where(live & (place < capacity), slot, -1.0))
    return slots


def bias_tables(relative_bias, table_width, offset):
    buckets = relative_bias.shape[1]
    place = iota((buckets, table_width), 1)
    distance = jnp.where(place < table_width // 2, place, place - table_width) + offset
    hot = jnp.where(bucket_of(distance) == iota((buckets, table_width), 0), 1.0, 0.0)
    return jnp.dot(relative_bias, hot, precision=highest, preferred_element_type=jnp.float32)


def skewed(row, rows):
    width = row.shape[1]
    full = pltpu.roll(jnp.broadcast_to(row, (rows, width)), 0, 1, stride=1, stride_axis=0)
    return full[:, : width // 2]


def front_kernel(
    dims,
    lengths,
    tokens,
    cotangent,
    routes_row,
    routes_true,
    attn_gain,
    moe_gain,
    relative_bias,
    router,
    query_weight,
    key_weight,
    value_weight,
    out_weight,
    normed_out,
    query_out,
    both_out,
    probs_out,
    mixed_out,
    residual_out,
    gates_out,
    rows_out,
    cot_landed,
    cot_near0,
    cot_far0,
    cot_near1,
    select,
    cot_slots,
    tables,
    held_weights,
    weight_sems,
    own_sem,
    send_sems,
    recv_sems,
    row_send,
    row_recv,
    near_send,
    near_recv,
):
    heads, experts, room, capacity, n_row, n_col = dims
    tok, width = tokens.shape
    pair_width = 2 * width // heads
    loads = []
    for at, source in enumerate((key_weight, value_weight, query_weight, out_weight)):
        load = pltpu.make_async_copy(source, held_weights.at[at], weight_sems.at[at])
        load.start()
        loads.append(load)
    devices = partners(n_row, n_col)
    spreads = [
        Spread(near, far, near_send.at[at], near_recv.at[at])
        for at, (near, far) in enumerate(((cot_near0, cot_far0), (cot_near1, None)))
    ]
    part = len(devices) // 4
    barrier = pltpu.get_barrier_semaphore()
    for device in devices[1:] + spreads[0].devices:
        pl.semaphore_signal(barrier, 1, device_id=device, device_id_type=MESH)

    piece = lax.axis_index("erow")
    length = lengths[0]
    live = iota((1, tok), 1) + piece * tok < length
    slots = row_slots(routes_row[...], live, experts, room, capacity)
    names = iota((experts * room, tok), 0).astype(jnp.float32)
    hot = [jnp.where(names == slot, 1.0, 0.0).astype(jnp.bfloat16) for slot in slots]
    select[...] = hot[0] + hot[1]
    cot_slots[...] = product(select[...], cotangent[...]).astype(jnp.bfloat16).reshape(cot_slots.shape)
    pl.semaphore_wait(barrier, len(devices) + 1)
    own = pltpu.make_async_copy(cot_slots.at[0], cot_landed.at[0], own_sem)
    copies = [own] + [
        remote(
            cot_slots.at[place],
            cot_landed.at[place],
            send_sems.at[place - 1],
            recv_sems.at[place - 1],
            devices[place],
        )
        for place in range(1, len(devices))
    ]
    start_all(copies)

    def cots_first(piece):
        return spreads[piece].first(cot_landed.at[pl.ds(piece * part, part)])

    inputs = tokens[...].astype(jnp.float32)
    scale = lax.rsqrt(jnp.mean(inputs * inputs, axis=1, keepdims=True) + epsilon)
    normed = (inputs * scale * attn_gain[...]).astype(jnp.bfloat16)
    normed_out[...] = normed
    loads[0].wait()
    both_out[:tok, :width] = product(normed, held_weights[0]).astype(jnp.bfloat16)
    loads[1].wait()
    both_out[:tok, width:] = product(normed, held_weights[1]).astype(jnp.bfloat16)
    pair_copy = remote(both_out.at[pl.ds(0, tok)], both_out.at[pl.ds(tok, tok)], row_send, row_recv, devices[1])
    pair_copy.start()
    loads[2].wait()
    query_out[...] = (product(normed, held_weights[2]) * 0.125).astype(jnp.bfloat16)
    offset = tok * (1 - 2 * piece)
    tables[:, : 2 * tok] = bias_tables(relative_bias[...], 2 * tok, 0)
    tables[:, 2 * tok :] = bias_tables(relative_bias[...], 2 * tok, offset)
    place = iota((1, 2 * tok), 1)
    position = jnp.where(place < tok, place + piece * tok, place - tok + (1 - piece) * tok)
    dead = jnp.where(position < length, 0.0, -1000000000.0)
    low_half = iota((tok, pair_width), 1) < pair_width // 2
    pair_copy.wait()

    def attend(pair, carry):
        lanes = pl.ds(pl.multiple_of(pair * pair_width, pair_width), pair_width)
        value_lanes = pl.ds(pl.multiple_of(width + pair * pair_width, pair_width), pair_width)
        queries, keys, values = query_out[:, lanes], both_out[:, lanes], both_out[:, value_lanes]

        @pl.when(pair == 0)
        def _():
            wait_all(copies[:part])
            start_all(cots_first(0))

        @pl.when(pair == heads // 4)
        def _():
            wait_all(cots_first(0))
            start_all(spreads[0].second())

        results = []
        for member in range(2):
            mask = low_half if member == 0 else jnp.logical_not(low_half)
            head = 2 * pair + member
            scores = product_back(jnp.where(mask, queries, jnp.zeros_like(queries)), keys)
            table = tables[pl.ds(head, 1)]
            bias = jnp.concatenate([skewed(table[:, : 2 * tok], tok), skewed(table[:, 2 * tok :], tok)], axis=1)
            scores = scores + bias + dead
            powers = jnp.exp(scores - jnp.max(scores, axis=1, keepdims=True))
            probs = (powers * (1.0 / jnp.sum(powers, axis=1, keepdims=True))).astype(jnp.bfloat16)
            probs_out[pl.ds(head, 1)] = probs[None]
            results.append(product(probs, values))
        mixed_out[:, lanes] = jnp.where(low_half, results[0], results[1]).astype(jnp.bfloat16)
        return carry

    lax.fori_loop(0, heads // 2, attend, 0)
    wait_all(copies[part : 2 * part])
    start_all(cots_first(1))
    loads[3].wait()
    residual = inputs + product(mixed_out[...], held_weights[3])
    residual_out[...] = residual
    scale = lax.rsqrt(jnp.mean(residual * residual, axis=1, keepdims=True) + epsilon)
    moe_in = residual * scale * moe_gain[...]
    logits = lax.dot_general(
        moe_in, router[...], (((1,), (1,)), ((), ())), precision=highest, preferred_element_type=jnp.float32
    )
    logits = jnp.concatenate([logits, jnp.full((tok, LANES - experts), -1e30, jnp.float32)], axis=1)
    lane = iota(logits.shape, 1)
    columns = columns_of(routes_true[...], 2)
    powers = jnp.exp(logits - jnp.max(logits, axis=1, keepdims=True))
    gates = powers / jnp.sum(powers, axis=1, keepdims=True)
    gates_out[...] = gates
    panel = jnp.zeros((experts * room, LANES), jnp.float32)
    for k in range(2):
        pick = jnp.sum(jnp.where(columns[:, k : k + 1] == lane.astype(jnp.float32), gates, 0.0), axis=1, keepdims=True)
        high = pick.astype(jnp.bfloat16)
        low = (pick - high.astype(jnp.float32)).astype(jnp.bfloat16)
        parts = jnp.where(lane == 0, high, jnp.where(lane == 1, low, jnp.zeros_like(low)))
        panel = panel + product(hot[k], parts)
    rows = product(select[...], moe_in.astype(jnp.bfloat16))
    rows_out[:, :, :width] = rows.astype(jnp.bfloat16).reshape(rows_out.shape[0], -1, width)
    rows_out[:, :, width:] = panel.astype(jnp.bfloat16).reshape(rows_out.shape[0], -1, LANES)
    wait_all(copies[2 * part :])
    wait_all(spreads[0].second() + cots_first(1))


def front(dims, number, lengths, tokens, cotangent, routes_row, routes_col, *params):
    heads, experts, room, capacity, n_row, n_col = dims
    tok, width = tokens.shape
    group = n_row * n_col
    blocks = experts * room // group
    half, single = jnp.bfloat16, jnp.float32
    vmem, anywhere = pl.BlockSpec(memory_space=pltpu.VMEM), pl.BlockSpec(memory_space=pl.ANY)
    shapes = [
        ((tok, width), half),
        ((tok, width), half),
        ((2 * tok, 2 * width), half),
        ((heads, tok, 2 * tok), half),
        ((tok, width), half),
        ((tok, width), single),
        ((tok, LANES), single),
        ((group, blocks, width + LANES), half),
        ((group, blocks, width), half),
        ((2, group // 4, blocks, width), half),
        ((group // 4, blocks, width), half),
    ]
    shapes += shapes[-2:-1]
    return pl.pallas_call(
        functools.partial(front_kernel, dims),
        out_shape=[jax.ShapeDtypeStruct(shape, kind) for shape, kind in shapes],
        in_specs=[pl.BlockSpec(memory_space=pltpu.SMEM)] + [vmem] * 8 + [anywhere] * 4,
        out_specs=[vmem] * 8 + [anywhere] * 4,
        scratch_shapes=[
            pltpu.VMEM((experts * room, tok), half),
            pltpu.VMEM((group, blocks, width), half),
            pltpu.VMEM((heads, 4 * tok), single),
            pltpu.VMEM((4, width, width), half),
            pltpu.SemaphoreType.DMA((4,)),
            pltpu.SemaphoreType.DMA,
            pltpu.SemaphoreType.DMA((group - 1,)),
            pltpu.SemaphoreType.DMA((group - 1,)),
            pltpu.SemaphoreType.DMA,
            pltpu.SemaphoreType.DMA,
            pltpu.SemaphoreType.DMA((2, 4)),
            pltpu.SemaphoreType.DMA((2, 4)),
        ],
        compiler_params=pltpu.CompilerParams(
            collective_id=number, has_side_effects=True, vmem_limit_bytes=VMEM_LIMIT
        ),
    )(lengths, tokens, cotangent, routes_row, routes_col, *params)


def panel_sum(panel):
    return panel[:, 0:1].astype(jnp.float32) + panel[:, 1:2].astype(jnp.float32)


def expert_kernel(
    tile,
    sizes,
    rows_sent,
    cot_own,
    cot_near0,
    cot_far0,
    cot_near1,
    gate_weight,
    up_weight,
    down_weight,
    back_landed,
    rows_landed,
    out_rows,
    parts_out,
    cot_far1,
    cot_near2,
    cot_far2,
    cot_near3,
    cot_far3,
    rows_near0,
    rows_far0,
    rows_near1,
    rows_far1,
    rows_near2,
    rows_far2,
    gate_mat,
    up_mat,
    down_mat,
    cot,
    down_rows,
    hidden_all,
    total,
    picks_back,
    back_sent,
    other_rows,
    other_cots,
    staged,
    load_sems,
    own_sems,
    send_sems,
    recv_sems,
    spread_send,
    spread_recv,
    stage_sems,
    other_sems,
):
    group, room, width = cot_own.shape
    hidden_width = gate_mat.shape[1]
    tiles = hidden_width // tile
    loads = []
    for at, (source, target) in enumerate(
        ((cot_own, cot), (down_weight, down_mat), (gate_weight, gate_mat), (up_weight, up_mat))
    ):
        load = pltpu.make_async_copy(source, target, load_sems.at[at])
        load.start()
        loads.append(load)
    devices = partners(*sizes)
    part, quarter = group // 2, group // 4
    strip = part * room
    cot_spreads = [None] + [
        Spread(near, far, spread_send.at[at], spread_recv.at[at])
        for at, (near, far) in enumerate(((cot_near1, cot_far1), (cot_near2, cot_far2), (cot_near3, cot_far3)))
    ]
    row_spreads = [
        Spread(near, far, spread_send.at[3 + at], spread_recv.at[3 + at])
        for at, (near, far) in enumerate(
            ((rows_near0, rows_far0), (rows_near1, rows_far1), (rows_near2, rows_far2))
        )
    ]
    greet(devices[1:] + row_spreads[0].devices)

    def cots_first(piece):
        return cot_spreads[piece].first(cot_own.at[pl.ds(piece * quarter, quarter)])

    def rows_first(piece):
        return row_spreads[piece].first(rows_landed.at[pl.ds(piece * quarter, quarter)])

    def row_copy(way, place):
        source, target = ((rows_sent, rows_landed), (back_sent, back_landed))[way]
        if place == 0:
            return pltpu.make_async_copy(source.at[0], target.at[0], own_sems.at[way])
        sems = (send_sems.at[way, place - 1], recv_sems.at[way, place - 1])
        return remote(source.at[place], target.at[place], *sems, devices[place])

    def stage_copy(at, slot, start, size):
        return pltpu.make_async_copy(
            staged.at[slot, :, pl.ds(0, size)], parts_out.at[at, :, pl.ds(start, size)], stage_sems.at[slot]
        )

    def stage_free(at, start, size):
        @pl.when(at >= 2)
        def _():
            stage_copy(at - 2, lax.rem(at, 2), start, size).wait()

    def stage(at, start, size, hidden, gate_back, up_back):
        slot = lax.rem(at, 2)
        for number, values in enumerate((hidden, gate_back, up_back)):
            staged[slot, number, pl.ds(0, size)] = values
        return stage_copy(at, slot, start, size)

    def stage_end(start, size):
        for at in (tiles - 2, tiles - 1):
            stage_copy(at, at % 2, start, size).wait()

    def own_half(half):
        held = slice(half * part, (half + 1) * part)
        cut_rows = pl.ds(half * strip, strip)
        rows = rows_landed[held, :, :width].reshape(strip, width)
        picks = panel_sum(rows_landed[held, :, width:].reshape(strip, LANES))
        total[...] = jnp.zeros_like(total)
        picks_back[...] = jnp.zeros_like(picks_back)

        def middle(at, carry):
            stage_free(at, half * strip, strip)
            cut = pl.ds(pl.multiple_of(at * tile, tile), tile)
            value, slope = gelu_parts(product(rows, gate_mat[:, cut]))
            up_part = product(rows, up_mat[:, cut])
            hidden = value * up_part
            hidden_low = hidden.astype(jnp.bfloat16)
            hidden_all[cut_rows, cut] = hidden_low
            back = down_rows[cut_rows, cut].astype(jnp.float32)
            weighed = hidden * back
            picks_back[...] += sum(weighed[:, lane : lane + LANES] for lane in range(0, tile, LANES))
            back = back * picks
            gate_back = (back * up_part * slope).astype(jnp.bfloat16)
            up_back = (back * value).astype(jnp.bfloat16)
            store = stage(at, half * strip, strip, hidden_low, gate_back, up_back)
            total[...] += product_back(
                jnp.concatenate([gate_back, up_back], axis=1),
                jnp.concatenate([gate_mat[:, cut], up_mat[:, cut]], axis=1),
            )
            store.start()
            return carry

        lax.fori_loop(0, tiles, middle, 0)
        back_sent[held, :, :width] = total[...].astype(jnp.bfloat16).reshape(part, room, width)
        high, low = halves(jnp.sum(picks_back[...], axis=1, keepdims=True))
        lane = iota((strip, LANES), 1)
        panel = jnp.where(lane == 0, high, jnp.where(lane == 1, low, jnp.zeros_like(low)))
        back_sent[held, :, width:] = panel.reshape(part, room, LANES)
        start_all([row_copy(1, place) for place in range(half * part, (half + 1) * part)])
        stage_end(half * strip, strip)

    def late_seconds():
        wait_all(cots_first(2) + cots_first(3) + rows_first(2))
        start_all(cot_spreads[2].second() + cot_spreads[3].second() + row_spreads[2].second())

    def others(start, sources):
        at, copies = 0, []
        for number, (row_source, cot_source) in enumerate(sources):
            size = row_source.shape[0]
            place = pl.ds(at, size)
            copies += [
                pltpu.make_async_copy(row_source, other_rows.at[place], other_sems.at[0, number]),
                pltpu.make_async_copy(cot_source, other_cots.at[place], other_sems.at[1, number]),
            ]
            at += size
        size = at
        start_all(copies)
        wait_all(copies)
        rows = other_rows[:size, :, :width].reshape(size * room, width)
        picks = panel_sum(other_rows[:size, :, width:].reshape(size * room, LANES))
        cots = (other_cots[:size].reshape(size * room, width).astype(jnp.float32) * picks).astype(jnp.bfloat16)
        size = size * room

        def middle(at, carry):
            pl.when(at == tiles // 2)(late_seconds)
            stage_free(at, start, size)
            cut = pl.ds(pl.multiple_of(at * tile, tile), tile)
            value, slope = gelu_parts(product(rows, gate_mat[:, cut]))
            up_part = product(rows, up_mat[:, cut])
            back = product_back(cots, down_mat[cut, :])
            store = stage(
                at,
                start,
                size,
                (value * up_part).astype(jnp.bfloat16),
                (back * up_part * slope).astype(jnp.bfloat16),
                (back * value).astype(jnp.bfloat16),
            )
            store.start()
            return carry

        lax.fori_loop(0, tiles, middle, 0)
        stage_end(start, size)

    start_all([row_copy(0, place) for place in range(part)])
    start_all(cot_spreads[1].second() + cots_first(2))
    wait_all(loads[:2])
    cot_rows = cot[...].reshape(group * room, width)

    def early(at, carry):
        cut = pl.ds(pl.multiple_of(at * tile, tile), tile)
        down_rows[:, cut] = product_back(cot_rows, down_mat[cut, :]).astype(jnp.bfloat16)
        return carry

    lax.fori_loop(0, tiles, early, 0)
    wait_all(loads[2:])
    wait_all([row_copy(0, place) for place in range(quarter)])
    start_all(rows_first(0))
    wait_all([row_copy(0, place) for place in range(quarter, part)])
    start_all([row_copy(0, place) for place in range(part, group)])
    start_all(rows_first(1))
    own_half(0)
    wait_all(rows_first(0) + rows_first(1))
    start_all(row_spreads[0].second() + row_spreads[1].second() + cots_first(3))
    wait_all([row_copy(0, place) for place in range(part, group)])
    start_all(rows_first(2))
    own_half(1)
    wait_all(cot_spreads[1].second() + row_spreads[0].second() + row_spreads[1].second())
    others(
        2 * strip,
        [(rows_near0.at[k], cot_near0.at[k]) for k in range(2)]
        + [(rows_near1.at[k], cot_near1.at[k]) for k in range(2)]
        + [(rows_far0, cot_far0), (rows_far1, cot_far1)],
    )

    def outward(at, carry):
        cut = pl.ds(pl.multiple_of(at * tile, tile), tile)
        out = product(hidden_all[...], down_mat[:, cut]).astype(jnp.bfloat16)
        out_rows[:, :, cut] = out.reshape(group, room, tile)
        return carry

    lax.fori_loop(0, width // tile, outward, 0)
    wait_all([row_copy(1, place) for place in range(group)])
    wait_all(cot_spreads[2].second() + cot_spreads[3].second() + row_spreads[2].second())


def experts_apply(sizes, number, tile, *operands):
    rows_sent, cot_own = operands[:2]
    group, room, width = cot_own.shape
    hidden_width = operands[5].shape[1]
    slots = group * room
    quarter = group // 4
    half, single = jnp.bfloat16, jnp.float32
    vmem, anywhere = pl.BlockSpec(memory_space=pltpu.VMEM), pl.BlockSpec(memory_space=pl.ANY)
    wide = rows_sent.shape[2]
    shapes = [rows_sent.shape, rows_sent.shape, cot_own.shape, (hidden_width // tile, 3, 5 * slots // 2, tile)]
    shapes += [(quarter, room, width)] + [(2, quarter, room, width), (quarter, room, width)] * 2
    shapes += [(2, quarter, room, wide), (quarter, room, wide)] * 3
    return pl.pallas_call(
        functools.partial(expert_kernel, tile, sizes),
        out_shape=[jax.ShapeDtypeStruct(shape, half) for shape in shapes],
        in_specs=[anywhere] * 8,
        out_specs=[anywhere] + [vmem] * 2 + [anywhere] * 12,
        scratch_shapes=[
            pltpu.VMEM((width, hidden_width), half),
            pltpu.VMEM((width, hidden_width), half),
            pltpu.VMEM((hidden_width, width), half),
            pltpu.VMEM((group, room, width), half),
            pltpu.VMEM((slots, hidden_width), half),
            pltpu.VMEM((slots, hidden_width), half),
            pltpu.VMEM((slots // 2, width), single),
            pltpu.VMEM((slots // 2, LANES), single),
            pltpu.VMEM(rows_sent.shape, half),
            pltpu.VMEM((6 * quarter, room, wide), half),
            pltpu.VMEM((6 * quarter, room, width), half),
            pltpu.VMEM((2, 3, 6 * quarter * room, tile), half),
            pltpu.SemaphoreType.DMA((4,)),
            pltpu.SemaphoreType.DMA((2,)),
            pltpu.SemaphoreType.DMA((2, group - 1)),
            pltpu.SemaphoreType.DMA((2, group - 1)),
            pltpu.SemaphoreType.DMA((6, 4)),
            pltpu.SemaphoreType.DMA((6, 4)),
            pltpu.SemaphoreType.DMA((2,)),
            pltpu.SemaphoreType.DMA((2, 6)),
        ],
        compiler_params=pltpu.CompilerParams(
            collective_id=number, has_side_effects=True, vmem_limit_bytes=VMEM_LIMIT
        ),
    )(*operands)


def column_slots(routes, live, experts, room, capacity):
    tok = live.shape[0]
    names = iota((tok, experts), 1).astype(jnp.float32)
    hot = [(routes[:, k : k + 1] == names) & live for k in range(2)]
    both = jnp.where(hot[0] | hot[1], 1.0, 0.0).astype(jnp.bfloat16)
    before = jnp.where(iota((tok, tok), 1) < iota((tok, tok), 0), 1.0, 0.0).astype(jnp.bfloat16)
    earlier = product(before, both)
    slots = []
    for k in range(2):
        place = jnp.sum(jnp.where(hot[k], earlier, 0.0), axis=1, keepdims=True)
        slot = routes[:, k : k + 1] * room + place
        slots.append(jnp.where(live & (place < capacity), slot, -1.0))
    return slots


def halves(values):
    high = values.astype(jnp.bfloat16)
    return high, (values - high.astype(jnp.float32)).astype(jnp.bfloat16)


def back_kernel(
    dims,
    lengths,
    tokens,
    cotangent,
    near_row,
    routes_true,
    attn_gain,
    moe_gain,
    router,
    residual_in,
    gates_in,
    mixed,
    probs_in,
    queries_in,
    both,
    normed,
    back_in,
    out_sent,
    rows_own,
    query_weight,
    key_weight,
    value_weight,
    out_weight,
    output,
    token_grad,
    query_wgrad,
    key_wgrad,
    value_wgrad,
    small,
    rows_near3,
    rows_far3,
    out_total,
    back,
    out_landed,
    query_grad,
    held_weights,
    mixed_back,
    residual_grad,
    far_sent,
    far_landed,
    near_sum,
    diagonals,
    load_sems,
    own_sem,
    send_sems,
    recv_sems,
    row_send,
    row_recv,
    near_send,
    near_recv,
    out_wgrad,
    *shared,
):
    *held, sum_send, sum_recv = shared
    heads, experts, room, capacity, n_row, n_col, share, depth = dims
    tok, width = tokens.shape
    pair_width = 2 * width // heads
    member_width = pair_width // 2
    slots_count = experts * room
    loads = []
    for at, (source, target) in enumerate(
        ((back_in, back), (out_weight, held_weights.at[0]))
        + tuple((w, held_weights.at[1 + k]) for k, w in enumerate((query_weight, key_weight, value_weight)))
    ):
        load = pltpu.make_async_copy(source, target, load_sems.at[at])
        load.start()
        loads.append(load)
    devices = partners(n_row, n_col)
    spread = Spread(rows_near3, rows_far3, near_send, near_recv)
    quarter = len(devices) // 4
    late_rows = rows_own.at[pl.ds(3 * quarter, quarter)]
    summed = ShareSum((n_row, n_col), depth, [out_wgrad], [out_total], [held], sum_send, sum_recv)
    greet(devices[1:] + spread.devices)
    start_all(spread.first(late_rows))
    copies = [pltpu.make_async_copy(out_sent.at[0], out_landed.at[0], own_sem)]
    for place in range(1, len(devices)):
        sems = (send_sems.at[place - 1], recv_sems.at[place - 1])
        copies.append(remote(out_sent.at[place], out_landed.at[place], *sems, devices[place]))
    start_all(copies)

    piece = lax.axis_index("erow")
    live = iota((tok, 1), 0) + piece * tok < lengths[0]
    slots = column_slots(columns_of(near_row[...], 2), live, experts, room, capacity)
    names = iota((tok, slots_count), 1).astype(jnp.float32)
    hot = [jnp.where(names == slot, 1.0, 0.0).astype(jnp.bfloat16) for slot in slots]
    lane = iota((tok, LANES), 1)
    columns = columns_of(routes_true[...], 2)
    chosen = [columns[:, k : k + 1] == lane.astype(jnp.float32) for k in range(2)]
    gates = gates_in[...]

    residual = residual_in[...]
    scale = lax.rsqrt(jnp.mean(residual * residual, axis=1, keepdims=True) + epsilon)
    moe_in = (residual * scale * moe_gain[...]).astype(jnp.bfloat16)
    loads[0].wait()
    panel = back[:, :, width:].reshape(slots_count, LANES)
    prob_back = jnp.zeros((tok, LANES), jnp.float32)
    for k in range(2):
        parts = product(hot[k], panel)
        prob_back = prob_back + jnp.where(chosen[k], parts[:, 0:1] + parts[:, 1:2], 0.0)
    logit_back = gates * (prob_back - jnp.sum(gates * prob_back, axis=1, keepdims=True))
    logit_high, logit_low = halves(logit_back)
    router_high, router_low = halves(router[...])
    few = slice(0, experts)
    moe_back = (
        product(hot[0] + hot[1], back[:, :, :width].reshape(slots_count, width))
        + product(logit_high[:, few], router_high)
        + product(logit_low[:, few], router_high)
        + product(logit_high[:, few], router_low)
    )
    left = moe_in.T
    router_grad = product(left, logit_high) + product(left, logit_low)
    moe_gain_grad = jnp.sum(residual * scale * moe_back, axis=0, keepdims=True)
    pulled = moe_gain[...] * moe_back
    total = (
        cotangent[...].astype(jnp.float32)
        + scale * pulled
        - residual * (scale * scale * scale * jnp.mean(residual * pulled, axis=1, keepdims=True))
    )
    residual_grad[...] = total
    branch = total.astype(jnp.bfloat16)
    loads[1].wait()
    mixed_back[...] = product_back(branch, held_weights[0]).astype(jnp.bfloat16)
    out_wgrad[...] = product(mixed[...].T, branch).astype(jnp.bfloat16).reshape(out_wgrad.shape)
    summed.turn(0)
    reversal = jnp.where(iota((tok, tok), 0) + iota((tok, tok), 1) == tok - 1, 1.0, 0.0).astype(jnp.bfloat16)
    low_half = iota((tok, pair_width), 1) < member_width

    def unattend(pair, carry):
        lanes = pl.ds(pl.multiple_of(pair * pair_width, pair_width), pair_width)
        value_lanes = pl.ds(pl.multiple_of(width + pair * pair_width, pair_width), pair_width)
        keys, values = both[:, lanes], both[:, value_lanes]
        grads = mixed_back[:, lanes]

        @pl.when(pair == 1)
        def _():
            summed.turn(1)

        @pl.when(pair == 3)
        def _():
            wait_all(spread.first(late_rows))
            start_all(spread.second())

        @pl.when(pair == 5)
        def _():
            summed.turn(2)

        @pl.when(pair == heads // 2 - 1)
        def _():
            summed.turn(3)

        queries_left, grads_left = queries_in[:, lanes].T, grads.T
        query_parts, key_parts, value_parts = [], [], []
        for member in range(2):
            head = 2 * pair + member
            mask = low_half if member == 0 else jnp.logical_not(low_half)
            low = probs_in[pl.ds(head, 1)][0]
            probs = low.astype(jnp.float32)
            part = product_back(jnp.where(mask, grads, jnp.zeros_like(grads)), values)
            weighed = probs * part
            score = (weighed - probs * jnp.sum(weighed, axis=1, keepdims=True)).astype(jnp.bfloat16)
            query_parts.append(product(score, keys))
            span = slice(member * member_width, (member + 1) * member_width)
            key_parts.append(product(queries_left[span], score))
            value_parts.append(product(grads_left[span], low))
            exact = product(reversal, score)
            empty = jnp.zeros((tok, tok), jnp.float32)
            padded = jnp.concatenate([exact[:, :tok], empty, exact[:, tok:], empty], axis=1)
            turned = pltpu.roll(padded, 3 * tok + 1, 1, stride=1, stride_axis=0)
            diagonals[pl.ds(head, 1)] = jnp.sum(turned, axis=0, keepdims=True)
        query_grad[:, lanes] = (jnp.where(low_half, query_parts[0], query_parts[1]) * 0.125).astype(jnp.bfloat16)
        key_part = jnp.concatenate(key_parts, axis=0).T
        value_part = jnp.concatenate(value_parts, axis=0).T
        near_sum[:, lanes] = key_part[:tok]
        near_sum[:, value_lanes] = value_part[:tok]
        far_sent[:, lanes] = key_part[tok:].astype(jnp.bfloat16)
        far_sent[:, value_lanes] = value_part[tok:].astype(jnp.bfloat16)
        return carry

    lax.fori_loop(0, heads // 2, unattend, 0)
    pair_copy = remote(far_sent, far_landed, row_send, row_recv, devices[1])
    pair_copy.start()
    left = normed[...].T
    shape = query_wgrad.shape
    query_wgrad[...] = product(left, query_grad[...]).astype(jnp.bfloat16).reshape(shape)

    segment = width // heads
    table = 4 * tok
    entry = iota((table, LANES), 0)
    other = entry >= table // 4
    other = other & (entry < 3 * table // 4)
    distance = jnp.where(
        other,
        entry - table // 2 + tok * (1 - 2 * piece),
        jnp.where(entry < table // 2, entry, entry - table),
    )
    bucket = bucket_of(distance)
    place = depth * lax.div(bucket, share) + lax.rem(bucket, share)
    target = lax.rem(iota((table, LANES), 1), segment)
    sorted_hot = jnp.where(place == target, 1.0, 0.0).astype(jnp.bfloat16)
    diagonal_high, diagonal_low = halves(diagonals[...])
    bias_rows = product(diagonal_high, sorted_hot) + product(diagonal_low, sorted_hot)
    bias_wide = jnp.concatenate([bias_rows] * (width // LANES), axis=1)
    mine = lax.div(iota((heads, width), 1), segment) == iota((heads, width), 0)
    bias_row = jnp.sum(jnp.where(mine, bias_wide, 0.0), axis=0, keepdims=True)

    loads[2].wait()
    normed_back = product_back(query_grad[...], held_weights[1])
    pair_copy.wait()
    key_total = (near_sum[:, :width] + far_landed[:, :width].astype(jnp.float32)).astype(jnp.bfloat16)
    value_total = (near_sum[:, width:] + far_landed[:, width:].astype(jnp.float32)).astype(jnp.bfloat16)
    key_wgrad[...] = product(left, key_total).astype(jnp.bfloat16).reshape(shape)
    value_wgrad[...] = product(left, value_total).astype(jnp.bfloat16).reshape(shape)
    loads[3].wait()
    loads[4].wait()
    normed_back = normed_back + product_back(key_total, held_weights[2]) + product_back(value_total, held_weights[3])
    inputs = tokens[...].astype(jnp.float32)
    scale = lax.rsqrt(jnp.mean(inputs * inputs, axis=1, keepdims=True) + epsilon)
    attn_gain_grad = jnp.sum(inputs * scale * normed_back, axis=0, keepdims=True)
    pulled = attn_gain[...] * normed_back
    token_grad[...] = (
        residual_grad[...]
        + scale * pulled
        - inputs * (scale * scale * scale * jnp.mean(inputs * pulled, axis=1, keepdims=True))
    )
    empty = jnp.zeros((LANES - 3, width), jnp.float32)
    small[...] = jnp.concatenate([empty, attn_gain_grad, moe_gain_grad, bias_row], axis=0).T + router_grad
    wait_all(copies)
    results = out_landed[...].reshape(slots_count, width)
    total = residual
    for k in range(2):
        pick = jnp.sum(jnp.where(chosen[k], gates, 0.0), axis=1, keepdims=True)
        total = total + pick * product(hot[k], results)
    output[...] = total.astype(jnp.bfloat16)
    wait_all(spread.second())
    summed.turn(4)


def backward(dims, number, *operands):
    heads, experts, room, capacity, n_row, n_col, share, depth = dims
    tokens, back_in, out_sent, rows_own = operands[1], operands[15], operands[16], operands[17]
    tok, width = tokens.shape
    group = n_row * n_col
    half, single = jnp.bfloat16, jnp.float32
    vmem, anywhere = pl.BlockSpec(memory_space=pltpu.VMEM), pl.BlockSpec(memory_space=pl.ANY)
    wgrad = (2, 2, n_row, n_col * depth, width)
    shapes = [((tok, width), half), ((tok, width), single)] + [(wgrad, half)] * 3 + [((width, LANES), single)]
    shapes += [((2, group // 4) + rows_own.shape[1:], half), ((group // 4,) + rows_own.shape[1:], half)]
    shapes += [((depth, width), single)]
    sems = (1, 4 + n_col)
    return pl.pallas_call(
        functools.partial(back_kernel, dims),
        out_shape=[jax.ShapeDtypeStruct(shape, kind) for shape, kind in shapes],
        in_specs=[pl.BlockSpec(memory_space=pltpu.SMEM)] + [vmem] * 14 + [anywhere] * 7,
        out_specs=[vmem] * 6 + [anywhere] * 2 + [vmem],
        scratch_shapes=[
            pltpu.VMEM(back_in.shape, half),
            pltpu.VMEM(out_sent.shape, half),
            pltpu.VMEM((tok, width), half),
            pltpu.VMEM((4, width, width), half),
            pltpu.VMEM((tok, width), half),
            pltpu.VMEM((tok, width), single),
            pltpu.VMEM((tok, 2 * width), half),
            pltpu.VMEM((tok, 2 * width), half),
            pltpu.VMEM((tok, 2 * width), single),
            pltpu.VMEM((heads, 4 * tok), single),
            pltpu.SemaphoreType.DMA((5,)),
            pltpu.SemaphoreType.DMA,
            pltpu.SemaphoreType.DMA((group - 1,)),
            pltpu.SemaphoreType.DMA((group - 1,)),
            pltpu.SemaphoreType.DMA,
            pltpu.SemaphoreType.DMA,
            pltpu.SemaphoreType.DMA((4,)),
            pltpu.SemaphoreType.DMA((4,)),
            pltpu.VMEM(wgrad, half),
        ]
        + share_scratch((n_row, n_col), depth, width, half)
        + [pltpu.SemaphoreType.DMA(sems), pltpu.SemaphoreType.DMA(sems)],
        compiler_params=pltpu.CompilerParams(
            collective_id=number, has_side_effects=True, vmem_limit_bytes=VMEM_LIMIT
        ),
    )(*operands)


def last_kernel(tile, sizes, depth, *refs):
    pieces = 9
    grads, small, refs = refs[:3], refs[3], refs[4:]
    rows_in, refs = refs[:pieces], refs[pieces:]
    cots_in, refs = refs[:pieces], refs[pieces:]
    parts_in, weights, sums, refs = refs[0], refs[1:4], refs[4:8], refs[8:]
    (gate_out, up_out, down_out), refs = refs[:3], refs[3:]
    (rows, cots, mats, tiles_of, own_mats, out_tiles, down_tiles), refs = refs[:7], refs[7:]
    held, refs = [refs[5 * at : 5 * at + 5] for at in range(4)], refs[20:]
    load_sems, weight_sems, own_sems, out_sems, down_sem, send_sems, recv_sems = refs
    width = grads[0].shape[4]
    hidden_width = weights[0].shape[1]
    tiles = hidden_width // tile
    ready = parts_in.shape[2]
    total_rows = rows.shape[0]
    chunk = (total_rows - ready) // 2
    share = width // 4
    hidden_share = hidden_width // 4
    replica = lax.axis_index("dp")
    summed = ShareSum(sizes, depth, list(grads) + [small], sums, held, send_sems, recv_sems)
    barrier = pltpu.get_barrier_semaphore()
    for device in summed.devices:
        pl.semaphore_signal(barrier, 1, device_id=device, device_id_type=MESH)
    loads, start = [], 0
    for at, (row_piece, cot_piece) in enumerate(zip(rows_in, cots_in)):
        size = row_piece.shape[0]
        for number, (piece, target) in enumerate(((row_piece, rows), (cot_piece, cots))):
            load = pltpu.make_async_copy(piece, target.at[pl.ds(start, size)], load_sems.at[number, at])
            load.start()
            loads.append(load)
        start += size

    def weight_loads(at, slot):
        cut = pl.ds(pl.multiple_of(at * tile, tile), tile)
        return [
            pltpu.make_async_copy(source, mats.at[number, slot], weight_sems.at[number, slot])
            for number, source in enumerate((weights[0].at[:, cut], weights[1].at[:, cut]))
        ] + [pltpu.make_async_copy(weights[2].at[cut], own_mats.at[slot], weight_sems.at[2, slot])]

    def own_loads(at, slot):
        return [
            pltpu.make_async_copy(parts_in.at[at], tiles_of.at[slot, :, pl.ds(0, ready)], own_sems.at[slot])
        ]

    def out_copies(at, slot):
        cut = pl.ds(pl.multiple_of(at * tile, tile), tile)
        return [
            pltpu.make_async_copy(out_tiles.at[number, slot], target.at[:, cut], out_sems.at[number, slot])
            for number, target in enumerate((gate_out, up_out))
        ]

    share_lanes = pl.ds(pl.multiple_of(replica * share, share), share)
    first = lax.div(replica * hidden_share, tile)
    spans = lax.div((replica + 1) * hidden_share - 1, tile) - first + 1

    def tile_at(turn):
        return lax.rem(first + turn, tiles)

    start_all(weight_loads(tile_at(0), 0) + own_loads(tile_at(0), 0))
    pl.semaphore_wait(barrier, len(summed.devices))
    summed.turn(0)
    for load in loads:
        load.wait()

    def weigh(at, carry):
        cut = pl.ds(pl.multiple_of(at * 256, 256), 256)
        panel = rows[cut, width:]
        picks = panel[:, 0:1].astype(jnp.float32) + panel[:, 1:2].astype(jnp.float32)
        cots[cut] = (cots[cut].astype(jnp.float32) * picks).astype(jnp.bfloat16)
        return carry

    lax.fori_loop(0, total_rows // 256, weigh, 0)
    summed.turn(1)
    turn_tiles = (1, 3, 5, 7, 9, 10)
    blocks = 1 if chunk <= 512 else 2

    def each_tile(turn, carry):
        slot = lax.rem(turn, 2)
        at = tile_at(turn)
        wait_all(weight_loads(at, slot) + own_loads(at, slot))

        @pl.when(turn + 1 < tiles)
        def _():
            start_all(weight_loads(tile_at(turn + 1), 1 - slot) + own_loads(tile_at(turn + 1), 1 - slot))

        for number in range(2, summed.turns):
            @pl.when(turn == turn_tiles[number - 2])
            def _(number=number):
                summed.turn(number)

        @pl.when(turn >= 2)
        def _():
            wait_all(out_copies(tile_at(turn - 2), slot))

        size = 2 * chunk // blocks
        for block in range(blocks):
            cut = pl.ds(ready + block * size, size)
            value, slope = gelu_parts(product(rows[cut, :width], mats[0, slot]))
            up_part = product(rows[cut, :width], mats[1, slot])
            back = product_back(cots[cut], own_mats[slot])
            tiles_of[slot, 0, cut] = (value * up_part).astype(jnp.bfloat16)
            tiles_of[slot, 1, cut] = (back * up_part * slope).astype(jnp.bfloat16)
            tiles_of[slot, 2, cut] = (back * value).astype(jnp.bfloat16)
        both = jnp.concatenate([tiles_of[slot, 1], tiles_of[slot, 2]], axis=1)
        turned = product_left(both, rows[:, share_lanes]).T
        out_tiles[0, slot] = turned[:, :tile]
        out_tiles[1, slot] = turned[:, tile:]
        start_all(out_copies(at, slot))

        @pl.when(turn < spans)
        def _():
            place = pl.ds(pl.multiple_of(turn * tile, tile), tile)
            down_tiles[place] = product_left(tiles_of[slot, 0], cots[...])

        return carry

    lax.fori_loop(0, tiles, each_tile, 0)
    offset = pl.multiple_of(replica * hidden_share - first * tile, 8)
    down_copy = pltpu.make_async_copy(down_tiles.at[pl.ds(offset, hidden_share)], down_out, down_sem)
    down_copy.start()
    for turn in (tiles - 2, tiles - 1):
        wait_all(out_copies(tile_at(turn), turn % 2))
    down_copy.wait()


def last(sizes, number, grads, small, rows_in, cots_in, parts_in, weights):
    n_dp, n_row, n_col = sizes
    width, hidden_width = weights[0].shape
    total_rows = sum(piece.shape[0] for piece in rows_in)
    tile = parts_in.shape[3]
    depth = width // (n_dp * n_row * n_col)
    strip = n_col * depth
    half, single = jnp.bfloat16, jnp.float32
    vmem, anywhere = pl.BlockSpec(memory_space=pltpu.VMEM), pl.BlockSpec(memory_space=pl.ANY)
    small = small.reshape(2, 2, n_row, strip, small.shape[1])
    hidden_share = hidden_width // n_dp
    spans = -(-hidden_share // tile) + 1
    scratch = [
        pltpu.VMEM((total_rows, width + LANES), half),
        pltpu.VMEM((total_rows, width), half),
        pltpu.VMEM((2, 2, width, tile), half),
        pltpu.VMEM((2, 3, total_rows, tile), half),
        pltpu.VMEM((2, tile, width), half),
        pltpu.VMEM((2, 2, width // n_dp, tile), single),
        pltpu.VMEM((spans * tile, width), single),
    ]
    for _ in range(3):
        scratch += share_scratch((n_row, n_col), depth, width, half)
    scratch += share_scratch((n_row, n_col), depth, LANES, single)
    sems = (4, 4 + n_col)
    scratch += [
        pltpu.SemaphoreType.DMA((2, len(rows_in))),
        pltpu.SemaphoreType.DMA((3, 2)),
        pltpu.SemaphoreType.DMA((2,)),
        pltpu.SemaphoreType.DMA((2, 2)),
        pltpu.SemaphoreType.DMA,
        pltpu.SemaphoreType.DMA(sems),
        pltpu.SemaphoreType.DMA(sems),
    ]
    out_shape = [jax.ShapeDtypeStruct((depth, width), single)] * 3
    out_shape += [jax.ShapeDtypeStruct((depth, LANES), single)]
    out_shape += [jax.ShapeDtypeStruct((width // n_dp, hidden_width), single)] * 2
    out_shape += [jax.ShapeDtypeStruct((hidden_share, width), single)]
    return pl.pallas_call(
        functools.partial(last_kernel, tile, (n_row, n_col), depth),
        out_shape=out_shape,
        in_specs=[vmem] * 4 + [anywhere] * (2 * len(rows_in) + 4),
        out_specs=[vmem] * 4 + [anywhere] * 3,
        scratch_shapes=scratch,
        compiler_params=pltpu.CompilerParams(
            collective_id=number, has_side_effects=True, vmem_limit_bytes=VMEM_LIMIT
        ),
    )(*grads, small, *rows_in, *cots_in, parts_in, *weights)


def finish_kernel(experts, bias_share, small, *refs):
    count = (len(refs) - 5) // 3
    sources, targets, rest = refs[:count], refs[count : 2 * count], refs[2 * count :]
    (attn_out, moe_out, bias_out, router_out), held, sems = rest[:4], rest[4:-1], rest[-1]
    loads = [
        pltpu.make_async_copy(source, place, sems.at[0, at]) for at, (source, place) in enumerate(zip(sources, held))
    ]
    stores = [
        pltpu.make_async_copy(place, target, sems.at[1, at]) for at, (place, target) in enumerate(zip(held, targets))
    ]
    start_all(loads)
    turned = small[...].T
    attn_out[...] = turned[LANES - 3 : LANES - 2]
    moe_out[...] = turned[LANES - 2 : LANES - 1]
    bias_out[...] = turned[LANES - 1 :, :bias_share]
    router_out[...] = turned[:experts]
    for load, store in zip(loads, stores):
        load.wait()
        store.start()
    wait_all(stores)


def finish(experts, bias_share, small, *arrays):
    depth = small.shape[0]
    vmem, anywhere = pl.BlockSpec(memory_space=pltpu.VMEM), pl.BlockSpec(memory_space=pl.ANY)
    shapes = [(array.shape, array.dtype) for array in arrays]
    shapes += [((1, depth), small.dtype)] * 2 + [((1, bias_share), small.dtype), ((experts, depth), small.dtype)]
    return pl.pallas_call(
        functools.partial(finish_kernel, experts, bias_share),
        out_shape=[jax.ShapeDtypeStruct(*shape) for shape in shapes],
        in_specs=[vmem] + [anywhere] * len(arrays),
        out_specs=[anywhere] * len(arrays) + [vmem] * 4,
        scratch_shapes=[pltpu.VMEM(array.shape, array.dtype) for array in arrays]
        + [pltpu.SemaphoreType.DMA((2, len(arrays)))],
        compiler_params=pltpu.CompilerParams(vmem_limit_bytes=VMEM_LIMIT),
    )(small, *arrays)


def gelu_parts(gate_part):
    square = gate_part * gate_part
    inner = gate_part * (0.7978845608028654 + 0.035677408136300125 * square)
    half = 0.5 + 0.5 * jnp.tanh(inner)
    value = gate_part * half
    slope = half + value * (1.0 - half) * (1.5957691216057308 + 0.21406444881780075 * square)
    return value, slope


def paired(own, *pieces):
    blocks = [own]
    for at in range(0, len(pieces), 2):
        blocks += [pieces[at][0], pieces[at + 1][0], pieces[at][1], pieces[at + 1][1]]
    return [block.reshape(-1, block.shape[-1]) for block in blocks]


def body(
    tokens,
    lengths,
    routes,
    attn_gain,
    query_weight,
    key_weight,
    value_weight,
    out_weight,
    relative_bias,
    moe_gain,
    router_weight,
    gate_weight,
    up_weight,
    down_weight,
    cotangent,
):
    tok_rows, width = tokens.shape[1:]
    head_count, bucket_count = relative_bias.shape
    expert_count = router_weight.shape[1]
    capacity = 5 * tok_rows // (2 * expert_count)
    room = -(-capacity // 16) * 16
    n_dp, n_row, n_col = (lax.axis_size(name) for name in ("dp", "erow", "ecol"))
    device_count = n_dp * n_row * n_col
    slot_count = expert_count * room
    gate_mat, up_mat, down_mat = gate_weight[0], up_weight[0], down_weight[0]
    routes_row = routes[0].T
    near_routes = mirrored((routes_row % n_col) ^ lax.axis_index("ecol"), n_col) * n_row + (
        (routes_row // n_col) ^ lax.axis_index("erow")
    )
    router = router_weight.T
    dims = (head_count, expert_count, room, capacity, n_row, n_col)
    normed, queries, both, probs, mixed, residual, gates, slot_rows, got_grads, *cots01 = front(
        dims,
        0,
        lengths,
        tokens[0],
        cotangent[0],
        near_routes,
        routes_row,
        attn_gain[None],
        moe_gain[None],
        relative_bias,
        router,
        query_weight,
        key_weight,
        value_weight,
        out_weight,
    )
    back, got, expert_out, parts, *moved = experts_apply(
        (n_row, n_col), 1, 256 if slot_count <= 768 else LANES, slot_rows, got_grads, *cots01, gate_mat, up_mat, down_mat
    )
    cots0, cots1, cots2, cots3, rows0, rows1, rows2 = ((cots01 + moved)[at : at + 2] for at in range(0, 14, 2))
    depth = width // device_count
    bias_share = head_count * bucket_count // device_count
    output, token_grad, query_wgrad, key_wgrad, value_wgrad, small, *rows3, out_sum = backward(
        dims + (bias_share, depth),
        2,
        lengths,
        tokens[0],
        cotangent[0],
        near_routes,
        routes_row,
        attn_gain[None],
        moe_gain[None],
        router,
        residual,
        gates,
        mixed,
        probs,
        queries,
        both,
        normed,
        back,
        expert_out,
        got,
        query_weight,
        key_weight,
        value_weight,
        out_weight,
    )
    query_sum, key_sum, value_sum, small_sum, gate_total, up_total, down_total = last(
        (n_dp, n_row, n_col),
        3,
        (query_wgrad, key_wgrad, value_wgrad),
        small,
        paired(got, rows0, rows1, rows2, rows3),
        paired(got_grads, cots0, cots1, cots2, cots3),
        parts,
        (gate_mat, up_mat, down_mat),
    )
    handed = finish(
        expert_count,
        bias_share,
        small_sum,
        output,
        token_grad,
        query_sum,
        key_sum,
        value_sum,
        out_sum,
        gate_total,
        up_total,
        down_total,
    )
    output, token_grad, query_sum, key_sum, value_sum, out_sum, gate_total, up_total, down_total = handed[:9]
    attn_sum, moe_sum, bias_sum, router_sum = handed[9:]
    return (
        output[None],
        token_grad[None],
        attn_sum[0],
        query_sum,
        key_sum,
        value_sum,
        out_sum,
        bias_sum[0],
        moe_sum[0],
        router_sum.T,
        gate_total[None],
        up_total[None],
        down_total[None],
    )


def solution(mesh):
    rows = P(("dp", "ecol"), "erow", None)
    experts = P(("erow", "ecol"), None, None)
    every = ("dp", "erow", "ecol")
    shares = P(("erow", "ecol"), "dp", None)
    return jax.shard_map(
        body,
        mesh=mesh,
        in_specs=(
            (rows, P(("dp", "ecol")), rows) + (P(),) * 8 + (experts, experts, experts, rows)
        ),
        out_specs=(rows, rows, P(every))
        + (P(every, None),) * 4
        + (P(every), P(every), P(every, None), shares, shares, shares),
        check_vma=False,
    )
```

```python
import functools

import jax
import jax.numpy as jnp
from jax import lax
from jax.experimental import pallas as pl
from jax.experimental.pallas import tpu as pltpu
from jax.sharding import PartitionSpec as P

epsilon = 1e-06
highest = lax.Precision.HIGHEST
thresholds = (12, 16, 23, 32, 46, 64, 91)
MESH = pl.DeviceIdType.MESH
LANES = 128
VMEM_LIMIT = 60 * 1024 * 1024


def bucket_of(offset):
    distance = jnp.abs(offset)
    larger = 8 + sum(((distance >= bound_at).astype(jnp.int32) for bound_at in thresholds))
    return jnp.where(offset > 0, 16, 0) + jnp.where(distance < 8, distance, larger)


def product(left_side, right_side):
    return jnp.dot(left_side, right_side, preferred_element_type=jnp.float32)


def product_back(left_side, right_side):
    return lax.dot_general(
        left_side, right_side, (((1,), (1,)), ((), ())), preferred_element_type=jnp.float32
    )


def product_left(left_side, right_side):
    return lax.dot_general(
        left_side, right_side, (((0,), (0,)), ((), ())), preferred_element_type=jnp.float32
    )


def greet(devices):
    barrier = pltpu.get_barrier_semaphore()
    for device in devices:
        pl.semaphore_signal(barrier, 1, device_id=device, device_id_type=MESH)
    pl.semaphore_wait(barrier, len(devices))


def remote(source, target, send_sem, recv_sem, device):
    return pltpu.make_async_remote_copy(
        src_ref=source,
        dst_ref=target,
        send_sem=send_sem,
        recv_sem=recv_sem,
        device_id=device,
        device_id_type=MESH,
    )


def flipped(index, mask, size):
    bit = 1
    while bit < size:
        if mask & bit:
            index = index + bit * (1 - 2 * lax.rem(lax.div(index, bit), 2))
        bit *= 2
    return index


def mirrored(value, size):
    result, bit = value * 0, 1
    while bit < size:
        result = result * 2 + (value // bit) % 2
        bit *= 2
    return result


def partners(n_row, n_col):
    row, col = lax.axis_index("erow"), lax.axis_index("ecol")
    return [
        {
            "erow": flipped(row, place % n_row, n_row),
            "ecol": flipped(col, mirrored(place // n_row, n_col), n_col),
        }
        for place in range(n_row * n_col)
    ]


class Spread:
    def __init__(self, near, far, send_sems, recv_sems):
        dp = lax.axis_index("dp")
        slow, fast = lax.div(dp, 2), lax.rem(dp, 2)
        self.devices = [{"dp": slow * 2 + 1 - fast}, {"dp": (1 - slow) * 2 + fast}]
        self.near, self.far, self.send_sems, self.recv_sems = near, far, send_sems, recv_sems

    def first(self, source):
        return [
            remote(source, self.near.at[k], self.send_sems.at[k], self.recv_sems.at[k], self.devices[k])
            for k in range(2)
        ]

    def second(self, near=None):
        near = self.near if near is None else near
        half = self.far.shape[0] // 2
        return [
            remote(
                near.at[k, pl.ds(k * half, half)],
                self.far.at[pl.ds(k * half, half)],
                self.send_sems.at[2 + k],
                self.recv_sems.at[2 + k],
                self.devices[1 - k],
            )
            for k in range(2)
        ]


def start_all(copies):
    for copy in copies:
        copy.start()


def wait_all(copies):
    for copy in copies:
        copy.wait()


class ShareSum:
    stages = 5

    def __init__(self, sizes, depth, grads, totals, held, send_sems, recv_sems):
        self.n_row, self.n_col = sizes
        self.depth, self.grads, self.totals, self.held = depth, grads, totals, held
        self.send_sems, self.recv_sems = send_sems, recv_sems
        dp, self.row, self.col = (lax.axis_index(name) for name in ("dp", "erow", "ecol"))
        self.slow, self.fast = lax.div(dp, 2), lax.rem(dp, 2)
        self.over_row = {"erow": 1 - self.row}
        self.over_fast = {"dp": self.slow * 2 + 1 - self.fast}
        self.over_slow = {"dp": (1 - self.slow) * 2 + self.fast}
        self.over_col = [{"ecol": flipped(self.col, mask, self.n_col)} for mask in range(1, self.n_col)]
        self.devices = [self.over_row, self.over_fast, self.over_slow] + self.over_col

    def parts(self, at):
        width = self.grads[at].shape[-1]
        if width >= 2 * LANES:
            return ((0, pl.ds(0, width // 2)), (1, pl.ds(width // 2, width // 2)))
        return ((0, pl.ds(0, width)),)

    def copy(self, at, number):
        from_row, from_near, from_far, late_sum, from_col = self.held[at]
        sems = (self.send_sems.at[at, number], self.recv_sems.at[at, number])
        if number == 0:
            return remote(self.grads[at].at[:, :, 1 - self.row], from_row, *sems, self.over_row)
        if number <= 4:
            which, cut = self.parts(at)[(number - 1) % 2]
            if number == 1:
                return remote(from_row.at[:, 1 - self.fast, :, cut], from_near.at[:, :, cut], *sems, self.over_fast)
            if number == 2:
                return remote(from_row.at[1 - self.slow, :, :, cut], from_near.at[:, :, cut], *sems, self.over_slow)
            if number == 3:
                return remote(from_near.at[1 - self.slow, :, cut], from_far.at[:, cut], *sems, self.over_slow)
            return remote(from_near.at[1 - self.fast, :, cut], from_far.at[:, cut], *sems, self.over_fast)
        mask = number - 4
        peer = flipped(self.col, mask, self.n_col)
        return remote(late_sum.at[peer], from_col.at[mask - 1], *sems, self.over_col[mask - 1])

    def step(self, at, stage):
        from_row, from_near, from_far, late_sum, from_col = self.held[at]
        if stage == 0:
            self.copy(at, 0).start()
        elif stage == 1:
            self.copy(at, 0).wait()
            for high in range(2):
                for low in range(2):
                    from_row[high, low] = (
                        self.grads[at][high, low, self.row].astype(jnp.float32)
                        + from_row[high, low].astype(jnp.float32)
                    ).astype(from_row.dtype)
            for which, _ in self.parts(at):
                self.copy(at, 1 + which).start()
        elif stage == 2:
            for which, cut in self.parts(at):
                self.copy(at, 1 + which).wait()
                for place in range(2):
                    kept = from_row[place, self.fast, :, cut] if which == 0 else from_row[self.slow, place, :, cut]
                    from_near[place, :, cut] = (
                        kept.astype(jnp.float32) + from_near[place, :, cut].astype(jnp.float32)
                    ).astype(from_near.dtype)
                self.copy(at, 3 + which).start()
        elif stage == 3:
            for which, cut in self.parts(at):
                self.copy(at, 3 + which).wait()
                kept = from_near[self.slow if which == 0 else self.fast, :, cut]
                total = kept.astype(jnp.float32) + from_far[:, cut].astype(jnp.float32)
                late_sum[:, :, cut] = total.reshape(self.n_col, self.depth, -1).astype(late_sum.dtype)
            for mask in range(1, self.n_col):
                self.copy(at, 4 + mask).start()
        else:
            total = late_sum[self.col].astype(jnp.float32)
            for mask in range(1, self.n_col):
                self.copy(at, 4 + mask).wait()
                total = total + from_col[mask - 1].astype(jnp.float32)
            self.totals[at][...] = total

    def turn(self, number):
        for at in range(len(self.grads)):
            if 0 <= number - at < self.stages:
                self.step(at, number - at)

    @property
    def turns(self):
        return len(self.grads) + self.stages - 1


def share_scratch(sizes, depth, width, kind):
    n_row, n_col = sizes
    strip = n_col * depth
    late = kind if depth % 16 == 0 else jnp.float32
    return [
        pltpu.VMEM((2, 2, strip, width), kind),
        pltpu.VMEM((2, strip, width), kind),
        pltpu.VMEM((strip, width), kind),
        pltpu.VMEM((n_col, depth, width), late),
        pltpu.VMEM((n_col - 1, depth, width), late),
    ]


def iota(shape, dimension):
    return lax.broadcasted_iota(jnp.int32, shape, dimension)


def columns_of(rows, count):
    padded = jnp.concatenate([rows.astype(jnp.float32), jnp.zeros((8 - count, rows.shape[1]), jnp.float32)], axis=0)
    return padded.T


def row_slots(routes, live, experts, room, capacity):
    tok = live.shape[1]
    names = iota((experts, tok), 0)
    hot = [(routes[k : k + 1] == names) & live for k in range(2)]
    both = jnp.where(hot[0] | hot[1], 1.0, 0.0).astype(jnp.bfloat16)
    before = jnp.where(iota((tok, tok), 0) < iota((tok, tok), 1), 1.0, 0.0).astype(jnp.bfloat16)
    earlier = product(both, before)
    slots = []
    for k in range(2):
        place = jnp.sum(jnp.where(hot[k], earlier, 0.0), axis=0, keepdims=True)
        slot = routes[k : k + 1].astype(jnp.float32) * room + place
        slots.append(jnp.where(live & (place < capacity), slot, -1.0))
    return slots


def bias_tables(relative_bias, table_width, offset):
    buckets = relative_bias.shape[1]
    place = iota((buckets, table_width), 1)
    distance = jnp.where(place < table_width // 2, place, place - table_width) + offset
    hot = jnp.where(bucket_of(distance) == iota((buckets, table_width), 0), 1.0, 0.0)
    return jnp.dot(relative_bias, hot, precision=highest, preferred_element_type=jnp.float32)


def skewed(row, rows):
    width = row.shape[1]
    full = pltpu.roll(jnp.broadcast_to(row, (rows, width)), 0, 1, stride=1, stride_axis=0)
    return full[:, : width // 2]


def front_kernel(
    dims,
    lengths,
    tokens,
    cotangent,
    routes_row,
    routes_true,
    attn_gain,
    moe_gain,
    relative_bias,
    router,
    query_weight,
    key_weight,
    value_weight,
    out_weight,
    normed_out,
    query_out,
    both_out,
    probs_out,
    mixed_out,
    residual_out,
    gates_out,
    rows_out,
    cot_landed,
    cot_near0,
    cot_far0,
    cot_near1,
    select,
    cot_slots,
    tables,
    held_weights,
    weight_sems,
    own_sem,
    send_sems,
    recv_sems,
    row_send,
    row_recv,
    near_send,
    near_recv,
):
    heads, experts, room, capacity, n_row, n_col = dims
    tok, width = tokens.shape
    pair_width = 2 * width // heads
    loads = []
    for at, source in enumerate((key_weight, value_weight, query_weight, out_weight)):
        load = pltpu.make_async_copy(source, held_weights.at[at], weight_sems.at[at])
        load.start()
        loads.append(load)
    devices = partners(n_row, n_col)
    spreads = [
        Spread(near, far, near_send.at[at], near_recv.at[at])
        for at, (near, far) in enumerate(((cot_near0, cot_far0), (cot_near1, None)))
    ]
    part = len(devices) // 4
    barrier = pltpu.get_barrier_semaphore()
    for device in devices[1:] + spreads[0].devices:
        pl.semaphore_signal(barrier, 1, device_id=device, device_id_type=MESH)

    piece = lax.axis_index("erow")
    length = lengths[0]
    live = iota((1, tok), 1) + piece * tok < length
    slots = row_slots(routes_row[...], live, experts, room, capacity)
    names = iota((experts * room, tok), 0).astype(jnp.float32)
    hot = [jnp.where(names == slot, 1.0, 0.0).astype(jnp.bfloat16) for slot in slots]
    select[...] = hot[0] + hot[1]
    cot_slots[...] = product(select[...], cotangent[...]).astype(jnp.bfloat16).reshape(cot_slots.shape)
    pl.semaphore_wait(barrier, len(devices) + 1)
    own = pltpu.make_async_copy(cot_slots.at[0], cot_landed.at[0], own_sem)
    copies = [own] + [
        remote(
            cot_slots.at[place],
            cot_landed.at[place],
            send_sems.at[place - 1],
            recv_sems.at[place - 1],
            devices[place],
        )
        for place in range(1, len(devices))
    ]
    start_all(copies)

    def cots_first(piece):
        return spreads[piece].first(cot_landed.at[pl.ds(piece * part, part)])

    inputs = tokens[...].astype(jnp.float32)
    scale = lax.rsqrt(jnp.mean(inputs * inputs, axis=1, keepdims=True) + epsilon)
    normed = (inputs * scale * attn_gain[...]).astype(jnp.bfloat16)
    normed_out[...] = normed
    loads[0].wait()
    both_out[:tok, :width] = product(normed, held_weights[0]).astype(jnp.bfloat16)
    loads[1].wait()
    both_out[:tok, width:] = product(normed, held_weights[1]).astype(jnp.bfloat16)
    pair_copy = remote(both_out.at[pl.ds(0, tok)], both_out.at[pl.ds(tok, tok)], row_send, row_recv, devices[1])
    pair_copy.start()
    loads[2].wait()
    query_out[...] = (product(normed, held_weights[2]) * 0.125).astype(jnp.bfloat16)
    offset = tok * (1 - 2 * piece)
    tables[:, : 2 * tok] = bias_tables(relative_bias[...], 2 * tok, 0)
    tables[:, 2 * tok :] = bias_tables(relative_bias[...], 2 * tok, offset)
    place = iota((1, 2 * tok), 1)
    position = jnp.where(place < tok, place + piece * tok, place - tok + (1 - piece) * tok)
    dead = jnp.where(position < length, 0.0, -1000000000.0)
    low_half = iota((tok, pair_width), 1) < pair_width // 2
    pair_copy.wait()

    def attend(pair, carry):
        lanes = pl.ds(pl.multiple_of(pair * pair_width, pair_width), pair_width)
        value_lanes = pl.ds(pl.multiple_of(width + pair * pair_width, pair_width), pair_width)
        queries, keys, values = query_out[:, lanes], both_out[:, lanes], both_out[:, value_lanes]

        @pl.when(pair == 0)
        def _():
            wait_all(copies[:part])
            start_all(cots_first(0))

        @pl.when(pair == heads // 4)
        def _():
            wait_all(cots_first(0))
            start_all(spreads[0].second())

        results = []
        for member in range(2):
            mask = low_half if member == 0 else jnp.logical_not(low_half)
            head = 2 * pair + member
            scores = product_back(jnp.where(mask, queries, jnp.zeros_like(queries)), keys)
            table = tables[pl.ds(head, 1)]
            bias = jnp.concatenate([skewed(table[:, : 2 * tok], tok), skewed(table[:, 2 * tok :], tok)], axis=1)
            scores = scores + bias + dead
            powers = jnp.exp(scores - jnp.max(scores, axis=1, keepdims=True))
            probs = (powers * (1.0 / jnp.sum(powers, axis=1, keepdims=True))).astype(jnp.bfloat16)
            probs_out[pl.ds(head, 1)] = probs[None]
            results.append(product(probs, values))
        mixed_out[:, lanes] = jnp.where(low_half, results[0], results[1]).astype(jnp.bfloat16)
        return carry

    lax.fori_loop(0, heads // 2, attend, 0)
    wait_all(copies[part : 2 * part])
    start_all(cots_first(1))
    loads[3].wait()
    residual = inputs + product(mixed_out[...], held_weights[3])
    residual_out[...] = residual
    scale = lax.rsqrt(jnp.mean(residual * residual, axis=1, keepdims=True) + epsilon)
    moe_in = residual * scale * moe_gain[...]
    logits = lax.dot_general(
        moe_in, router[...], (((1,), (1,)), ((), ())), precision=highest, preferred_element_type=jnp.float32
    )
    logits = jnp.concatenate([logits, jnp.full((tok, LANES - experts), -1e30, jnp.float32)], axis=1)
    lane = iota(logits.shape, 1)
    columns = columns_of(routes_true[...], 2)
    powers = jnp.exp(logits - jnp.max(logits, axis=1, keepdims=True))
    gates = powers / jnp.sum(powers, axis=1, keepdims=True)
    gates_out[...] = gates
    panel = jnp.zeros((experts * room, LANES), jnp.float32)
    for k in range(2):
        pick = jnp.sum(jnp.where(columns[:, k : k + 1] == lane.astype(jnp.float32), gates, 0.0), axis=1, keepdims=True)
        high = pick.astype(jnp.bfloat16)
        low = (pick - high.astype(jnp.float32)).astype(jnp.bfloat16)
        parts = jnp.where(lane == 0, high, jnp.where(lane == 1, low, jnp.zeros_like(low)))
        panel = panel + product(hot[k], parts)
    rows = product(select[...], moe_in.astype(jnp.bfloat16))
    rows_out[:, :, :width] = rows.astype(jnp.bfloat16).reshape(rows_out.shape[0], -1, width)
    rows_out[:, :, width:] = panel.astype(jnp.bfloat16).reshape(rows_out.shape[0], -1, LANES)
    wait_all(copies[2 * part :])
    wait_all(spreads[0].second() + cots_first(1))


def front(dims, number, lengths, tokens, cotangent, routes_row, routes_col, *params):
    heads, experts, room, capacity, n_row, n_col = dims
    tok, width = tokens.shape
    group = n_row * n_col
    blocks = experts * room // group
    half, single = jnp.bfloat16, jnp.float32
    vmem, anywhere = pl.BlockSpec(memory_space=pltpu.VMEM), pl.BlockSpec(memory_space=pl.ANY)
    shapes = [
        ((tok, width), half),
        ((tok, width), half),
        ((2 * tok, 2 * width), half),
        ((heads, tok, 2 * tok), half),
        ((tok, width), half),
        ((tok, width), single),
        ((tok, LANES), single),
        ((group, blocks, width + LANES), half),
        ((group, blocks, width), half),
        ((2, group // 4, blocks, width), half),
        ((group // 4, blocks, width), half),
    ]
    shapes += shapes[-2:-1]
    return pl.pallas_call(
        functools.partial(front_kernel, dims),
        out_shape=[jax.ShapeDtypeStruct(shape, kind) for shape, kind in shapes],
        in_specs=[pl.BlockSpec(memory_space=pltpu.SMEM)] + [vmem] * 8 + [anywhere] * 4,
        out_specs=[vmem] * 8 + [anywhere] * 4,
        scratch_shapes=[
            pltpu.VMEM((experts * room, tok), half),
            pltpu.VMEM((group, blocks, width), half),
            pltpu.VMEM((heads, 4 * tok), single),
            pltpu.VMEM((4, width, width), half),
            pltpu.SemaphoreType.DMA((4,)),
            pltpu.SemaphoreType.DMA,
            pltpu.SemaphoreType.DMA((group - 1,)),
            pltpu.SemaphoreType.DMA((group - 1,)),
            pltpu.SemaphoreType.DMA,
            pltpu.SemaphoreType.DMA,
            pltpu.SemaphoreType.DMA((2, 4)),
            pltpu.SemaphoreType.DMA((2, 4)),
        ],
        compiler_params=pltpu.CompilerParams(
            collective_id=number, has_side_effects=True, vmem_limit_bytes=VMEM_LIMIT
        ),
    )(lengths, tokens, cotangent, routes_row, routes_col, *params)


def panel_sum(panel):
    return panel[:, 0:1].astype(jnp.float32) + panel[:, 1:2].astype(jnp.float32)


def expert_kernel(
    tile,
    sizes,
    rows_sent,
    cot_own,
    cot_near0,
    cot_far0,
    cot_near1,
    gate_weight,
    up_weight,
    down_weight,
    back_landed,
    rows_landed,
    out_rows,
    parts_out,
    cot_far1,
    cot_near2,
    cot_far2,
    cot_near3,
    cot_far3,
    rows_near0,
    rows_far0,
    rows_near1,
    rows_far1,
    rows_near2,
    rows_far2,
    gate_mat,
    up_mat,
    down_mat,
    cot,
    down_rows,
    hidden_all,
    total,
    picks_back,
    back_sent,
    other_rows,
    other_cots,
    staged,
    load_sems,
    own_sems,
    send_sems,
    recv_sems,
    spread_send,
    spread_recv,
    stage_sems,
    other_sems,
):
    group, room, width = cot_own.shape
    hidden_width = gate_mat.shape[1]
    tiles = hidden_width // tile
    loads = []
    for at, (source, target) in enumerate(
        ((cot_own, cot), (down_weight, down_mat), (gate_weight, gate_mat), (up_weight, up_mat))
    ):
        load = pltpu.make_async_copy(source, target, load_sems.at[at])
        load.start()
        loads.append(load)
    devices = partners(*sizes)
    part, quarter = group // 2, group // 4
    strip = part * room
    cot_spreads = [None] + [
        Spread(near, far, spread_send.at[at], spread_recv.at[at])
        for at, (near, far) in enumerate(((cot_near1, cot_far1), (cot_near2, cot_far2), (cot_near3, cot_far3)))
    ]
    row_spreads = [
        Spread(near, far, spread_send.at[3 + at], spread_recv.at[3 + at])
        for at, (near, far) in enumerate(
            ((rows_near0, rows_far0), (rows_near1, rows_far1), (rows_near2, rows_far2))
        )
    ]
    greet(devices[1:] + row_spreads[0].devices)

    def cots_first(piece):
        return cot_spreads[piece].first(cot_own.at[pl.ds(piece * quarter, quarter)])

    def rows_first(piece):
        return row_spreads[piece].first(rows_landed.at[pl.ds(piece * quarter, quarter)])

    def row_copy(way, place):
        source, target = ((rows_sent, rows_landed), (back_sent, back_landed))[way]
        if place == 0:
            return pltpu.make_async_copy(source.at[0], target.at[0], own_sems.at[way])
        sems = (send_sems.at[way, place - 1], recv_sems.at[way, place - 1])
        return remote(source.at[place], target.at[place], *sems, devices[place])

    def stage_copy(at, slot, start, size):
        return pltpu.make_async_copy(
            staged.at[slot, :, pl.ds(0, size)], parts_out.at[at, :, pl.ds(start, size)], stage_sems.at[slot]
        )

    def stage_free(at, start, size):
        @pl.when(at >= 2)
        def _():
            stage_copy(at - 2, lax.rem(at, 2), start, size).wait()

    def stage(at, start, size, hidden, gate_back, up_back):
        slot = lax.rem(at, 2)
        for number, values in enumerate((hidden, gate_back, up_back)):
            staged[slot, number, pl.ds(0, size)] = values
        return stage_copy(at, slot, start, size)

    def stage_end(start, size):
        for at in (tiles - 2, tiles - 1):
            stage_copy(at, at % 2, start, size).wait()

    def own_half(half):
        held = slice(half * part, (half + 1) * part)
        cut_rows = pl.ds(half * strip, strip)
        rows = rows_landed[held, :, :width].reshape(strip, width)
        picks = panel_sum(rows_landed[held, :, width:].reshape(strip, LANES))
        total[...] = jnp.zeros_like(total)
        picks_back[...] = jnp.zeros_like(picks_back)

        def middle(at, carry):
            stage_free(at, half * strip, strip)
            cut = pl.ds(pl.multiple_of(at * tile, tile), tile)
            value, slope = gelu_parts(product(rows, gate_mat[:, cut]))
            up_part = product(rows, up_mat[:, cut])
            hidden = value * up_part
            hidden_low = hidden.astype(jnp.bfloat16)
            hidden_all[cut_rows, cut] = hidden_low
            back = down_rows[cut_rows, cut].astype(jnp.float32)
            weighed = hidden * back
            picks_back[...] += sum(weighed[:, lane : lane + LANES] for lane in range(0, tile, LANES))
            back = back * picks
            gate_back = (back * up_part * slope).astype(jnp.bfloat16)
            up_back = (back * value).astype(jnp.bfloat16)
            store = stage(at, half * strip, strip, hidden_low, gate_back, up_back)
            total[...] += product_back(
                jnp.concatenate([gate_back, up_back], axis=1),
                jnp.concatenate([gate_mat[:, cut], up_mat[:, cut]], axis=1),
            )
            store.start()
            return carry

        lax.fori_loop(0, tiles, middle, 0)
        back_sent[held, :, :width] = total[...].astype(jnp.bfloat16).reshape(part, room, width)
        high, low = halves(jnp.sum(picks_back[...], axis=1, keepdims=True))
        lane = iota((strip, LANES), 1)
        panel = jnp.where(lane == 0, high, jnp.where(lane == 1, low, jnp.zeros_like(low)))
        back_sent[held, :, width:] = panel.reshape(part, room, LANES)
        start_all([row_copy(1, place) for place in range(half * part, (half + 1) * part)])
        stage_end(half * strip, strip)

    def late_seconds():
        wait_all(cots_first(2) + cots_first(3) + rows_first(2))
        start_all(cot_spreads[2].second() + cot_spreads[3].second() + row_spreads[2].second())

    def others(start, sources):
        at, copies = 0, []
        for number, (row_source, cot_source) in enumerate(sources):
            size = row_source.shape[0]
            place = pl.ds(at, size)
            copies += [
                pltpu.make_async_copy(row_source, other_rows.at[place], other_sems.at[0, number]),
                pltpu.make_async_copy(cot_source, other_cots.at[place], other_sems.at[1, number]),
            ]
            at += size
        size = at
        start_all(copies)
        wait_all(copies)
        rows = other_rows[:size, :, :width].reshape(size * room, width)
        picks = panel_sum(other_rows[:size, :, width:].reshape(size * room, LANES))
        cots = (other_cots[:size].reshape(size * room, width).astype(jnp.float32) * picks).astype(jnp.bfloat16)
        size = size * room

        def middle(at, carry):
            pl.when(at == tiles // 2)(late_seconds)
            stage_free(at, start, size)
            cut = pl.ds(pl.multiple_of(at * tile, tile), tile)
            value, slope = gelu_parts(product(rows, gate_mat[:, cut]))
            up_part = product(rows, up_mat[:, cut])
            back = product_back(cots, down_mat[cut, :])
            store = stage(
                at,
                start,
                size,
                (value * up_part).astype(jnp.bfloat16),
                (back * up_part * slope).astype(jnp.bfloat16),
                (back * value).astype(jnp.bfloat16),
            )
            store.start()
            return carry

        lax.fori_loop(0, tiles, middle, 0)
        stage_end(start, size)

    start_all([row_copy(0, place) for place in range(part)])
    start_all(cot_spreads[1].second() + cots_first(2))
    wait_all(loads[:2])
    cot_rows = cot[...].reshape(group * room, width)

    def early(at, carry):
        cut = pl.ds(pl.multiple_of(at * tile, tile), tile)
        down_rows[:, cut] = product_back(cot_rows, down_mat[cut, :]).astype(jnp.bfloat16)
        return carry

    lax.fori_loop(0, tiles, early, 0)
    wait_all(loads[2:])
    wait_all([row_copy(0, place) for place in range(quarter)])
    start_all(rows_first(0))
    wait_all([row_copy(0, place) for place in range(quarter, part)])
    start_all([row_copy(0, place) for place in range(part, group)])
    start_all(rows_first(1))
    own_half(0)
    wait_all(rows_first(0) + rows_first(1))
    start_all(row_spreads[0].second() + row_spreads[1].second() + cots_first(3))
    wait_all([row_copy(0, place) for place in range(part, group)])
    start_all(rows_first(2))
    own_half(1)
    wait_all(cot_spreads[1].second() + row_spreads[0].second() + row_spreads[1].second())
    others(
        2 * strip,
        [(rows_near0.at[k], cot_near0.at[k]) for k in range(2)]
        + [(rows_near1.at[k], cot_near1.at[k]) for k in range(2)]
        + [(rows_far0, cot_far0), (rows_far1, cot_far1)],
    )

    def outward(at, carry):
        cut = pl.ds(pl.multiple_of(at * tile, tile), tile)
        out = product(hidden_all[...], down_mat[:, cut]).astype(jnp.bfloat16)
        out_rows[:, :, cut] = out.reshape(group, room, tile)
        return carry

    lax.fori_loop(0, width // tile, outward, 0)
    wait_all([row_copy(1, place) for place in range(group)])
    wait_all(cot_spreads[2].second() + cot_spreads[3].second() + row_spreads[2].second())


def experts_apply(sizes, number, tile, *operands):
    rows_sent, cot_own = operands[:2]
    group, room, width = cot_own.shape
    hidden_width = operands[5].shape[1]
    slots = group * room
    quarter = group // 4
    half, single = jnp.bfloat16, jnp.float32
    vmem, anywhere = pl.BlockSpec(memory_space=pltpu.VMEM), pl.BlockSpec(memory_space=pl.ANY)
    wide = rows_sent.shape[2]
    shapes = [rows_sent.shape, rows_sent.shape, cot_own.shape, (hidden_width // tile, 3, 5 * slots // 2, tile)]
    shapes += [(quarter, room, width)] + [(2, quarter, room, width), (quarter, room, width)] * 2
    shapes += [(2, quarter, room, wide), (quarter, room, wide)] * 3
    return pl.pallas_call(
        functools.partial(expert_kernel, tile, sizes),
        out_shape=[jax.ShapeDtypeStruct(shape, half) for shape in shapes],
        in_specs=[anywhere] * 8,
        out_specs=[anywhere] + [vmem] * 2 + [anywhere] * 12,
        scratch_shapes=[
            pltpu.VMEM((width, hidden_width), half),
            pltpu.VMEM((width, hidden_width), half),
            pltpu.VMEM((hidden_width, width), half),
            pltpu.VMEM((group, room, width), half),
            pltpu.VMEM((slots, hidden_width), half),
            pltpu.VMEM((slots, hidden_width), half),
            pltpu.VMEM((slots // 2, width), single),
            pltpu.VMEM((slots // 2, LANES), single),
            pltpu.VMEM(rows_sent.shape, half),
            pltpu.VMEM((6 * quarter, room, wide), half),
            pltpu.VMEM((6 * quarter, room, width), half),
            pltpu.VMEM((2, 3, 6 * quarter * room, tile), half),
            pltpu.SemaphoreType.DMA((4,)),
            pltpu.SemaphoreType.DMA((2,)),
            pltpu.SemaphoreType.DMA((2, group - 1)),
            pltpu.SemaphoreType.DMA((2, group - 1)),
            pltpu.SemaphoreType.DMA((6, 4)),
            pltpu.SemaphoreType.DMA((6, 4)),
            pltpu.SemaphoreType.DMA((2,)),
            pltpu.SemaphoreType.DMA((2, 6)),
        ],
        compiler_params=pltpu.CompilerParams(
            collective_id=number, has_side_effects=True, vmem_limit_bytes=VMEM_LIMIT
        ),
    )(*operands)


def column_slots(routes, live, experts, room, capacity):
    tok = live.shape[0]
    names = iota((tok, experts), 1).astype(jnp.float32)
    hot = [(routes[:, k : k + 1] == names) & live for k in range(2)]
    both = jnp.where(hot[0] | hot[1], 1.0, 0.0).astype(jnp.bfloat16)
    before = jnp.where(iota((tok, tok), 1) < iota((tok, tok), 0), 1.0, 0.0).astype(jnp.bfloat16)
    earlier = product(before, both)
    slots = []
    for k in range(2):
        place = jnp.sum(jnp.where(hot[k], earlier, 0.0), axis=1, keepdims=True)
        slot = routes[:, k : k + 1] * room + place
        slots.append(jnp.where(live & (place < capacity), slot, -1.0))
    return slots


def halves(values):
    high = values.astype(jnp.bfloat16)
    return high, (values - high.astype(jnp.float32)).astype(jnp.bfloat16)


def back_kernel(
    dims,
    lengths,
    tokens,
    cotangent,
    near_row,
    routes_true,
    attn_gain,
    moe_gain,
    router,
    residual_in,
    gates_in,
    mixed,
    probs_in,
    queries_in,
    both,
    normed,
    back_in,
    out_sent,
    rows_own,
    query_weight,
    key_weight,
    value_weight,
    out_weight,
    output,
    token_grad,
    query_wgrad,
    key_wgrad,
    value_wgrad,
    small,
    rows_near3,
    rows_far3,
    out_total,
    back,
    out_landed,
    query_grad,
    held_weights,
    mixed_back,
    residual_grad,
    far_sent,
    far_landed,
    near_sum,
    diagonals,
    load_sems,
    own_sem,
    send_sems,
    recv_sems,
    row_send,
    row_recv,
    near_send,
    near_recv,
    out_wgrad,
    *shared,
):
    *held, sum_send, sum_recv = shared
    heads, experts, room, capacity, n_row, n_col, share, depth = dims
    tok, width = tokens.shape
    pair_width = 2 * width // heads
    member_width = pair_width // 2
    slots_count = experts * room
    loads = []
    for at, (source, target) in enumerate(
        ((back_in, back), (out_weight, held_weights.at[0]))
        + tuple((w, held_weights.at[1 + k]) for k, w in enumerate((query_weight, key_weight, value_weight)))
    ):
        load = pltpu.make_async_copy(source, target, load_sems.at[at])
        load.start()
        loads.append(load)
    devices = partners(n_row, n_col)
    spread = Spread(rows_near3, rows_far3, near_send, near_recv)
    quarter = len(devices) // 4
    late_rows = rows_own.at[pl.ds(3 * quarter, quarter)]
    summed = ShareSum((n_row, n_col), depth, [out_wgrad], [out_total], [held], sum_send, sum_recv)
    greet(devices[1:] + spread.devices)
    start_all(spread.first(late_rows))
    copies = [pltpu.make_async_copy(out_sent.at[0], out_landed.at[0], own_sem)]
    for place in range(1, len(devices)):
        sems = (send_sems.at[place - 1], recv_sems.at[place - 1])
        copies.append(remote(out_sent.at[place], out_landed.at[place], *sems, devices[place]))
    start_all(copies)

    piece = lax.axis_index("erow")
    live = iota((tok, 1), 0) + piece * tok < lengths[0]
    slots = column_slots(columns_of(near_row[...], 2), live, experts, room, capacity)
    names = iota((tok, slots_count), 1).astype(jnp.float32)
    hot = [jnp.where(names == slot, 1.0, 0.0).astype(jnp.bfloat16) for slot in slots]
    lane = iota((tok, LANES), 1)
    columns = columns_of(routes_true[...], 2)
    chosen = [columns[:, k : k + 1] == lane.astype(jnp.float32) for k in range(2)]
    gates = gates_in[...]

    residual = residual_in[...]
    scale = lax.rsqrt(jnp.mean(residual * residual, axis=1, keepdims=True) + epsilon)
    moe_in = (residual * scale * moe_gain[...]).astype(jnp.bfloat16)
    loads[0].wait()
    panel = back[:, :, width:].reshape(slots_count, LANES)
    prob_back = jnp.zeros((tok, LANES), jnp.float32)
    for k in range(2):
        parts = product(hot[k], panel)
        prob_back = prob_back + jnp.where(chosen[k], parts[:, 0:1] + parts[:, 1:2], 0.0)
    logit_back = gates * (prob_back - jnp.sum(gates * prob_back, axis=1, keepdims=True))
    logit_high, logit_low = halves(logit_back)
    router_high, router_low = halves(router[...])
    few = slice(0, experts)
    moe_back = (
        product(hot[0] + hot[1], back[:, :, :width].reshape(slots_count, width))
        + product(logit_high[:, few], router_high)
        + product(logit_low[:, few], router_high)
        + product(logit_high[:, few], router_low)
    )
    left = moe_in.T
    router_grad = product(left, logit_high) + product(left, logit_low)
    moe_gain_grad = jnp.sum(residual * scale * moe_back, axis=0, keepdims=True)
    pulled = moe_gain[...] * moe_back
    total = (
        cotangent[...].astype(jnp.float32)
        + scale * pulled
        - residual * (scale * scale * scale * jnp.mean(residual * pulled, axis=1, keepdims=True))
    )
    residual_grad[...] = total
    branch = total.astype(jnp.bfloat16)
    loads[1].wait()
    mixed_back[...] = product_back(branch, held_weights[0]).astype(jnp.bfloat16)
    out_wgrad[...] = product(mixed[...].T, branch).astype(jnp.bfloat16).reshape(out_wgrad.shape)
    summed.turn(0)
    reversal = jnp.where(iota((tok, tok), 0) + iota((tok, tok), 1) == tok - 1, 1.0, 0.0).astype(jnp.bfloat16)
    low_half = iota((tok, pair_width), 1) < member_width

    def unattend(pair, carry):
        lanes = pl.ds(pl.multiple_of(pair * pair_width, pair_width), pair_width)
        value_lanes = pl.ds(pl.multiple_of(width + pair * pair_width, pair_width), pair_width)
        keys, values = both[:, lanes], both[:, value_lanes]
        grads = mixed_back[:, lanes]

        @pl.when(pair == 1)
        def _():
            summed.turn(1)

        @pl.when(pair == 3)
        def _():
            wait_all(spread.first(late_rows))
            start_all(spread.second())

        @pl.when(pair == 5)
        def _():
            summed.turn(2)

        @pl.when(pair == heads // 2 - 1)
        def _():
            summed.turn(3)

        queries_left, grads_left = queries_in[:, lanes].T, grads.T
        query_parts, key_parts, value_parts = [], [], []
        for member in range(2):
            head = 2 * pair + member
            mask = low_half if member == 0 else jnp.logical_not(low_half)
            low = probs_in[pl.ds(head, 1)][0]
            probs = low.astype(jnp.float32)
            part = product_back(jnp.where(mask, grads, jnp.zeros_like(grads)), values)
            weighed = probs * part
            score = (weighed - probs * jnp.sum(weighed, axis=1, keepdims=True)).astype(jnp.bfloat16)
            query_parts.append(product(score, keys))
            span = slice(member * member_width, (member + 1) * member_width)
            key_parts.append(product(queries_left[span], score))
            value_parts.append(product(grads_left[span], low))
            exact = product(reversal, score)
            empty = jnp.zeros((tok, tok), jnp.float32)
            padded = jnp.concatenate([exact[:, :tok], empty, exact[:, tok:], empty], axis=1)
            turned = pltpu.roll(padded, 3 * tok + 1, 1, stride=1, stride_axis=0)
            diagonals[pl.ds(head, 1)] = jnp.sum(turned, axis=0, keepdims=True)
        query_grad[:, lanes] = (jnp.where(low_half, query_parts[0], query_parts[1]) * 0.125).astype(jnp.bfloat16)
        key_part = jnp.concatenate(key_parts, axis=0).T
        value_part = jnp.concatenate(value_parts, axis=0).T
        near_sum[:, lanes] = key_part[:tok]
        near_sum[:, value_lanes] = value_part[:tok]
        far_sent[:, lanes] = key_part[tok:].astype(jnp.bfloat16)
        far_sent[:, value_lanes] = value_part[tok:].astype(jnp.bfloat16)
        return carry

    lax.fori_loop(0, heads // 2, unattend, 0)
    pair_copy = remote(far_sent, far_landed, row_send, row_recv, devices[1])
    pair_copy.start()
    left = normed[...].T
    shape = query_wgrad.shape
    query_wgrad[...] = product(left, query_grad[...]).astype(jnp.bfloat16).reshape(shape)

    segment = width // heads
    table = 4 * tok
    entry = iota((table, LANES), 0)
    other = entry >= table // 4
    other = other & (entry < 3 * table // 4)
    distance = jnp.where(
        other,
        entry - table // 2 + tok * (1 - 2 * piece),
        jnp.where(entry < table // 2, entry, entry - table),
    )
    bucket = bucket_of(distance)
    place = depth * lax.div(bucket, share) + lax.rem(bucket, share)
    target = lax.rem(iota((table, LANES), 1), segment)
    sorted_hot = jnp.where(place == target, 1.0, 0.0).astype(jnp.bfloat16)
    diagonal_high, diagonal_low = halves(diagonals[...])
    bias_rows = product(diagonal_high, sorted_hot) + product(diagonal_low, sorted_hot)
    bias_wide = jnp.concatenate([bias_rows] * (width // LANES), axis=1)
    mine = lax.div(iota((heads, width), 1), segment) == iota((heads, width), 0)
    bias_row = jnp.sum(jnp.where(mine, bias_wide, 0.0), axis=0, keepdims=True)

    loads[2].wait()
    normed_back = product_back(query_grad[...], held_weights[1])
    pair_copy.wait()
    key_total = (near_sum[:, :width] + far_landed[:, :width].astype(jnp.float32)).astype(jnp.bfloat16)
    value_total = (near_sum[:, width:] + far_landed[:, width:].astype(jnp.float32)).astype(jnp.bfloat16)
    key_wgrad[...] = product(left, key_total).astype(jnp.bfloat16).reshape(shape)
    value_wgrad[...] = product(left, value_total).astype(jnp.bfloat16).reshape(shape)
    loads[3].wait()
    loads[4].wait()
    normed_back = normed_back + product_back(key_total, held_weights[2]) + product_back(value_total, held_weights[3])
    inputs = tokens[...].astype(jnp.float32)
    scale = lax.rsqrt(jnp.mean(inputs * inputs, axis=1, keepdims=True) + epsilon)
    attn_gain_grad = jnp.sum(inputs * scale * normed_back, axis=0, keepdims=True)
    pulled = attn_gain[...] * normed_back
    token_grad[...] = (
        residual_grad[...]
        + scale * pulled
        - inputs * (scale * scale * scale * jnp.mean(inputs * pulled, axis=1, keepdims=True))
    )
    empty = jnp.zeros((LANES - 3, width), jnp.float32)
    small[...] = jnp.concatenate([empty, attn_gain_grad, moe_gain_grad, bias_row], axis=0).T + router_grad
    wait_all(copies)
    results = out_landed[...].reshape(slots_count, width)
    total = residual
    for k in range(2):
        pick = jnp.sum(jnp.where(chosen[k], gates, 0.0), axis=1, keepdims=True)
        total = total + pick * product(hot[k], results)
    output[...] = total.astype(jnp.bfloat16)
    wait_all(spread.second())
    summed.turn(4)


def backward(dims, number, *operands):
    heads, experts, room, capacity, n_row, n_col, share, depth = dims
    tokens, back_in, out_sent, rows_own = operands[1], operands[15], operands[16], operands[17]
    tok, width = tokens.shape
    group = n_row * n_col
    half, single = jnp.bfloat16, jnp.float32
    vmem, anywhere = pl.BlockSpec(memory_space=pltpu.VMEM), pl.BlockSpec(memory_space=pl.ANY)
    wgrad = (2, 2, n_row, n_col * depth, width)
    shapes = [((tok, width), half), ((tok, width), single)] + [(wgrad, half)] * 3 + [((width, LANES), single)]
    shapes += [((2, group // 4) + rows_own.shape[1:], half), ((group // 4,) + rows_own.shape[1:], half)]
    shapes += [((depth, width), single)]
    sems = (1, 4 + n_col)
    return pl.pallas_call(
        functools.partial(back_kernel, dims),
        out_shape=[jax.ShapeDtypeStruct(shape, kind) for shape, kind in shapes],
        in_specs=[pl.BlockSpec(memory_space=pltpu.SMEM)] + [vmem] * 14 + [anywhere] * 7,
        out_specs=[vmem] * 6 + [anywhere] * 2 + [vmem],
        scratch_shapes=[
            pltpu.VMEM(back_in.shape, half),
            pltpu.VMEM(out_sent.shape, half),
            pltpu.VMEM((tok, width), half),
            pltpu.VMEM((4, width, width), half),
            pltpu.VMEM((tok, width), half),
            pltpu.VMEM((tok, width), single),
            pltpu.VMEM((tok, 2 * width), half),
            pltpu.VMEM((tok, 2 * width), half),
            pltpu.VMEM((tok, 2 * width), single),
            pltpu.VMEM((heads, 4 * tok), single),
            pltpu.SemaphoreType.DMA((5,)),
            pltpu.SemaphoreType.DMA,
            pltpu.SemaphoreType.DMA((group - 1,)),
            pltpu.SemaphoreType.DMA((group - 1,)),
            pltpu.SemaphoreType.DMA,
            pltpu.SemaphoreType.DMA,
            pltpu.SemaphoreType.DMA((4,)),
            pltpu.SemaphoreType.DMA((4,)),
            pltpu.VMEM(wgrad, half),
        ]
        + share_scratch((n_row, n_col), depth, width, half)
        + [pltpu.SemaphoreType.DMA(sems), pltpu.SemaphoreType.DMA(sems)],
        compiler_params=pltpu.CompilerParams(
            collective_id=number, has_side_effects=True, vmem_limit_bytes=VMEM_LIMIT
        ),
    )(*operands)


def last_kernel(tile, sizes, depth, *refs):
    pieces = 9
    grads_in, small, refs = refs[:3], refs[3], refs[4:]
    rows_in, refs = refs[:pieces], refs[pieces:]
    cots_in, refs = refs[:pieces], refs[pieces:]
    parts_in, weights, sums, refs = refs[0], refs[1:4], refs[4:8], refs[8:]
    (gate_out, up_out, down_out), refs = refs[:3], refs[3:]
    grads, grad_sems, refs = refs[:3], refs[3], refs[4:]
    (rows, cots, mats, tiles_of, own_mats, out_tiles, down_tiles), refs = refs[:7], refs[7:]
    held, refs = [refs[5 * at : 5 * at + 5] for at in range(4)], refs[20:]
    load_sems, weight_sems, own_sems, out_sems, down_sem, send_sems, recv_sems = refs
    width = grads[0].shape[4]
    hidden_width = weights[0].shape[1]
    tiles = hidden_width // tile
    ready = parts_in.shape[2]
    total_rows = rows.shape[0]
    chunk = (total_rows - ready) // 2
    share = width // 4
    hidden_share = hidden_width // 4
    replica = lax.axis_index("dp")
    summed = ShareSum(sizes, depth, list(grads) + [small], sums, held, send_sems, recv_sems)
    barrier = pltpu.get_barrier_semaphore()
    for device in summed.devices:
        pl.semaphore_signal(barrier, 1, device_id=device, device_id_type=MESH)
    grad_loads = [
        pltpu.make_async_copy(source, target, grad_sems.at[at])
        for at, (source, target) in enumerate(zip(grads_in, grads))
    ]
    start_all(grad_loads)
    loads, start = [], 0
    for at, (row_piece, cot_piece) in enumerate(zip(rows_in, cots_in)):
        size = row_piece.shape[0]
        for number, (piece, target) in enumerate(((row_piece, rows), (cot_piece, cots))):
            load = pltpu.make_async_copy(piece, target.at[pl.ds(start, size)], load_sems.at[number, at])
            load.start()
            loads.append(load)
        start += size

    def weight_loads(at, slot):
        cut = pl.ds(pl.multiple_of(at * tile, tile), tile)
        return [
            pltpu.make_async_copy(source, mats.at[number, slot], weight_sems.at[number, slot])
            for number, source in enumerate((weights[0].at[:, cut], weights[1].at[:, cut]))
        ] + [pltpu.make_async_copy(weights[2].at[cut], own_mats.at[slot], weight_sems.at[2, slot])]

    def own_loads(at, slot):
        return [
            pltpu.make_async_copy(parts_in.at[at], tiles_of.at[slot, :, pl.ds(0, ready)], own_sems.at[slot])
        ]

    def out_copies(at, slot):
        cut = pl.ds(pl.multiple_of(at * tile, tile), tile)
        return [
            pltpu.make_async_copy(out_tiles.at[number, slot], target.at[:, cut], out_sems.at[number, slot])
            for number, target in enumerate((gate_out, up_out))
        ]

    share_lanes = pl.ds(pl.multiple_of(replica * share, share), share)
    first = lax.div(replica * hidden_share, tile)
    spans = lax.div((replica + 1) * hidden_share - 1, tile) - first + 1

    def tile_at(turn):
        return lax.rem(first + turn, tiles)

    start_all(weight_loads(tile_at(0), 0) + own_loads(tile_at(0), 0))
    wait_all(grad_loads)
    pl.semaphore_wait(barrier, len(summed.devices))
    summed.turn(0)
    for load in loads:
        load.wait()

    def weigh(at, carry):
        cut = pl.ds(pl.multiple_of(at * 256, 256), 256)
        panel = rows[cut, width:]
        picks = panel[:, 0:1].astype(jnp.float32) + panel[:, 1:2].astype(jnp.float32)
        cots[cut] = (cots[cut].astype(jnp.float32) * picks).astype(jnp.bfloat16)
        return carry

    lax.fori_loop(0, total_rows // 256, weigh, 0)
    summed.turn(1)
    turn_tiles = (1, 3, 5, 7, 9, 10)
    blocks = 1 if chunk <= 512 else 2

    def each_tile(turn, carry):
        slot = lax.rem(turn, 2)
        at = tile_at(turn)
        wait_all(weight_loads(at, slot) + own_loads(at, slot))

        @pl.when(turn + 1 < tiles)
        def _():
            start_all(weight_loads(tile_at(turn + 1), 1 - slot) + own_loads(tile_at(turn + 1), 1 - slot))

        for number in range(2, summed.turns):
            @pl.when(turn == turn_tiles[number - 2])
            def _(number=number):
                summed.turn(number)

        @pl.when(turn >= 2)
        def _():
            wait_all(out_copies(tile_at(turn - 2), slot))

        size = 2 * chunk // blocks
        for block in range(blocks):
            cut = pl.ds(ready + block * size, size)
            value, slope = gelu_parts(product(rows[cut, :width], mats[0, slot]))
            up_part = product(rows[cut, :width], mats[1, slot])
            back = product_back(cots[cut], own_mats[slot])
            tiles_of[slot, 0, cut] = (value * up_part).astype(jnp.bfloat16)
            tiles_of[slot, 1, cut] = (back * up_part * slope).astype(jnp.bfloat16)
            tiles_of[slot, 2, cut] = (back * value).astype(jnp.bfloat16)
        both = jnp.concatenate([tiles_of[slot, 1], tiles_of[slot, 2]], axis=1)
        turned = product_left(both, rows[:, share_lanes]).T
        out_tiles[0, slot] = turned[:, :tile]
        out_tiles[1, slot] = turned[:, tile:]
        start_all(out_copies(at, slot))

        @pl.when(turn < spans)
        def _():
            place = pl.ds(pl.multiple_of(turn * tile, tile), tile)
            down_tiles[place] = product_left(tiles_of[slot, 0], cots[...])

        return carry

    lax.fori_loop(0, tiles, each_tile, 0)
    offset = pl.multiple_of(replica * hidden_share - first * tile, 8)
    down_copy = pltpu.make_async_copy(down_tiles.at[pl.ds(offset, hidden_share)], down_out, down_sem)
    down_copy.start()
    for turn in (tiles - 2, tiles - 1):
        wait_all(out_copies(tile_at(turn), turn % 2))
    down_copy.wait()


def last(sizes, number, grads, small, rows_in, cots_in, parts_in, weights):
    n_dp, n_row, n_col = sizes
    width, hidden_width = weights[0].shape
    total_rows = sum(piece.shape[0] for piece in rows_in)
    tile = parts_in.shape[3]
    depth = width // (n_dp * n_row * n_col)
    strip = n_col * depth
    half, single = jnp.bfloat16, jnp.float32
    vmem, anywhere = pl.BlockSpec(memory_space=pltpu.VMEM), pl.BlockSpec(memory_space=pl.ANY)
    small = small.reshape(2, 2, n_row, strip, small.shape[1])
    hidden_share = hidden_width // n_dp
    spans = -(-hidden_share // tile) + 1
    scratch = [pltpu.VMEM(grad.shape, half) for grad in grads] + [pltpu.SemaphoreType.DMA((3,))]
    scratch += [
        pltpu.VMEM((total_rows, width + LANES), half),
        pltpu.VMEM((total_rows, width), half),
        pltpu.VMEM((2, 2, width, tile), half),
        pltpu.VMEM((2, 3, total_rows, tile), half),
        pltpu.VMEM((2, tile, width), half),
        pltpu.VMEM((2, 2, width // n_dp, tile), single),
        pltpu.VMEM((spans * tile, width), single),
    ]
    for _ in range(3):
        scratch += share_scratch((n_row, n_col), depth, width, half)
    scratch += share_scratch((n_row, n_col), depth, LANES, single)
    sems = (4, 4 + n_col)
    scratch += [
        pltpu.SemaphoreType.DMA((2, len(rows_in))),
        pltpu.SemaphoreType.DMA((3, 2)),
        pltpu.SemaphoreType.DMA((2,)),
        pltpu.SemaphoreType.DMA((2, 2)),
        pltpu.SemaphoreType.DMA,
        pltpu.SemaphoreType.DMA(sems),
        pltpu.SemaphoreType.DMA(sems),
    ]
    out_shape = [jax.ShapeDtypeStruct((depth, width), single)] * 3
    out_shape += [jax.ShapeDtypeStruct((depth, LANES), single)]
    out_shape += [jax.ShapeDtypeStruct((width // n_dp, hidden_width), single)] * 2
    out_shape += [jax.ShapeDtypeStruct((hidden_share, width), single)]
    return pl.pallas_call(
        functools.partial(last_kernel, tile, (n_row, n_col), depth),
        out_shape=out_shape,
        in_specs=[anywhere] * 3 + [vmem] + [anywhere] * (2 * len(rows_in) + 4),
        out_specs=[vmem] * 4 + [anywhere] * 3,
        scratch_shapes=scratch,
        compiler_params=pltpu.CompilerParams(
            collective_id=number, has_side_effects=True, vmem_limit_bytes=VMEM_LIMIT
        ),
    )(*grads, small, *rows_in, *cots_in, parts_in, *weights)


def finish_kernel(experts, bias_share, small, *refs):
    count = (len(refs) - 5) // 3
    sources, targets, rest = refs[:count], refs[count : 2 * count], refs[2 * count :]
    (attn_out, moe_out, bias_out, router_out), held, sems = rest[:4], rest[4:-1], rest[-1]
    loads = [
        pltpu.make_async_copy(source, place, sems.at[0, at]) for at, (source, place) in enumerate(zip(sources, held))
    ]
    stores = [
        pltpu.make_async_copy(place, target, sems.at[1, at]) for at, (place, target) in enumerate(zip(held, targets))
    ]
    start_all(loads)
    turned = small[...].T
    attn_out[...] = turned[LANES - 3 : LANES - 2]
    moe_out[...] = turned[LANES - 2 : LANES - 1]
    bias_out[...] = turned[LANES - 1 :, :bias_share]
    router_out[...] = turned[:experts]
    for load, store in zip(loads, stores):
        load.wait()
        store.start()
    wait_all(stores)


def finish(experts, bias_share, small, *arrays):
    depth = small.shape[0]
    vmem, anywhere = pl.BlockSpec(memory_space=pltpu.VMEM), pl.BlockSpec(memory_space=pl.ANY)
    shapes = [(array.shape, array.dtype) for array in arrays]
    shapes += [((1, depth), small.dtype)] * 2 + [((1, bias_share), small.dtype), ((experts, depth), small.dtype)]
    return pl.pallas_call(
        functools.partial(finish_kernel, experts, bias_share),
        out_shape=[jax.ShapeDtypeStruct(*shape) for shape in shapes],
        in_specs=[vmem] + [anywhere] * len(arrays),
        out_specs=[anywhere] * len(arrays) + [vmem] * 4,
        scratch_shapes=[pltpu.VMEM(array.shape, array.dtype) for array in arrays]
        + [pltpu.SemaphoreType.DMA((2, len(arrays)))],
        compiler_params=pltpu.CompilerParams(vmem_limit_bytes=VMEM_LIMIT),
    )(small, *arrays)


def gelu_parts(gate_part):
    square = gate_part * gate_part
    inner = gate_part * (0.7978845608028654 + 0.035677408136300125 * square)
    half = 0.5 + 0.5 * jnp.tanh(inner)
    value = gate_part * half
    slope = half + value * (1.0 - half) * (1.5957691216057308 + 0.21406444881780075 * square)
    return value, slope


def paired(own, *pieces):
    blocks = [own]
    for at in range(0, len(pieces), 2):
        blocks += [pieces[at][0], pieces[at + 1][0], pieces[at][1], pieces[at + 1][1]]
    return [block.reshape(-1, block.shape[-1]) for block in blocks]


def body(
    tokens,
    lengths,
    routes,
    attn_gain,
    query_weight,
    key_weight,
    value_weight,
    out_weight,
    relative_bias,
    moe_gain,
    router_weight,
    gate_weight,
    up_weight,
    down_weight,
    cotangent,
):
    tok_rows, width = tokens.shape[1:]
    head_count, bucket_count = relative_bias.shape
    expert_count = router_weight.shape[1]
    capacity = 5 * tok_rows // (2 * expert_count)
    room = -(-capacity // 16) * 16
    n_dp, n_row, n_col = (lax.axis_size(name) for name in ("dp", "erow", "ecol"))
    device_count = n_dp * n_row * n_col
    slot_count = expert_count * room
    gate_mat, up_mat, down_mat = gate_weight[0], up_weight[0], down_weight[0]
    routes_row = routes[0].T
    near_routes = mirrored((routes_row % n_col) ^ lax.axis_index("ecol"), n_col) * n_row + (
        (routes_row // n_col) ^ lax.axis_index("erow")
    )
    router = router_weight.T
    dims = (head_count, expert_count, room, capacity, n_row, n_col)
    normed, queries, both, probs, mixed, residual, gates, slot_rows, got_grads, *cots01 = front(
        dims,
        0,
        lengths,
        tokens[0],
        cotangent[0],
        near_routes,
        routes_row,
        attn_gain[None],
        moe_gain[None],
        relative_bias,
        router,
        query_weight,
        key_weight,
        value_weight,
        out_weight,
    )
    back, got, expert_out, parts, *moved = experts_apply(
        (n_row, n_col), 1, 256 if slot_count <= 768 else LANES, slot_rows, got_grads, *cots01, gate_mat, up_mat, down_mat
    )
    cots0, cots1, cots2, cots3, rows0, rows1, rows2 = ((cots01 + moved)[at : at + 2] for at in range(0, 14, 2))
    depth = width // device_count
    bias_share = head_count * bucket_count // device_count
    output, token_grad, query_wgrad, key_wgrad, value_wgrad, small, *rows3, out_sum = backward(
        dims + (bias_share, depth),
        2,
        lengths,
        tokens[0],
        cotangent[0],
        near_routes,
        routes_row,
        attn_gain[None],
        moe_gain[None],
        router,
        residual,
        gates,
        mixed,
        probs,
        queries,
        both,
        normed,
        back,
        expert_out,
        got,
        query_weight,
        key_weight,
        value_weight,
        out_weight,
    )
    query_sum, key_sum, value_sum, small_sum, gate_total, up_total, down_total = last(
        (n_dp, n_row, n_col),
        3,
        (query_wgrad, key_wgrad, value_wgrad),
        small,
        paired(got, rows0, rows1, rows2, rows3),
        paired(got_grads, cots0, cots1, cots2, cots3),
        parts,
        (gate_mat, up_mat, down_mat),
    )
    handed = finish(
        expert_count,
        bias_share,
        small_sum,
        output,
        token_grad,
        query_sum,
        key_sum,
        value_sum,
        out_sum,
        gate_total,
        up_total,
        down_total,
    )
    output, token_grad, query_sum, key_sum, value_sum, out_sum, gate_total, up_total, down_total = handed[:9]
    attn_sum, moe_sum, bias_sum, router_sum = handed[9:]
    return (
        output[None],
        token_grad[None],
        attn_sum[0],
        query_sum,
        key_sum,
        value_sum,
        out_sum,
        bias_sum[0],
        moe_sum[0],
        router_sum.T,
        gate_total[None],
        up_total[None],
        down_total[None],
    )


def solution(mesh):
    rows = P(("dp", "ecol"), "erow", None)
    experts = P(("erow", "ecol"), None, None)
    every = ("dp", "erow", "ecol")
    shares = P(("erow", "ecol"), "dp", None)
    return jax.shard_map(
        body,
        mesh=mesh,
        in_specs=(
            (rows, P(("dp", "ecol")), rows) + (P(),) * 8 + (experts, experts, experts, rows)
        ),
        out_specs=(rows, rows, P(every))
        + (P(every, None),) * 4
        + (P(every), P(every), P(every, None), shares, shares, shares),
        check_vma=False,
    )
```
